512 devices in a mesh: tm: 64 (over y, x, z_hi, core), section: 8 (over z_lo).
Axes of the slice: x: 4, y: 4, z: 16 (z_hi: 2, z_lo: 8; z = z_hi * 8 + z_lo), core: 2. Of those that a mesh axis runs over, the one named last changes fastest.
Arguments:
- layer_five: bfloat16 [16, 8192, 512], P('section', 'tm'), may hold values from -6 to 6
- conv_six: bfloat16 [1024, 512], P('tm'), may hold values from -0.1875 to 0.1875
- conv_seven: bfloat16 [1024, 512], P('tm'), may hold values from -0.1875 to 0.1875
- gains: float32 [3, 512], replicated, may hold values from 0.25 to 1.75
- biases: float32 [3, 512], replicated, may hold values from -1.5 to 1.5
- proj_weight: bfloat16 [512, 1920], P(None, 'section'), may hold values from -0.25 to 0.25
- feature_grad: bfloat16 [16, 2048, 1920], P(None, ('tm', 'section')), may hold values from -0.08984375 to 0.08984375
Outputs:
- grad_layer_five: bfloat16 [16, 8192, 512], P('section', 'tm')
- grad_conv_six: float32 [1024, 512], P('tm', 'section')
- grad_conv_seven: float32 [1024, 512], P('tm', 'section')
- grad_proj: float32 [512, 1920], P('tm', 'section')
- grad_gains: float32 [3, 512], replicated
- grad_biases: float32 [3, 512], replicated
The draws below stay inside these ranges and needn't reach their ends.
All inputs are finite; a program needn't handle non-finite values.
Results may differ from the reference program's by a relative error of at most 0.023.
Values may be sent and summed in bfloat16 or wider, within the bound.
No kernel may reach another device: no remote copies, remote signals or barrier semaphores. Data moves between devices by JAX's collectives and lax.ppermute only.
A program may use at most 64 MiB of HBM per device.

```python
import jax
import jax.numpy as jnp
from jax import lax

C = 512
PROJ = 1920
UTT_DEV = 2
FR_DEV = 32
UTT = 16
FRAMES = 2048
POS = 8192
N_TM = 64
N_SECTION = 8


def block_scale(own_key, shape, cuts, least, top_value):
    factor_of = 1.0
    for dim, shards_of in cuts:
        heights = jax.random.uniform(jax.random.fold_in(jax.random.fold_in(own_key, 6), dim), (shards_of,), jnp.float32, least / len(cuts), top_value / len(cuts))
        factor_of = factor_of * jnp.repeat(jnp.exp(heights), shape[dim] // shards_of).reshape((-1,) + (1,) * (len(shape) - 1 - dim))
    return factor_of


def scatter_about(own_key, shape, deviation, reach, cuts=(), kind=jnp.bfloat16):
    drawn = deviation * jax.random.normal(own_key, shape, jnp.float32)
    if cuts:
        drawn = drawn * block_scale(own_key, shape, cuts, -0.22, 0.18)
    return jnp.clip(drawn, -reach, reach).astype(kind)


def setup_inputs(seed: int = 0) -> dict:
    key_list = jax.random.split(jax.random.key(seed), 8)
    layer_five = scatter_about(key_list[0], (UTT, POS, C), 1.0, 6.0, ((0, 8), (1, 64)))
    conv_six = scatter_about(key_list[1], (2 * C, C), (2 * C) ** -0.5, 0.1875, ((0, 64),))
    conv_seven = scatter_about(key_list[2], (2 * C, C), (2 * C) ** -0.5, 0.1875, ((0, 64),))
    gains = jnp.clip(1.0 + 0.15 * jax.random.normal(key_list[3], (3, C), jnp.float32), 0.25, 1.75)
    biases = scatter_about(key_list[4], (3, C), 0.3, 1.5, (), jnp.float32)
    proj_weight = scatter_about(key_list[5], (C, PROJ), C ** -0.5, 0.25, ((1, 8),))
    feature_grad = scatter_about(key_list[6], (UTT, FRAMES, PROJ), 0.015, 0.08984375, ((1, 512),))
    return {"layer_five": layer_five, "conv_six": conv_six, "conv_seven": conv_seven, "gains": gains, "biases": biases, "proj_weight": proj_weight, "feature_grad": feature_grad}


norm_epsilon = 1e-05
half_root = 0.7071067811865476
inv_root_tau = 0.3989422804014327

def gelu_parts(preact):
    normal_cdf = 0.5 * (1.0 + lax.erf(preact * half_root))
    density = jnp.exp(-0.5 * preact * preact) * inv_root_tau
    return (preact * normal_cdf, normal_cdf + preact * density)

def norm_forward(hidden, gain_row, bias_row):
    average = lax.optimization_barrier(jnp.mean(hidden, axis=-1, keepdims=True))
    centred = hidden - average
    inv_scale = lax.rsqrt(lax.optimization_barrier(jnp.mean(centred * centred, axis=-1, keepdims=True)) + norm_epsilon)
    normal_part = centred * inv_scale
    return (normal_part * gain_row + bias_row, normal_part, inv_scale)

def norm_backward(incoming, normal_part, inv_scale, gain_row):
    scaled = incoming * gain_row
    first_mean = lax.optimization_barrier(jnp.mean(scaled, axis=-1, keepdims=True))
    second_mean = lax.optimization_barrier(jnp.mean(scaled * normal_part, axis=-1, keepdims=True))
    return inv_scale * (scaled - first_mean - normal_part * second_mean)

def rounded(value):
    narrow = lax.optimization_barrier(value.astype(jnp.bfloat16))
    return narrow.astype(jnp.float32)

def block_terms(inputs, grad_rows, run_length):
    channels_in = inputs.shape[-1]
    channels_out = grad_rows.shape[-1]
    in_blocks = inputs.reshape(N_SECTION, UTT_DEV, N_TM, run_length, channels_in)
    grad_blocks = grad_rows.reshape(N_SECTION, UTT_DEV, N_TM, run_length, channels_out)

    def accumulate(running, pair):
        block_in, block_grad = pair
        part = jnp.einsum('uirk,uirc->ikc', block_in.astype(jnp.float32), block_grad.astype(jnp.float32))
        return (running + lax.optimization_barrier(jnp.sum(rounded(part), axis=0)), None)
    running, unused = lax.scan(accumulate, jnp.zeros((channels_in, channels_out), jnp.float32), (in_blocks, grad_blocks))
    return running

def reference(layer_five, conv_six, conv_seven, gains, biases, proj_weight, feature_grad):
    channels = layer_five.shape[2]
    unf_six = layer_five.reshape(-1, 2 * channels)
    hid_six = jnp.dot(unf_six, conv_six, preferred_element_type=jnp.float32)
    pre_six, part_six, scale_six = norm_forward(hid_six, gains[0], biases[0])
    act_six_f, deriv_six = gelu_parts(pre_six)
    act_six = act_six_f.astype(jnp.bfloat16)
    unf_seven = act_six.reshape(-1, 2 * channels)
    hid_seven = jnp.dot(unf_seven, conv_seven, preferred_element_type=jnp.float32)
    pre_seven, part_seven, scale_seven = norm_forward(hid_seven, gains[1], biases[1])
    act_seven_f, deriv_seven = gelu_parts(pre_seven)
    act_seven = act_seven_f.astype(jnp.bfloat16)
    pre_feat, part_feat, scale_feat = norm_forward(act_seven.astype(jnp.float32), gains[2], biases[2])
    normed = pre_feat.astype(jnp.bfloat16)
    grad_flat = feature_grad.reshape(-1, PROJ)
    grad_proj = jnp.dot(normed.T, grad_flat, preferred_element_type=jnp.float32)
    columns = PROJ // N_SECTION
    grad_normed = jnp.zeros(normed.shape, jnp.float32)
    for column_block in range(N_SECTION):
        lower = column_block * columns
        part = jnp.dot(grad_flat[:, lower:lower + columns], proj_weight[:, lower:lower + columns].T, preferred_element_type=jnp.float32)
        grad_normed = grad_normed + rounded(part)
    dact_seven = norm_backward(grad_normed, part_feat, scale_feat, gains[2])
    dpre_seven = dact_seven * deriv_seven
    dhid_seven = norm_backward(dpre_seven, part_seven, scale_seven, gains[1]).astype(jnp.bfloat16)
    grad_conv_seven = block_terms(unf_seven, dhid_seven, FR_DEV)
    dact_six = jnp.dot(dhid_seven, conv_seven.T, preferred_element_type=jnp.float32).reshape(-1, channels)
    dpre_six = dact_six * deriv_six
    dhid_six = norm_backward(dpre_six, part_six, scale_six, gains[0]).astype(jnp.bfloat16)
    grad_conv_six = block_terms(unf_six, dhid_six, 2 * FR_DEV)
    grad_layer_five = jnp.dot(dhid_six, conv_six.T, preferred_element_type=jnp.float32).reshape(layer_five.shape).astype(jnp.bfloat16)
    grad_gains = jnp.stack([lax.optimization_barrier(jnp.sum(dpre_six * part_six, axis=0)), lax.optimization_barrier(jnp.sum(dpre_seven * part_seven, axis=0)), lax.optimization_barrier(jnp.sum(grad_normed * part_feat, axis=0))])
    grad_biases = jnp.stack([lax.optimization_barrier(jnp.sum(dpre_six, axis=0)), lax.optimization_barrier(jnp.sum(dpre_seven, axis=0)), lax.optimization_barrier(jnp.sum(grad_normed, axis=0))])
    return (grad_layer_five, grad_conv_six, grad_conv_seven, grad_proj, grad_gains, grad_biases)
```

```python
import jax
import jax.numpy as jnp
from jax import lax
from jax.sharding import Mesh, PartitionSpec as P

norm_epsilon = 1e-05
half_root = 0.7071067811865476
inv_root_tau = 0.3989422804014327
narrow = jnp.bfloat16
wide = jnp.float32


def gelu_parts(preact):
    normal_cdf = 0.5 * (1.0 + lax.erf(preact * half_root))
    density = jnp.exp(-0.5 * preact * preact) * inv_root_tau
    return (preact * normal_cdf, normal_cdf + preact * density)


def norm_forward(hidden, gain_row, bias_row):
    average = jnp.mean(hidden, axis=-1, keepdims=True)
    centred = hidden - average
    inv_scale = lax.rsqrt(jnp.mean(centred * centred, axis=-1, keepdims=True) + norm_epsilon)
    normal_part = centred * inv_scale
    return (normal_part * gain_row + bias_row, normal_part, inv_scale)


def norm_backward(incoming, normal_part, inv_scale, gain_row):
    scaled = incoming * gain_row
    first_mean = jnp.mean(scaled, axis=-1, keepdims=True)
    second_mean = jnp.mean(scaled * normal_part, axis=-1, keepdims=True)
    return inv_scale * (scaled - first_mean - normal_part * second_mean)


def spread(block, axes):
    count = lax.axis_size(axes)
    copies = jnp.broadcast_to(block[None], (count,) + block.shape)
    return lax.all_to_all(copies, axes, 0, 0, tiled=True)


def swap(value, axis):
    return lax.ppermute(value, axis, [(0, 1), (1, 0)])


def on_device(layer_five, conv_six, conv_seven, gains, biases, proj_weight, feature_grad):
    utt_local, positions, channels = layer_five.shape
    features = proj_weight.shape[0]
    width = feature_grad.shape[2]
    part_width = proj_weight.shape[1]
    sections = lax.axis_size("s")
    planes = lax.axis_size(("y", "x"))
    place = lax.axis_index(("y", "x"))
    half = lax.axis_index("zh")
    core = lax.axis_index("c")
    rows_conv = conv_six.shape[0]
    runs = feature_grad.shape[1]

    own_rows = jnp.stack([conv_six, conv_seven])
    other_rows = swap(own_rows, "zh")
    pair = jnp.where(
        half == 0, jnp.stack([own_rows, other_rows]), jnp.stack([other_rows, own_rows])
    )

    slice_rows = features // (2 * planes)
    start = core * (features // 2) + place * slice_rows
    proj_slice = lax.dynamic_slice_in_dim(proj_weight, start, slice_rows, 0)
    proj_copies = jnp.broadcast_to(
        proj_slice.reshape(1, -1, width), (sections, slice_rows * part_width // width, width)
    )
    grads_out = feature_grad.reshape(sections, utt_local * runs, width)
    arrived = lax.all_to_all(
        jnp.concatenate([grads_out, proj_copies], axis=1), "s", 0, 0, tiled=True
    )
    grad_rows = (
        arrived[:, : utt_local * runs]
        .reshape(sections, utt_local, runs, width)
        .transpose(1, 0, 2, 3)
        .reshape(-1, width)
    )
    proj_rows = (
        arrived[:, utt_local * runs :]
        .reshape(sections, slice_rows, part_width)
        .transpose(1, 0, 2)
        .reshape(-1, channels)
    )

    conv_part = 2 * 2 * rows_conv
    bundle = jnp.concatenate([pair.reshape(conv_part, channels), proj_rows], axis=0)
    gathered = spread(bundle, ("y", "x"))
    sibling = swap(gathered, "c")
    both = jnp.where(
        core == 0, jnp.stack([gathered, sibling]), jnp.stack([sibling, gathered])
    )
    kernels = both[:, :, :conv_part].reshape(2, planes, 2, 2, rows_conv, channels)
    kernels = kernels.transpose(3, 1, 2, 0, 4, 5).reshape(2, -1, channels)
    kernel_six, kernel_seven = kernels[0], kernels[1]
    proj_full = both[:, :, conv_part:].reshape(features, width)

    unf_six = layer_five.reshape(-1, 2 * channels)
    hid_six = jnp.dot(unf_six, kernel_six, preferred_element_type=wide)
    pre_six, part_six, scale_six = norm_forward(hid_six, gains[0], biases[0])
    act_six_f, deriv_six = gelu_parts(pre_six)
    unf_seven = act_six_f.astype(narrow).reshape(-1, 2 * channels)
    hid_seven = jnp.dot(unf_seven, kernel_seven, preferred_element_type=wide)
    pre_seven, part_seven, scale_seven = norm_forward(hid_seven, gains[1], biases[1])
    act_seven_f, deriv_seven = gelu_parts(pre_seven)
    act_seven = act_seven_f.astype(narrow)
    pre_feat, part_feat, scale_feat = norm_forward(act_seven.astype(wide), gains[2], biases[2])
    normed = pre_feat.astype(narrow)

    grad_normed = lax.dot_general(
        grad_rows, proj_full, (((1,), (1,)), ((), ())), preferred_element_type=wide
    )
    dact_seven = norm_backward(grad_normed, part_feat, scale_feat, gains[2])
    dpre_seven = dact_seven * deriv_seven
    dhid_seven = norm_backward(dpre_seven, part_seven, scale_seven, gains[1]).astype(narrow)
    dact_six = lax.dot_general(
        dhid_seven, kernel_seven, (((1,), (1,)), ((), ())), preferred_element_type=wide
    ).reshape(-1, channels)
    dpre_six = dact_six * deriv_six
    dhid_six = norm_backward(dpre_six, part_six, scale_six, gains[0]).astype(narrow)
    grad_input = lax.dot_general(
        dhid_six, kernel_six, (((1,), (1,)), ((), ())), preferred_element_type=wide
    )
    grad_layer_five = grad_input.reshape(utt_local, positions, channels).astype(narrow)

    over_rows = (((0,), (0,)), ((), ()))
    term_six = lax.dot_general(unf_six, dhid_six, over_rows, preferred_element_type=wide)
    term_seven = lax.dot_general(unf_seven, dhid_seven, over_rows, preferred_element_type=wide)
    term_proj = lax.dot_general(normed, grad_rows, over_rows, preferred_element_type=wide)
    sums = jnp.stack(
        [
            jnp.sum(dpre_six * part_six, axis=0),
            jnp.sum(dpre_seven * part_seven, axis=0),
            jnp.sum(grad_normed * part_feat, axis=0),
            jnp.sum(dpre_six, axis=0),
            jnp.sum(dpre_seven, axis=0),
            jnp.sum(grad_normed, axis=0),
        ]
    )

    rows_proj = features // (4 * planes)
    terms = jnp.concatenate(
        [
            term_six.reshape(planes, 2, 2, -1, channels),
            term_seven.reshape(planes, 2, 2, -1, channels),
            term_proj.reshape(planes, 2, 2, -1, channels),
        ],
        axis=3,
    ).astype(narrow)
    kept = jnp.where(core == 0, terms[:, :, 0], terms[:, :, 1])
    given = jnp.where(core == 0, terms[:, :, 1], terms[:, :, 0])
    chip = kept.astype(wide) + swap(given, "c").astype(wide)

    count = chip.shape[2]
    sums_high = lax.reduce_precision(sums, 8, 7)
    sum_pair = jnp.concatenate([sums_high, sums - sums_high], axis=0).astype(narrow)
    sum_rows = sum_pair.shape[0]
    plane_send = jnp.concatenate(
        [
            chip.astype(narrow).reshape(planes, -1, channels),
            jnp.broadcast_to(sum_pair[None], (planes, sum_rows, channels)),
        ],
        axis=1,
    )
    plane_sum = jnp.sum(
        lax.all_to_all(plane_send, ("y", "x"), 0, 0, tiled=True).astype(wide), axis=0
    )

    parts = plane_sum[: 2 * count].reshape(2, count, channels)
    conv_rows = parts[:, : 2 * rows_conv].reshape(2, 2 * rows_conv, sections, -1)
    conv_rows = conv_rows.transpose(0, 2, 1, 3).reshape(2 * sections, -1)
    proj_part = parts[:, 2 * rows_conv :].reshape(2, rows_proj, sections, part_width)
    proj_part = proj_part.transpose(0, 2, 1, 3).reshape(2 * sections, -1)
    totals = plane_sum[2 * count :].reshape(2, -1, channels).sum(axis=0)
    totals_high = lax.reduce_precision(totals, 8, 7)
    total_pair = jnp.stack([totals_high, totals - totals_high]).reshape(1, -1)
    line_send = jnp.concatenate(
        [conv_rows, proj_part, jnp.broadcast_to(total_pair, (2 * sections, total_pair.shape[1]))],
        axis=1,
    ).astype(narrow)
    line_sum = jnp.sum(
        lax.all_to_all(line_send, ("zh", "s"), 0, 0, tiled=True).astype(wide), axis=0
    )
    conv_size, proj_size = conv_rows.shape[1], proj_part.shape[1]
    out_conv = line_sum[:conv_size].reshape(2, rows_conv, -1)
    out_proj = line_sum[conv_size : conv_size + proj_size].reshape(rows_proj, part_width)
    out_sums = line_sum[conv_size + proj_size :].reshape(2, 6, channels).sum(axis=0)
    out_sums = out_sums + swap(out_sums, "c")
    return (
        grad_layer_five,
        out_conv[0],
        out_conv[1],
        out_proj,
        out_sums[:3],
        out_sums[3:],
    )


def solution(mesh):
    fine = Mesh(mesh.devices.reshape(4, 4, 2, 2, 8), ("y", "x", "zh", "c", "s"))
    tm = ("y", "x", "zh", "c")
    return jax.shard_map(
        on_device,
        mesh=fine,
        in_specs=(
            P("s", tm, None),
            P(tm, None),
            P(tm, None),
            P(),
            P(),
            P(None, "s"),
            P(None, tm + ("s",), None),
        ),
        out_specs=(
            P("s", tm, None),
            P(tm, "s"),
            P(tm, "s"),
            P(tm, "s"),
            P(),
            P(),
        ),
        check_vma=False,
    )
```

```python
import jax
import jax.numpy as jnp
from jax import lax
from jax.experimental import pallas as pl
from jax.experimental.pallas import tpu as pltpu
from jax.sharding import Mesh, PartitionSpec as P

norm_epsilon = 1e-05
half_root = 0.7071067811865476
inv_root_tau = 0.3989422804014327
narrow = jnp.bfloat16
wide = jnp.float32
LANES = 128
TILE = 16
VMEM_BYTES = 56 * 1024 * 1024


def gelu_parts(preact):
    normal_cdf = 0.5 * (1.0 + lax.erf(preact * half_root))
    density = jnp.exp(-0.5 * preact * preact) * inv_root_tau
    return (preact * normal_cdf, normal_cdf + preact * density)


def norm_forward(hidden, gain_row, bias_row):
    average = jnp.mean(hidden, axis=-1, keepdims=True)
    centred = hidden - average
    inv_scale = lax.rsqrt(jnp.mean(centred * centred, axis=-1, keepdims=True) + norm_epsilon)
    normal_part = centred * inv_scale
    return (normal_part * gain_row + bias_row, normal_part, inv_scale)


def norm_backward(incoming, normal_part, inv_scale, gain_row):
    scaled = incoming * gain_row
    first_mean = jnp.mean(scaled, axis=-1, keepdims=True)
    second_mean = jnp.mean(scaled * normal_part, axis=-1, keepdims=True)
    return inv_scale * (scaled - first_mean - normal_part * second_mean)


def matmul(left, right, over=(1, 0)):
    return lax.dot_general(
        left, right, (((over[0],), (over[1],)), ((), ())), preferred_element_type=wide
    )


def one_hot(shape, column_of_row):
    rows = lax.broadcasted_iota(jnp.int32, shape, 0)
    columns = lax.broadcasted_iota(jnp.int32, shape, 1)
    return jnp.where(columns == column_of_row(rows), 1.0, 0.0).astype(narrow)


def exchange(value, axes):
    return lax.all_to_all(value, axes, 0, 0, tiled=True)


def swap(value, axis):
    return lax.ppermute(value, axis, [(0, 1), (1, 0)])


def on_core(kernel, out_shape, scalars, arrays, scratch=(), flops=0, moved=0):
    multiple = isinstance(out_shape, (list, tuple))
    vmem = pl.BlockSpec(memory_space=pltpu.VMEM)
    return pl.pallas_call(
        kernel,
        out_shape=out_shape,
        in_specs=[pl.BlockSpec(memory_space=pltpu.SMEM)] * len(scalars) + [vmem] * len(arrays),
        out_specs=[vmem] * len(out_shape) if multiple else vmem,
        scratch_shapes=list(scratch),
        compiler_params=pltpu.CompilerParams(vmem_limit_bytes=VMEM_BYTES),
        cost_estimate=pl.CostEstimate(flops=flops, bytes_accessed=moved, transcendentals=0),
    )(*scalars, *arrays)


def pick_kernel(place_ref, six_ref, seven_ref, proj_ref, out_ref):
    plane, half, core, section = (place_ref[k] for k in range(4))
    lanes_conv = pl.ds(pl.multiple_of(lax.rem(section, 4) * LANES, LANES), LANES)
    first = section < 4
    conv = jnp.where(first, six_ref[:, lanes_conv].astype(wide), seven_ref[:, lanes_conv].astype(wide))
    row_tiles = proj_ref.shape[0] // TILE
    row = pl.multiple_of(jnp.minimum(plane, row_tiles - 1) * TILE, TILE)
    lane = pl.multiple_of((half * 2 + core) * LANES, LANES)
    block = jnp.concatenate(
        [conv.astype(narrow), proj_ref[pl.ds(row, TILE), pl.ds(lane, LANES)]], axis=0
    )
    out_ref[...] = jnp.broadcast_to(block[None], out_ref.shape)


def layer_kernel(
    place_ref,
    input_ref,
    own_ref,
    other_ref,
    grad_ref,
    gains_ref,
    biases_ref,
    back_ref,
    kept_ref,
    given_ref,
    six_ref,
    seven_ref,
    proj_ref,
    term_six_ref,
    term_seven_ref,
    term_proj_ref,
):
    core = place_ref[2]
    channels = input_ref.shape[1]
    frames = grad_ref.shape[0]
    lane_tiles = channels // LANES
    planes = own_ref.shape[0]
    sections = own_ref.shape[1] // 2
    width = grad_ref.shape[1]
    section_rows = width // sections
    row_tiles = section_rows // TILE

    def place_tiles(plane, carry):
        for half in range(2):
            for source, index in ((own_ref, core), (other_ref, 1 - core)):
                rows = pl.ds(
                    pl.multiple_of(((plane * 2 + half) * 2 + index) * TILE, TILE), TILE
                )
                for lane in range(lane_tiles):
                    lanes = slice(lane * LANES, (lane + 1) * LANES)
                    six_ref[rows, lanes] = source[plane, half * sections + lane, :TILE]
                    seven_ref[rows, lanes] = source[
                        plane, half * sections + lane_tiles + lane, :TILE
                    ]
        return carry

    lax.fori_loop(0, planes, place_tiles, 0)

    def place_proj(plane, carry):
        for half in range(2):
            for source, index in ((own_ref, core), (other_ref, 1 - core)):
                lanes = pl.ds(pl.multiple_of((half * 2 + index) * LANES, LANES), LANES)
                for section in range(sections):
                    rows = pl.ds(
                        pl.multiple_of(section * section_rows + plane * TILE, TILE), TILE
                    )
                    proj_ref[rows, lanes] = source[plane, half * sections + section, TILE:]
        return carry

    lax.fori_loop(0, row_tiles, place_proj, 0)

    count = 4 * frames

    def source_row(rows):
        run = rows // frames
        return 4 * (rows % frames) + (run % 2) * 2 + run // 2

    order = one_hot((count, count), source_row)
    positions = matmul(order, input_ref[...]).astype(narrow)
    tap_zero, tap_one = positions[: 2 * frames], positions[2 * frames :]
    hid_six = matmul(tap_zero, six_ref[:channels]) + matmul(tap_one, six_ref[channels:])
    pre_six, part_six, scale_six = norm_forward(hid_six, gains_ref[0:1], biases_ref[0:1])
    act_six_f, deriv_six = gelu_parts(pre_six)
    act_six = act_six_f.astype(narrow)
    act_zero, act_one = act_six[:frames], act_six[frames:]
    hid_seven = matmul(act_zero, seven_ref[:channels]) + matmul(act_one, seven_ref[channels:])
    pre_seven, part_seven, scale_seven = norm_forward(
        hid_seven, gains_ref[1:2], biases_ref[1:2]
    )
    act_seven_f, deriv_seven = gelu_parts(pre_seven)
    pre_feat, part_feat, scale_feat = norm_forward(
        act_seven_f.astype(narrow).astype(wide), gains_ref[2:3], biases_ref[2:3]
    )
    normed = pre_feat.astype(narrow)

    run = frames // (2 * sections)

    def arrived_row(rows):
        utterance = rows // (sections * run)
        rest = rows % (sections * run)
        return (rest // run) * (2 * run) + utterance * run + rest % run

    grad_rows = matmul(one_hot((frames, frames), arrived_row), grad_ref[...]).astype(narrow)
    term_proj_ref[...] = matmul(normed, grad_rows, (0, 0))

    grad_normed = matmul(grad_rows, proj_ref[...])
    dact_seven = norm_backward(grad_normed, part_feat, scale_feat, gains_ref[2:3])
    dpre_seven = dact_seven * deriv_seven
    dhid_seven = norm_backward(dpre_seven, part_seven, scale_seven, gains_ref[1:2]).astype(narrow)
    term_seven_ref[:channels] = matmul(act_zero, dhid_seven, (0, 0))
    term_seven_ref[channels:] = matmul(act_one, dhid_seven, (0, 0))
    dact_six = jnp.concatenate(
        [
            matmul(dhid_seven, seven_ref[:channels], (1, 1)),
            matmul(dhid_seven, seven_ref[channels:], (1, 1)),
        ],
        axis=0,
    )
    dpre_six = dact_six * deriv_six
    dhid_six = norm_backward(dpre_six, part_six, scale_six, gains_ref[0:1]).astype(narrow)
    term_six_ref[:channels] = matmul(tap_zero, dhid_six, (0, 0))
    term_six_ref[channels:] = matmul(tap_one, dhid_six, (0, 0))
    back = jnp.concatenate(
        [
            matmul(dhid_six, six_ref[:channels], (1, 1)).astype(narrow),
            matmul(dhid_six, six_ref[channels:], (1, 1)).astype(narrow),
        ],
        axis=0,
    )
    back_ref[...] = matmul(order, back, (0, 0)).astype(narrow)

    half_rows = TILE // 2

    def pack(plane, carry):
        for target, index in ((kept_ref, core), (given_ref, 1 - core)):
            proj_rows = []
            for half in range(2):
                group = (plane * 2 + half) * 2 + index
                rows = pl.ds(pl.multiple_of(group * TILE, TILE), TILE)
                for lane in range(lane_tiles):
                    lanes = slice(lane * LANES, (lane + 1) * LANES)
                    at = (half * lane_tiles + lane) * TILE
                    target[plane, at : at + TILE] = term_six_ref[rows, lanes].astype(narrow)
                    at += 2 * lane_tiles * TILE
                    target[plane, at : at + TILE] = term_seven_ref[rows, lanes].astype(narrow)
                proj_rows.append(
                    term_proj_ref[pl.ds(pl.multiple_of(group * half_rows, half_rows), half_rows)]
                )
            proj_block = jnp.concatenate(proj_rows, axis=0).astype(narrow)
            for lane in range(width // LANES):
                at = (4 * lane_tiles + lane) * TILE
                target[plane, at : at + TILE] = proj_block[:, lane * LANES : (lane + 1) * LANES]
        return carry

    lax.fori_loop(0, planes, pack, 0)

    def total(value):
        return jnp.sum(value, axis=0, keepdims=True)

    sums = jnp.concatenate(
        [
            total(dpre_six * part_six),
            total(dpre_seven * part_seven),
            total(grad_normed * part_feat),
            total(dpre_six),
            total(dpre_seven),
            total(grad_normed),
            jnp.zeros((2, channels), wide),
        ],
        axis=0,
    )
    sums = jnp.concatenate(
        [sums[:, lane * LANES : (lane + 1) * LANES] for lane in range(lane_tiles)], axis=0
    ).astype(narrow)
    at = (4 * lane_tiles + width // LANES) * TILE
    spread_sums = jnp.broadcast_to(sums[None], (planes,) + sums.shape)
    kept_ref[:, at:] = spread_sums
    given_ref[:, at:] = spread_sums


def add_kernel(left_ref, right_ref, out_ref):
    for plane in range(out_ref.shape[0]):
        out_ref[plane] = (left_ref[plane].astype(wide) + right_ref[plane].astype(wide)).astype(
            narrow
        )


def plane_kernel(arrived_ref, out_ref, total_ref):
    planes, rows = arrived_ref.shape[0], arrived_ref.shape[1]
    running = arrived_ref[0].astype(wide)
    for plane in range(1, planes):
        running += arrived_ref[plane].astype(wide)
    total_ref[...] = running
    sections = out_ref.shape[0] // 2
    lane_tiles = sections // 2
    proj_tiles = rows // TILE - 4 * lane_tiles - 2
    left = lax.broadcasted_iota(jnp.int32, (TILE, LANES), 1) < LANES // 2
    for half in range(2):
        for lane in range(lane_tiles):
            at = (half * lane_tiles + lane) * TILE
            six = total_ref[at : at + TILE]
            at += 2 * lane_tiles * TILE
            seven = total_ref[at : at + TILE]
            place = half * sections + 2 * lane
            out_ref[place, :TILE] = jnp.where(
                left, six, pltpu.roll(seven, LANES // 2, 1)
            ).astype(narrow)
            out_ref[place + 1, :TILE] = jnp.where(
                left, pltpu.roll(six, LANES // 2, 1), seven
            ).astype(narrow)
    base = 4 * lane_tiles * TILE
    proj = jnp.concatenate(
        [total_ref[base + lane * TILE : base + (lane + 1) * TILE] for lane in range(proj_tiles)],
        axis=1,
    )
    width = proj.shape[1]
    part = width // sections
    for section in range(sections):
        shift = (width - section * part) % width
        moved = pltpu.roll(proj, shift, 1) if shift else proj
        for half in range(2):
            rows_of = slice(half * (TILE // 2), (half + 1) * (TILE // 2))
            out_ref[half * sections + section, TILE : 2 * TILE] = jnp.concatenate(
                [moved[rows_of, :LANES], moved[rows_of, LANES : 2 * LANES]], axis=0
            ).astype(narrow)
    sums = total_ref[rows - 2 * TILE :].astype(narrow)
    out_ref[:, 2 * TILE :] = jnp.broadcast_to(sums[None], (2 * sections,) + sums.shape)


def line_kernel(arrived_ref, six_ref, seven_ref, proj_ref, gains_ref, biases_ref):
    running = arrived_ref[0].astype(wide)
    for source in range(1, arrived_ref.shape[0]):
        running += arrived_ref[source].astype(wide)
    half = LANES // 2
    six_ref[...] = running[:TILE, :half]
    seven_ref[...] = running[:TILE, half:]
    rows = TILE // 2
    proj = jnp.concatenate(
        [running[TILE : TILE + rows], running[TILE + rows : 2 * TILE]], axis=1
    )
    proj_ref[...] = proj[:, : proj_ref.shape[1]]
    sums = jnp.concatenate(
        [running[2 * TILE + k * rows : 2 * TILE + (k + 1) * rows] for k in range(4)], axis=1
    )
    gains_ref[...] = sums[:3]
    biases_ref[...] = sums[3:6]


def on_device(layer_five, conv_six, conv_seven, gains, biases, proj_weight, feature_grad):
    utt_local, positions, channels = layer_five.shape
    width = feature_grad.shape[2]
    part_width = proj_weight.shape[1]
    sections = lax.axis_size("s")
    planes = lax.axis_size(("y", "x"))
    frames = utt_local * positions // 4
    shape = jax.ShapeDtypeStruct
    place = jnp.stack(
        [lax.axis_index(("y", "x")), lax.axis_index("zh"), lax.axis_index("c"), lax.axis_index("s")]
    ).astype(jnp.int32)

    picked = on_core(
        pick_kernel,
        shape((2 * sections, 2 * TILE, LANES), narrow),
        [place],
        [conv_six, conv_seven, proj_weight.T],
    )
    line = exchange(picked, ("zh", "s"))
    bundle = line.reshape(1, 2 * sections * 2 * TILE, LANES)
    gathered = exchange(jnp.broadcast_to(bundle, (planes,) + bundle.shape[1:]), ("y", "x"))
    gathered_flat = gathered.reshape(-1, LANES)
    sibling = swap(gathered_flat, "c")

    grads = exchange(feature_grad.reshape(sections, -1, width), "s").reshape(frames, width)

    tiles_shape = (planes, 2 * sections, 2 * TILE, LANES)
    send_rows = (4 * (channels // LANES) + width // LANES + 2) * TILE
    back, kept, given = on_core(
        layer_kernel,
        [
            shape((4 * frames, channels), narrow),
            shape((planes, send_rows, LANES), narrow),
            shape((planes, send_rows, LANES), narrow),
        ],
        [place],
        [
            layer_five.reshape(4 * frames, channels),
            gathered.reshape(tiles_shape),
            sibling.reshape(tiles_shape),
            grads,
            gains,
            biases,
        ],
        scratch=[
            pltpu.VMEM((2 * channels, channels), narrow),
            pltpu.VMEM((2 * channels, channels), narrow),
            pltpu.VMEM((width, channels), narrow),
            pltpu.VMEM((2 * channels, channels), wide),
            pltpu.VMEM((2 * channels, channels), wide),
            pltpu.VMEM((channels, width), wide),
        ],
    )
    received = swap(given.reshape(-1, LANES), "c").reshape(given.shape)
    chip = on_core(add_kernel, shape(kept.shape, narrow), [], [kept, received])
    plane_in = exchange(chip, ("y", "x"))
    line_out = on_core(
        plane_kernel,
        shape((2 * sections, 4 * TILE, LANES), narrow),
        [],
        [plane_in],
        scratch=[pltpu.VMEM((send_rows, LANES), wide)],
    )
    line_in = exchange(line_out, ("zh", "s"))
    out_six, out_seven, out_proj, out_gains, out_biases = on_core(
        line_kernel,
        [
            shape((TILE, channels // sections), wide),
            shape((TILE, channels // sections), wide),
            shape((TILE // 2, part_width), wide),
            shape((3, channels), wide),
            shape((3, channels), wide),
        ],
        [],
        [line_in],
    )
    return (
        back.reshape(utt_local, positions, channels),
        out_six,
        out_seven,
        out_proj,
        out_gains,
        out_biases,
    )


def solution(mesh):
    fine = Mesh(mesh.devices.reshape(4, 4, 2, 2, 8), ("y", "x", "zh", "c", "s"))
    tm = ("y", "x", "zh", "c")
    return jax.shard_map(
        on_device,
        mesh=fine,
        in_specs=(
            P("s", tm, None),
            P(tm, None),
            P(tm, None),
            P(),
            P(),
            P(None, "s"),
            P(None, tm + ("s",), None),
        ),
        out_specs=(
            P("s", tm, None),
            P(tm, "s"),
            P(tm, "s"),
            P(tm, "s"),
            P(),
            P(),
        ),
        check_vma=False,
    )
```

```python
import jax
import jax.numpy as jnp
from jax import lax
from jax.experimental import pallas as pl
from jax.experimental.pallas import tpu as pltpu
from jax.sharding import Mesh, PartitionSpec as P

norm_epsilon = 1e-05
half_root = 0.7071067811865476
inv_root_tau = 0.3989422804014327
narrow = jnp.bfloat16
wide = jnp.float32
LANES = 128
TILE = 16


def gelu_parts(preact):
    normal_cdf = 0.5 * (1.0 + lax.erf(preact * half_root))
    density = jnp.exp(-0.5 * preact * preact) * inv_root_tau
    return (preact * normal_cdf, normal_cdf + preact * density)


def norm_forward(hidden, gain_row, bias_row):
    average = jnp.mean(hidden, axis=-1, keepdims=True)
    centred = hidden - average
    inv_scale = lax.rsqrt(jnp.mean(centred * centred, axis=-1, keepdims=True) + norm_epsilon)
    normal_part = centred * inv_scale
    return (normal_part * gain_row + bias_row, normal_part, inv_scale)


def norm_backward(incoming, normal_part, inv_scale, gain_row):
    scaled = incoming * gain_row
    first_mean = jnp.mean(scaled, axis=-1, keepdims=True)
    second_mean = jnp.mean(scaled * normal_part, axis=-1, keepdims=True)
    return inv_scale * (scaled - first_mean - normal_part * second_mean)


def matmul(left, right, over=(1, 0)):
    return lax.dot_general(
        left, right, (((over[0],), (over[1],)), ((), ())), preferred_element_type=wide
    )


def one_hot(shape, column_of_row):
    rows = lax.broadcasted_iota(jnp.int32, shape, 0)
    columns = lax.broadcasted_iota(jnp.int32, shape, 1)
    return jnp.where(columns == column_of_row(rows), 1.0, 0.0).astype(narrow)


def exchange(value, axes):
    return lax.all_to_all(value, axes, 0, 0, tiled=True)


def swap(value, axis):
    return lax.ppermute(value, axis, [(0, 1), (1, 0)])


def on_core(kernel, out_shape, scalars, arrays, scratch=(), megabytes=8):
    multiple = isinstance(out_shape, (list, tuple))
    vmem = pl.BlockSpec(memory_space=pltpu.VMEM)
    return pl.pallas_call(
        kernel,
        out_shape=out_shape,
        in_specs=[pl.BlockSpec(memory_space=pltpu.SMEM)] * len(scalars) + [vmem] * len(arrays),
        out_specs=[vmem] * len(out_shape) if multiple else vmem,
        scratch_shapes=list(scratch),
        compiler_params=pltpu.CompilerParams(vmem_limit_bytes=megabytes * 1024 * 1024),
    )(*scalars, *arrays)


def pick_kernel(place_ref, six_ref, seven_ref, proj_ref, grad_ref, conv_ref, out_ref):
    plane, core = place_ref[0], place_ref[2]
    lane_tiles = six_ref.shape[1] // LANES
    for index, source in enumerate((six_ref, seven_ref)):
        for lane in range(lane_tiles):
            at = (index * lane_tiles + lane) * TILE
            conv_ref[at : at + TILE] = source[:, lane * LANES : (lane + 1) * LANES]

    sections = out_ref.shape[0]
    rows = grad_ref.shape[0] // sections
    width = grad_ref.shape[1]
    wide_tiles = width // LANES
    proj_at = (wide_tiles + 1) // 2 * TILE
    row_tiles = proj_ref.shape[0] // TILE
    row = pl.multiple_of(jnp.minimum(plane, row_tiles - 1) * TILE, TILE)
    proj = [
        proj_ref[pl.ds(row, TILE), pl.ds(pl.multiple_of((core * 2 + k) * LANES, LANES), LANES)]
        for k in range(2)
    ]
    for pair in range(sections // 2):
        block = grad_ref[pair * 2 * rows : (pair + 1) * 2 * rows].astype(wide)
        block = jnp.concatenate([block, jnp.zeros((2 * rows, LANES), wide)], axis=1)
        for inner in range(2):
            section = pair * 2 + inner
            part = block[inner * rows : (inner + 1) * rows]
            for tile in range(proj_at // TILE):
                lane = 2 * tile * LANES
                stacked = jnp.concatenate(
                    [part[:, lane : lane + LANES], part[:, lane + LANES : lane + 2 * LANES]], axis=0
                )
                out_ref[section, tile * TILE : (tile + 1) * TILE] = stacked.astype(narrow)
            for k in range(2):
                out_ref[section, proj_at + k * TILE : proj_at + (k + 1) * TILE] = proj[k]


def bundle_kernel(place_ref, own_ref, other_ref, arrived_ref, out_ref):
    half = place_ref[1]
    rows = own_ref.shape[0]
    out_ref[pl.ds(pl.multiple_of(half * rows, TILE), rows)] = own_ref[...]
    out_ref[pl.ds(pl.multiple_of((1 - half) * rows, TILE), rows)] = other_ref[...]
    start = arrived_ref.shape[1] - 2 * TILE
    for section in range(arrived_ref.shape[0]):
        at = 2 * rows + section * 2 * TILE
        out_ref[at : at + 2 * TILE] = arrived_ref[section, start:]


def layer_kernel(
    place_ref,
    input_ref,
    own_ref,
    other_ref,
    grad_ref,
    gains_ref,
    biases_ref,
    back_ref,
    kept_ref,
    given_ref,
    six_ref,
    seven_ref,
    proj_ref,
    rows_ref,
    term_six_ref,
    term_seven_ref,
    term_proj_ref,
):
    core = place_ref[2]
    channels = input_ref.shape[1]
    frames, width = rows_ref.shape
    lane_tiles = channels // LANES
    planes = own_ref.shape[0]
    sections = grad_ref.shape[0]
    section_rows = width // sections
    row_tiles = section_rows // TILE

    def place_tiles(plane, carry):
        for half in range(2):
            for source, index in ((own_ref, core), (other_ref, 1 - core)):
                rows = pl.ds(
                    pl.multiple_of(((plane * 2 + half) * 2 + index) * TILE, TILE), TILE
                )
                for lane in range(lane_tiles):
                    lanes = slice(lane * LANES, (lane + 1) * LANES)
                    tile = half * 2 * lane_tiles + lane
                    six_ref[rows, lanes] = source[plane, tile]
                    seven_ref[rows, lanes] = source[plane, tile + lane_tiles]
        return carry

    lax.fori_loop(0, planes, place_tiles, 0)

    def place_proj(plane, carry):
        for k in range(2):
            for source, index in ((own_ref, core), (other_ref, 1 - core)):
                lanes = pl.ds(pl.multiple_of((index * 2 + k) * LANES, LANES), LANES)
                for section in range(sections):
                    rows = pl.ds(
                        pl.multiple_of(section * section_rows + plane * TILE, TILE), TILE
                    )
                    tile = 4 * lane_tiles + section * 2 + k
                    proj_ref[rows, lanes] = source[plane, tile]
        return carry

    lax.fori_loop(0, row_tiles, place_proj, 0)

    count = 4 * frames

    def source_row(rows):
        run = rows // frames
        return 4 * (rows % frames) + (run % 2) * 2 + run // 2

    order = one_hot((count, count), source_row)
    positions = matmul(order, input_ref[...]).astype(narrow)
    tap_zero, tap_one = positions[: 2 * frames], positions[2 * frames :]
    hid_six = matmul(tap_zero, six_ref[:channels]) + matmul(tap_one, six_ref[channels:])
    pre_six, part_six, scale_six = norm_forward(hid_six, gains_ref[0:1], biases_ref[0:1])
    act_six_f, deriv_six = gelu_parts(pre_six)
    act_six = act_six_f.astype(narrow)
    act_zero, act_one = act_six[:frames], act_six[frames:]
    hid_seven = matmul(act_zero, seven_ref[:channels]) + matmul(act_one, seven_ref[channels:])
    pre_seven, part_seven, scale_seven = norm_forward(
        hid_seven, gains_ref[1:2], biases_ref[1:2]
    )
    act_seven_f, deriv_seven = gelu_parts(pre_seven)
    pre_feat, part_feat, scale_feat = norm_forward(
        act_seven_f.astype(narrow).astype(wide), gains_ref[2:3], biases_ref[2:3]
    )
    normed = pre_feat.astype(narrow)

    run = frames // (2 * sections)

    def arrived_row(rows):
        utterance = rows // (sections * run)
        rest = rows % (sections * run)
        return (rest // run) * (2 * run) + utterance * run + rest % run

    eight = frames // sections
    for section in range(sections):
        for lane in range(width // LANES):
            if lane % 2 == 0:
                stacked = grad_ref[section, lane // 2 * TILE : (lane // 2 + 1) * TILE].astype(wide)
            rows_ref[
                section * eight : (section + 1) * eight, lane * LANES : (lane + 1) * LANES
            ] = stacked[(lane % 2) * eight : (lane % 2 + 1) * eight]
    grad_rows = matmul(
        one_hot((frames, frames), arrived_row), rows_ref[...].astype(narrow)
    ).astype(narrow)
    term_proj_ref[...] = matmul(normed, grad_rows, (0, 0))

    grad_normed = matmul(grad_rows, proj_ref[...])
    dact_seven = norm_backward(grad_normed, part_feat, scale_feat, gains_ref[2:3])
    dpre_seven = dact_seven * deriv_seven
    dhid_seven = norm_backward(dpre_seven, part_seven, scale_seven, gains_ref[1:2]).astype(narrow)
    term_seven_ref[:channels] = matmul(act_zero, dhid_seven, (0, 0))
    term_seven_ref[channels:] = matmul(act_one, dhid_seven, (0, 0))
    dact_six = jnp.concatenate(
        [
            matmul(dhid_seven, seven_ref[:channels], (1, 1)),
            matmul(dhid_seven, seven_ref[channels:], (1, 1)),
        ],
        axis=0,
    )
    dpre_six = dact_six * deriv_six
    dhid_six = norm_backward(dpre_six, part_six, scale_six, gains_ref[0:1]).astype(narrow)
    term_six_ref[:channels] = matmul(tap_zero, dhid_six, (0, 0))
    term_six_ref[channels:] = matmul(tap_one, dhid_six, (0, 0))
    back = jnp.concatenate(
        [
            matmul(dhid_six, six_ref[:channels], (1, 1)).astype(narrow),
            matmul(dhid_six, six_ref[channels:], (1, 1)).astype(narrow),
        ],
        axis=0,
    )
    back_ref[...] = matmul(order, back, (0, 0)).astype(narrow)

    half_rows = TILE // 2

    def pack(plane, carry):
        for target, index in ((kept_ref, core), (given_ref, 1 - core)):
            proj_rows = []
            for half in range(2):
                group = (plane * 2 + half) * 2 + index
                rows = pl.ds(pl.multiple_of(group * TILE, TILE), TILE)
                for lane in range(lane_tiles):
                    lanes = slice(lane * LANES, (lane + 1) * LANES)
                    at = (half * lane_tiles + lane) * TILE
                    target[plane, at : at + TILE] = term_six_ref[rows, lanes].astype(narrow)
                    at += 2 * lane_tiles * TILE
                    target[plane, at : at + TILE] = term_seven_ref[rows, lanes].astype(narrow)
                proj_rows.append(
                    term_proj_ref[pl.ds(pl.multiple_of(group * half_rows, half_rows), half_rows)]
                )
            proj_block = jnp.concatenate(proj_rows, axis=0).astype(narrow)
            for lane in range(width // LANES):
                at = (4 * lane_tiles + lane) * TILE
                target[plane, at : at + TILE] = proj_block[:, lane * LANES : (lane + 1) * LANES]
        return carry

    lax.fori_loop(0, planes, pack, 0)

    def total(value):
        return jnp.sum(value, axis=0, keepdims=True)

    sums = jnp.concatenate(
        [
            total(dpre_six * part_six),
            total(dpre_seven * part_seven),
            total(grad_normed * part_feat),
            total(dpre_six),
            total(dpre_seven),
            total(grad_normed),
            jnp.zeros((2, channels), wide),
        ],
        axis=0,
    )
    sums = jnp.concatenate(
        [sums[:, lane * LANES : (lane + 1) * LANES] for lane in range(lane_tiles)], axis=0
    ).astype(narrow)
    at = (4 * lane_tiles + width // LANES) * TILE
    spread_sums = jnp.broadcast_to(sums[None], (planes,) + sums.shape)
    kept_ref[:, at:] = spread_sums
    given_ref[:, at:] = spread_sums


def plane_kernel(arrived_ref, out_ref, total_ref):
    planes, rows = arrived_ref.shape[0], arrived_ref.shape[1]
    running = arrived_ref[0].astype(wide)
    for plane in range(1, planes):
        running += arrived_ref[plane].astype(wide)
    total_ref[...] = running
    sections = out_ref.shape[0] // 2
    lane_tiles = sections // 2
    proj_tiles = rows // TILE - 4 * lane_tiles - 2
    left = lax.broadcasted_iota(jnp.int32, (TILE, LANES), 1) < LANES // 2
    for half in range(2):
        for lane in range(lane_tiles):
            at = (half * lane_tiles + lane) * TILE
            six = total_ref[at : at + TILE]
            at += 2 * lane_tiles * TILE
            seven = total_ref[at : at + TILE]
            place = half * sections + 2 * lane
            out_ref[place, :TILE] = jnp.where(
                left, six, pltpu.roll(seven, LANES // 2, 1)
            ).astype(narrow)
            out_ref[place + 1, :TILE] = jnp.where(
                left, pltpu.roll(six, LANES // 2, 1), seven
            ).astype(narrow)
    base = 4 * lane_tiles * TILE
    proj = jnp.concatenate(
        [total_ref[base + lane * TILE : base + (lane + 1) * TILE] for lane in range(proj_tiles)],
        axis=1,
    )
    width = proj.shape[1]
    part = width // sections
    for section in range(sections):
        shift = (width - section * part) % width
        moved = pltpu.roll(proj, shift, 1) if shift else proj
        for half in range(2):
            rows_of = slice(half * (TILE // 2), (half + 1) * (TILE // 2))
            out_ref[half * sections + section, TILE : 2 * TILE] = jnp.concatenate(
                [moved[rows_of, :LANES], moved[rows_of, LANES : 2 * LANES]], axis=0
            ).astype(narrow)
    sums = total_ref[rows - 2 * TILE :].astype(narrow)
    out_ref[:, 2 * TILE :] = jnp.broadcast_to(sums[None], (2 * sections,) + sums.shape)


def line_kernel(arrived_ref, six_ref, seven_ref, proj_ref, gains_ref, biases_ref):
    running = arrived_ref[0].astype(wide)
    for source in range(1, arrived_ref.shape[0]):
        running += arrived_ref[source].astype(wide)
    half = LANES // 2
    six_ref[...] = running[:TILE, :half]
    seven_ref[...] = running[:TILE, half:]
    rows = TILE // 2
    proj = jnp.concatenate(
        [running[TILE : TILE + rows], running[TILE + rows : 2 * TILE]], axis=1
    )
    proj_ref[...] = proj[:, : proj_ref.shape[1]]
    sums = jnp.concatenate(
        [running[2 * TILE + k * rows : 2 * TILE + (k + 1) * rows] for k in range(4)], axis=1
    )
    gains_ref[...] = sums[:3]
    biases_ref[...] = sums[3:6]


def on_device(layer_five, conv_six, conv_seven, gains, biases, proj_weight, feature_grad):
    utt_local, positions, channels = layer_five.shape
    width = feature_grad.shape[2]
    part_width = proj_weight.shape[1]
    sections = lax.axis_size("s")
    planes = lax.axis_size(("y", "x"))
    frames = utt_local * positions // 4
    shape = jax.ShapeDtypeStruct
    place = jnp.stack(
        [lax.axis_index(("y", "x")), lax.axis_index("zh"), lax.axis_index("c"), lax.axis_index("s")]
    ).astype(jnp.int32)

    tile_rows = 2 * (channels // LANES) * TILE
    grad_tiles = (width // LANES + 1) // 2
    convs, outgoing = on_core(
        pick_kernel,
        [
            shape((tile_rows, LANES), narrow),
            shape((sections, (grad_tiles + 2) * TILE, LANES), narrow),
        ],
        [place],
        [conv_six, conv_seven, proj_weight.T, feature_grad.reshape(frames, width)],
    )
    line = 2 * sections
    opposite = [
        (z, (1 - z // sections) * sections + (z % sections + sections // 2) % sections)
        for z in range(line)
    ]
    other_convs = lax.ppermute(convs, ("zh", "s"), opposite)
    arrived = exchange(outgoing, "s")
    bundle = on_core(
        bundle_kernel,
        shape((2 * tile_rows + sections * 2 * TILE, LANES), narrow),
        [place],
        [convs, other_convs, arrived],
    )
    gathered = exchange(jnp.broadcast_to(bundle[None], (planes,) + bundle.shape), ("y", "x"))
    sibling = swap(gathered.reshape(-1, LANES), "c")

    tiles_shape = (planes, bundle.shape[0] // TILE, TILE, LANES)
    send_rows = (4 * (channels // LANES) + width // LANES + 2) * TILE
    back, kept, given = on_core(
        layer_kernel,
        [
            shape((4 * frames, channels), narrow),
            shape((planes, send_rows, LANES), narrow),
            shape((planes, send_rows, LANES), narrow),
        ],
        [place],
        [
            layer_five.reshape(4 * frames, channels),
            gathered.reshape(tiles_shape),
            sibling.reshape(tiles_shape),
            arrived,
            gains,
            biases,
        ],
        scratch=[
            pltpu.VMEM((2 * channels, channels), narrow),
            pltpu.VMEM((2 * channels, channels), narrow),
            pltpu.VMEM((width, channels), narrow),
            pltpu.VMEM((frames, width), wide),
            pltpu.VMEM((2 * channels, channels), wide),
            pltpu.VMEM((2 * channels, channels), wide),
            pltpu.VMEM((channels, width), wide),
        ],
        megabytes=36,
    )
    received = swap(given.reshape(-1, LANES), "c").reshape(given.shape)
    chip = (kept.astype(wide) + received.astype(wide)).astype(narrow)
    plane_in = exchange(chip, ("y", "x"))
    line_out = on_core(
        plane_kernel,
        shape((2 * sections, 4 * TILE, LANES), narrow),
        [],
        [plane_in],
        scratch=[pltpu.VMEM((send_rows, LANES), wide)],
    )
    line_in = exchange(line_out, ("zh", "s"))
    out_six, out_seven, out_proj, out_gains, out_biases = on_core(
        line_kernel,
        [
            shape((TILE, channels // sections), wide),
            shape((TILE, channels // sections), wide),
            shape((TILE // 2, part_width), wide),
            shape((3, channels), wide),
            shape((3, channels), wide),
        ],
        [],
        [line_in],
    )
    return (
        back.reshape(utt_local, positions, channels),
        out_six,
        out_seven,
        out_proj,
        out_gains,
        out_biases,
    )


def solution(mesh):
    fine = Mesh(mesh.devices.reshape(4, 4, 2, 2, 8), ("y", "x", "zh", "c", "s"))
    tm = ("y", "x", "zh", "c")
    return jax.shard_map(
        on_device,
        mesh=fine,
        in_specs=(
            P("s", tm, None),
            P(tm, None),
            P(tm, None),
            P(),
            P(),
            P(None, "s"),
            P(None, tm + ("s",), None),
        ),
        out_specs=(
            P("s", tm, None),
            P(tm, "s"),
            P(tm, "s"),
            P(tm, "s"),
            P(),
            P(),
        ),
        check_vma=False,
    )
```

```python
import jax
import jax.numpy as jnp
from jax import lax
from jax.experimental import pallas as pl
from jax.experimental.pallas import tpu as pltpu
from jax.sharding import Mesh, PartitionSpec as P

norm_epsilon = 1e-05
half_root = 0.7071067811865476
inv_root_tau = 0.3989422804014327
narrow = jnp.bfloat16
wide = jnp.float32
LANES = 128
TILE = 16


def gelu_parts(preact):
    normal_cdf = 0.5 * (1.0 + lax.erf(preact * half_root))
    density = jnp.exp(-0.5 * preact * preact) * inv_root_tau
    return (preact * normal_cdf, normal_cdf + preact * density)


def norm_forward(hidden, gain_row, bias_row):
    average = jnp.mean(hidden, axis=-1, keepdims=True)
    centred = hidden - average
    inv_scale = lax.rsqrt(jnp.mean(centred * centred, axis=-1, keepdims=True) + norm_epsilon)
    normal_part = centred * inv_scale
    return (normal_part * gain_row + bias_row, normal_part, inv_scale)


def norm_backward(incoming, normal_part, inv_scale, gain_row):
    scaled = incoming * gain_row
    first_mean = jnp.mean(scaled, axis=-1, keepdims=True)
    second_mean = jnp.mean(scaled * normal_part, axis=-1, keepdims=True)
    return inv_scale * (scaled - first_mean - normal_part * second_mean)


def matmul(left, right, over=(1, 0)):
    return lax.dot_general(
        left, right, (((over[0],), (over[1],)), ((), ())), preferred_element_type=wide
    )


def one_hot(shape, column_of_row):
    rows = lax.broadcasted_iota(jnp.int32, shape, 0)
    columns = lax.broadcasted_iota(jnp.int32, shape, 1)
    return jnp.where(columns == column_of_row(rows), 1.0, 0.0).astype(narrow)


def exchange(value, axes):
    return lax.all_to_all(value, axes, 0, 0, tiled=True)


def swap(value, axis):
    return lax.ppermute(value, axis, [(0, 1), (1, 0)])


def on_core(kernel, out_shape, scalars, arrays, scratch=(), megabytes=8):
    multiple = isinstance(out_shape, (list, tuple))
    vmem = pl.BlockSpec(memory_space=pltpu.VMEM)
    return pl.pallas_call(
        kernel,
        out_shape=out_shape,
        in_specs=[pl.BlockSpec(memory_space=pltpu.SMEM)] * len(scalars) + [vmem] * len(arrays),
        out_specs=[vmem] * len(out_shape) if multiple else vmem,
        scratch_shapes=list(scratch),
        compiler_params=pltpu.CompilerParams(vmem_limit_bytes=megabytes * 1024 * 1024),
    )(*scalars, *arrays)


def conv_kernel(six_ref, seven_ref, conv_ref):
    lane_tiles = six_ref.shape[1] // LANES
    for index, source in enumerate((six_ref, seven_ref)):
        for lane in range(lane_tiles):
            at = (index * lane_tiles + lane) * TILE
            conv_ref[at : at + TILE] = source[:, lane * LANES : (lane + 1) * LANES]


def pick_kernel(place_ref, proj_ref, grad_ref, out_ref):
    sections = out_ref.shape[0]
    utterances = grad_ref.shape[0] // sections
    width = grad_ref.shape[2]
    proj_at = (width // LANES + 1) // 2 * TILE
    for section in range(sections):
        part = jnp.concatenate(
            [grad_ref[section * utterances + k].astype(wide) for k in range(utterances)], axis=0
        )
        part = jnp.concatenate([part, jnp.zeros((part.shape[0], LANES), wide)], axis=1)
        for tile in range(proj_at // TILE):
            lane = 2 * tile * LANES
            stacked = jnp.concatenate(
                [part[:, lane : lane + LANES], part[:, lane + LANES : lane + 2 * LANES]], axis=0
            )
            out_ref[section, tile * TILE : (tile + 1) * TILE] = stacked.astype(narrow)
        for k in range(2):
            out_ref[section, proj_at + k * TILE : proj_at + (k + 1) * TILE] = proj_ref[
                :, k * LANES : (k + 1) * LANES
            ]


def bundle_kernel(place_ref, own_ref, other_ref, arrived_ref, out_ref):
    half = place_ref[1]
    rows = own_ref.shape[0]
    start = arrived_ref.shape[1] - 2 * TILE
    for plane in range(out_ref.shape[0]):
        out_ref[plane, pl.ds(pl.multiple_of(half * rows, TILE), rows)] = own_ref[...]
        out_ref[plane, pl.ds(pl.multiple_of((1 - half) * rows, TILE), rows)] = other_ref[...]
        for section in range(arrived_ref.shape[0]):
            at = 2 * rows + section * 2 * TILE
            out_ref[plane, at : at + 2 * TILE] = arrived_ref[section, start:]


def position_order(frames):
    def source_row(rows):
        run = rows // frames
        return 4 * (rows % frames) + (run % 2) * 2 + run // 2

    return one_hot((4 * frames, 4 * frames), source_row)


def place_proj(source_ref, proj_ref, row_tiles, section_rows):
    sections = proj_ref.shape[0] // section_rows
    first = source_ref.shape[1] - 2 * sections

    def step(plane, carry):
        for section in range(sections):
            rows = pl.ds(pl.multiple_of(section * section_rows + plane * TILE, TILE), TILE)
            for k in range(2):
                proj_ref[rows, k * LANES : (k + 1) * LANES] = source_ref[
                    plane, first + section * 2 + k
                ]
        return carry

    lax.fori_loop(0, row_tiles, step, 0)


def early_kernel(input_ref, own_ref, grad_ref, taps_ref, cotangent_ref, part_ref, proj_ref, rows_ref):
    frames, width = rows_ref.shape
    sections = grad_ref.shape[0]
    taps_ref[...] = matmul(position_order(frames), input_ref[...]).astype(narrow)

    run = frames // (2 * sections)

    def arrived_row(rows):
        utterance = rows // (sections * run)
        rest = rows % (sections * run)
        return (rest // run) * (2 * run) + utterance * run + rest % run

    eight = frames // sections
    for section in range(sections):
        for lane in range(width // LANES):
            if lane % 2 == 0:
                stacked = grad_ref[section, lane // 2 * TILE : (lane // 2 + 1) * TILE].astype(wide)
            rows_ref[
                section * eight : (section + 1) * eight, lane * LANES : (lane + 1) * LANES
            ] = stacked[(lane % 2) * eight : (lane % 2 + 1) * eight]
    grad_rows = matmul(
        one_hot((frames, frames), arrived_row), rows_ref[...].astype(narrow)
    ).astype(narrow)
    cotangent_ref[...] = grad_rows
    place_proj(own_ref, proj_ref, width // sections // TILE, width // sections)
    part_ref[...] = matmul(grad_rows, proj_ref[...])


def layer_kernel(
    place_ref,
    taps_ref,
    own_ref,
    other_ref,
    cotangent_ref,
    part_ref,
    gains_ref,
    biases_ref,
    six_ref,
    dhid_ref,
    kept_ref,
    given_ref,
    seven_ref,
    proj_ref,
    term_six_ref,
    term_seven_ref,
    term_proj_ref,
):
    core = place_ref[2]
    channels = taps_ref.shape[1]
    frames, width = cotangent_ref.shape
    lane_tiles = channels // LANES
    planes = own_ref.shape[0]
    sections = (own_ref.shape[1] - 4 * lane_tiles) // 2
    section_rows = width // sections

    def place_tiles(plane, carry):
        for half in range(2):
            for source, index in ((own_ref, core), (other_ref, 1 - core)):
                rows = pl.ds(
                    pl.multiple_of(((plane * 2 + half) * 2 + index) * TILE, TILE), TILE
                )
                for lane in range(lane_tiles):
                    lanes = slice(lane * LANES, (lane + 1) * LANES)
                    tile = half * 2 * lane_tiles + lane
                    six_ref[rows, lanes] = source[plane, tile]
                    seven_ref[rows, lanes] = source[plane, tile + lane_tiles]
        return carry

    lax.fori_loop(0, planes, place_tiles, 0)

    place_proj(other_ref, proj_ref, section_rows // TILE, section_rows)
    tap_zero, tap_one = taps_ref[: 2 * frames], taps_ref[2 * frames :]
    hid_six = matmul(tap_zero, six_ref[:channels]) + matmul(tap_one, six_ref[channels:])
    pre_six, part_six, scale_six = norm_forward(hid_six, gains_ref[0:1], biases_ref[0:1])
    act_six_f, deriv_six = gelu_parts(pre_six)
    act_six = act_six_f.astype(narrow)
    act_zero, act_one = act_six[:frames], act_six[frames:]
    hid_seven = matmul(act_zero, seven_ref[:channels]) + matmul(act_one, seven_ref[channels:])
    pre_seven, part_seven, scale_seven = norm_forward(
        hid_seven, gains_ref[1:2], biases_ref[1:2]
    )
    act_seven_f, deriv_seven = gelu_parts(pre_seven)
    pre_feat, part_feat, scale_feat = norm_forward(
        act_seven_f.astype(narrow).astype(wide), gains_ref[2:3], biases_ref[2:3]
    )
    normed = pre_feat.astype(narrow)

    grad_rows = cotangent_ref[...]
    term_proj_ref[...] = matmul(normed, grad_rows, (0, 0))
    own_half, other_half = part_ref[...], matmul(grad_rows, proj_ref[...])
    first = core == 0
    grad_normed = jnp.concatenate(
        [jnp.where(first, own_half, other_half), jnp.where(first, other_half, own_half)], axis=1
    )
    dact_seven = norm_backward(grad_normed, part_feat, scale_feat, gains_ref[2:3])
    dpre_seven = dact_seven * deriv_seven
    dhid_seven = norm_backward(dpre_seven, part_seven, scale_seven, gains_ref[1:2]).astype(narrow)
    term_seven_ref[:channels] = matmul(act_zero, dhid_seven, (0, 0))
    term_seven_ref[channels:] = matmul(act_one, dhid_seven, (0, 0))
    dact_six = jnp.concatenate(
        [
            matmul(dhid_seven, seven_ref[:channels], (1, 1)),
            matmul(dhid_seven, seven_ref[channels:], (1, 1)),
        ],
        axis=0,
    )
    dpre_six = dact_six * deriv_six
    dhid_six = norm_backward(dpre_six, part_six, scale_six, gains_ref[0:1]).astype(narrow)
    dhid_ref[...] = dhid_six
    term_six_ref[:channels] = matmul(tap_zero, dhid_six, (0, 0))
    term_six_ref[channels:] = matmul(tap_one, dhid_six, (0, 0))
    half_rows = TILE // 2

    def pack(plane, carry):
        for target, index in ((kept_ref, core), (given_ref, 1 - core)):
            proj_rows = []
            for half in range(2):
                group = (plane * 2 + half) * 2 + index
                rows = pl.ds(pl.multiple_of(group * TILE, TILE), TILE)
                for lane in range(lane_tiles):
                    lanes = slice(lane * LANES, (lane + 1) * LANES)
                    at = (half * lane_tiles + lane) * TILE
                    target[plane, at : at + TILE] = term_six_ref[rows, lanes].astype(narrow)
                    at += 2 * lane_tiles * TILE
                    target[plane, at : at + TILE] = term_seven_ref[rows, lanes].astype(narrow)
                proj_rows.append(
                    term_proj_ref[pl.ds(pl.multiple_of(group * half_rows, half_rows), half_rows)]
                )
            proj_block = jnp.concatenate(proj_rows, axis=0).astype(narrow)
            for lane in range(width // LANES):
                at = (4 * lane_tiles + lane) * TILE
                target[plane, at : at + TILE] = proj_block[:, lane * LANES : (lane + 1) * LANES]
        return carry

    lax.fori_loop(0, planes, pack, 0)

    def total(value):
        return jnp.sum(value, axis=0, keepdims=True)

    sums = jnp.concatenate(
        [
            total(dpre_six * part_six),
            total(dpre_seven * part_seven),
            total(grad_normed * part_feat),
            total(dpre_six),
            total(dpre_seven),
            total(grad_normed),
        ],
        axis=0,
    )
    sums = jnp.concatenate(
        [sums[:, lane * LANES : (lane + 1) * LANES] for lane in range(lane_tiles)]
        + [jnp.zeros((TILE // 2, LANES), wide)],
        axis=0,
    ).astype(narrow)
    at = (4 * lane_tiles + width // LANES) * TILE
    spread_sums = jnp.broadcast_to(sums[None], (planes,) + sums.shape)
    kept_ref[:, at:] = spread_sums
    given_ref[:, at:] = spread_sums


def input_kernel(dhid_ref, six_ref, back_ref):
    channels = back_ref.shape[1]
    back = jnp.concatenate(
        [
            matmul(dhid_ref[...], six_ref[:channels], (1, 1)).astype(narrow),
            matmul(dhid_ref[...], six_ref[channels:], (1, 1)).astype(narrow),
        ],
        axis=0,
    )
    back_ref[...] = matmul(position_order(back_ref.shape[0] // 4), back, (0, 0)).astype(narrow)


def plane_kernel(arrived_ref, out_ref, total_ref):
    planes, rows = arrived_ref.shape[0], arrived_ref.shape[1]
    running = arrived_ref[0].astype(wide)
    for plane in range(1, planes):
        running += arrived_ref[plane].astype(wide)
    total_ref[...] = running
    sections = out_ref.shape[0] // 2
    lane_tiles = sections // 2
    proj_tiles = rows // TILE - 4 * lane_tiles - 2
    left = lax.broadcasted_iota(jnp.int32, (TILE, LANES), 1) < LANES // 2
    for half in range(2):
        for lane in range(lane_tiles):
            at = (half * lane_tiles + lane) * TILE
            six = total_ref[at : at + TILE]
            at += 2 * lane_tiles * TILE
            seven = total_ref[at : at + TILE]
            place = half * sections + 2 * lane
            out_ref[place, :TILE] = jnp.where(
                left, six, pltpu.roll(seven, LANES // 2, 1)
            ).astype(narrow)
            out_ref[place + 1, :TILE] = jnp.where(
                left, pltpu.roll(six, LANES // 2, 1), seven
            ).astype(narrow)
    base = 4 * lane_tiles * TILE
    proj = jnp.concatenate(
        [total_ref[base + lane * TILE : base + (lane + 1) * TILE] for lane in range(proj_tiles)],
        axis=1,
    )
    width = proj.shape[1]
    part = width // sections
    for section in range(sections):
        shift = (width - section * part) % width
        moved = pltpu.roll(proj, shift, 1) if shift else proj
        for half in range(2):
            rows_of = slice(half * (TILE // 2), (half + 1) * (TILE // 2))
            out_ref[half * sections + section, TILE : 2 * TILE] = jnp.concatenate(
                [moved[rows_of, :LANES], moved[rows_of, LANES : 2 * LANES]], axis=0
            ).astype(narrow)
    sums = total_ref[rows - 2 * TILE : rows - TILE // 2].astype(narrow)
    out_ref[:, 2 * TILE :] = jnp.broadcast_to(sums[None], (2 * sections,) + sums.shape)


def line_kernel(arrived_ref, six_ref, seven_ref, proj_ref, gains_ref, biases_ref):
    running = arrived_ref[0].astype(wide)
    for source in range(1, arrived_ref.shape[0]):
        running += arrived_ref[source].astype(wide)
    half = LANES // 2
    six_ref[...] = running[:TILE, :half]
    seven_ref[...] = running[:TILE, half:]
    rows = TILE // 2
    proj = jnp.concatenate(
        [running[TILE : TILE + rows], running[TILE + rows : 2 * TILE]], axis=1
    )
    proj_ref[...] = proj[:, : proj_ref.shape[1]]
    sums = jnp.concatenate(
        [running[2 * TILE + k * 6 : 2 * TILE + (k + 1) * 6] for k in range(4)], axis=1
    )
    gains_ref[...] = sums[:3]
    biases_ref[...] = sums[3:6]


def on_device(layer_five, conv_six, conv_seven, gains, biases, proj_weight, feature_grad):
    utt_local, positions, channels = layer_five.shape
    width = feature_grad.shape[2]
    part_width = proj_weight.shape[1]
    sections = lax.axis_size("s")
    planes = lax.axis_size(("y", "x"))
    frames = utt_local * positions // 4
    shape = jax.ShapeDtypeStruct
    place = jnp.stack(
        [lax.axis_index(("y", "x")), lax.axis_index("zh"), lax.axis_index("c"), lax.axis_index("s")]
    ).astype(jnp.int32)

    tile_rows = 2 * (channels // LANES) * TILE
    grad_tiles = (width // LANES + 1) // 2
    convs = on_core(conv_kernel, shape((tile_rows, LANES), narrow), [], [conv_six, conv_seven])
    row_tiles = part_width // TILE
    out_block = (sections, (grad_tiles + 2) * TILE, LANES)
    outgoing = pl.pallas_call(
        pick_kernel,
        out_shape=shape(out_block, narrow),
        grid_spec=pltpu.PrefetchScalarGridSpec(
            num_scalar_prefetch=1,
            grid=(1,),
            in_specs=[
                pl.BlockSpec(
                    (TILE, 2 * LANES), lambda i, at: (jnp.minimum(at[0], row_tiles - 1), at[2])
                ),
                pl.BlockSpec(feature_grad.shape, lambda i, at: (0, 0, 0)),
            ],
            out_specs=pl.BlockSpec(out_block, lambda i, at: (0, 0, 0)),
        ),
        compiler_params=pltpu.CompilerParams(vmem_limit_bytes=8 * 1024 * 1024),
    )(place, proj_weight.T, feature_grad)
    line = 2 * sections
    opposite = [
        (z, (1 - z // sections) * sections + (z % sections + sections // 2) % sections)
        for z in range(line)
    ]
    other_convs = lax.ppermute(convs, ("zh", "s"), opposite)
    arrived = exchange(outgoing, "s")
    bundle = on_core(
        bundle_kernel,
        shape((planes, 2 * tile_rows + sections * 2 * TILE, LANES), narrow),
        [place],
        [convs, other_convs, arrived],
    )
    gathered = exchange(bundle, ("y", "x"))
    sibling = swap(gathered.reshape(-1, LANES), "c")

    tiles_shape = (planes, bundle.shape[1] // TILE, TILE, LANES)
    send_rows = (4 * (channels // LANES) + width // LANES + 2) * TILE
    taps, cotangents, part = on_core(
        early_kernel,
        [
            shape((4 * frames, channels), narrow),
            shape((frames, width), narrow),
            shape((frames, 2 * LANES), wide),
        ],
        [],
        [layer_five.reshape(4 * frames, channels), gathered.reshape(tiles_shape), arrived],
        scratch=[pltpu.VMEM((width, 2 * LANES), narrow), pltpu.VMEM((frames, width), wide)],
    )
    six_full, dhid_six, kept, given = on_core(
        layer_kernel,
        [
            shape((2 * channels, channels), narrow),
            shape((2 * frames, channels), narrow),
            shape((planes, send_rows, LANES), narrow),
            shape((planes, send_rows, LANES), narrow),
        ],
        [place],
        [
            taps,
            gathered.reshape(tiles_shape),
            sibling.reshape(tiles_shape),
            cotangents,
            part,
            gains,
            biases,
        ],
        scratch=[
            pltpu.VMEM((2 * channels, channels), narrow),
            pltpu.VMEM((width, 2 * LANES), narrow),
            pltpu.VMEM((2 * channels, channels), wide),
            pltpu.VMEM((2 * channels, channels), wide),
            pltpu.VMEM((channels, width), wide),
        ],
        megabytes=36,
    )
    back = on_core(
        input_kernel, shape((4 * frames, channels), narrow), [], [dhid_six, six_full]
    )
    received = swap(given.reshape(-1, LANES), "c").reshape(given.shape)
    chip = (kept.astype(wide) + received.astype(wide)).astype(narrow)
    plane_in = exchange(chip, ("y", "x"))
    line_out = on_core(
        plane_kernel,
        shape((2 * sections, 3 * TILE + TILE // 2, LANES), narrow),
        [],
        [plane_in],
        scratch=[pltpu.VMEM((send_rows, LANES), wide)],
    )
    line_in = exchange(line_out, ("zh", "s"))
    out_six, out_seven, out_proj, out_gains, out_biases = on_core(
        line_kernel,
        [
            shape((TILE, channels // sections), wide),
            shape((TILE, channels // sections), wide),
            shape((TILE // 2, part_width), wide),
            shape((3, channels), wide),
            shape((3, channels), wide),
        ],
        [],
        [line_in],
    )
    return (
        back.reshape(utt_local, positions, channels),
        out_six,
        out_seven,
        out_proj,
        out_gains,
        out_biases,
    )


def solution(mesh):
    fine = Mesh(mesh.devices.reshape(4, 4, 2, 2, 8), ("y", "x", "zh", "c", "s"))
    tm = ("y", "x", "zh", "c")
    return jax.shard_map(
        on_device,
        mesh=fine,
        in_specs=(
            P("s", tm, None),
            P(tm, None),
            P(tm, None),
            P(),
            P(),
            P(None, "s"),
            P(None, tm + ("s",), None),
        ),
        out_specs=(
            P("s", tm, None),
            P(tm, "s"),
            P(tm, "s"),
            P(tm, "s"),
            P(),
            P(),
        ),
        check_vma=False,
    )
```

```python
import functools

import jax
import jax.numpy as jnp
from jax import lax
from jax.experimental import pallas as pl
from jax.experimental.pallas import tpu as pltpu
from jax.sharding import Mesh, PartitionSpec as P

norm_epsilon = 1e-05
half_root = 0.7071067811865476
inv_root_tau = 0.3989422804014327
narrow = jnp.bfloat16
wide = jnp.float32
LANES = 128
TILE = 16


def gelu_parts(preact):
    normal_cdf = 0.5 * (1.0 + lax.erf(preact * half_root))
    density = jnp.exp(-0.5 * preact * preact) * inv_root_tau
    return (preact * normal_cdf, normal_cdf + preact * density)


def norm_forward(hidden, gain_row, bias_row):
    average = jnp.mean(hidden, axis=-1, keepdims=True)
    centred = hidden - average
    inv_scale = lax.rsqrt(jnp.mean(centred * centred, axis=-1, keepdims=True) + norm_epsilon)
    normal_part = centred * inv_scale
    return (normal_part * gain_row + bias_row, normal_part, inv_scale)


def norm_backward(incoming, normal_part, inv_scale, gain_row):
    scaled = incoming * gain_row
    first_mean = jnp.mean(scaled, axis=-1, keepdims=True)
    second_mean = jnp.mean(scaled * normal_part, axis=-1, keepdims=True)
    return inv_scale * (scaled - first_mean - normal_part * second_mean)


def matmul(left, right, over=(1, 0)):
    return lax.dot_general(
        left, right, (((over[0],), (over[1],)), ((), ())), preferred_element_type=wide
    )


def one_hot(shape, column_of_row):
    rows = lax.broadcasted_iota(jnp.int32, shape, 0)
    columns = lax.broadcasted_iota(jnp.int32, shape, 1)
    return jnp.where(columns == column_of_row(rows), 1.0, 0.0).astype(narrow)


def exchange(value, axes):
    return lax.all_to_all(value, axes, 0, 0, tiled=True)


def swap(value, axis):
    return lax.ppermute(value, axis, [(0, 1), (1, 0)])


def on_core(kernel, out_shape, scalars, arrays, scratch=(), megabytes=8):
    multiple = isinstance(out_shape, (list, tuple))
    vmem = pl.BlockSpec(memory_space=pltpu.VMEM)
    return pl.pallas_call(
        kernel,
        out_shape=out_shape,
        in_specs=[pl.BlockSpec(memory_space=pltpu.SMEM)] * len(scalars) + [vmem] * len(arrays),
        out_specs=[vmem] * len(out_shape) if multiple else vmem,
        scratch_shapes=list(scratch),
        compiler_params=pltpu.CompilerParams(vmem_limit_bytes=megabytes * 1024 * 1024),
    )(*scalars, *arrays)


def conv_kernel(six_ref, seven_ref, conv_ref):
    lane_tiles = six_ref.shape[1] // LANES
    for index, source in enumerate((six_ref, seven_ref)):
        for lane in range(lane_tiles):
            at = (index * lane_tiles + lane) * TILE
            conv_ref[at : at + TILE] = source[:, lane * LANES : (lane + 1) * LANES]


def pick_kernel(place_ref, proj_ref, grad_ref, out_ref):
    sections = out_ref.shape[0]
    utterances = grad_ref.shape[0] // sections
    width = grad_ref.shape[2]
    for section in range(sections):
        for k in range(2):
            out_ref[section, k * TILE : (k + 1) * TILE] = proj_ref[:, k * LANES : (k + 1) * LANES]
        part = jnp.concatenate(
            [grad_ref[section * utterances + k].astype(wide) for k in range(utterances)], axis=0
        )
        for lane in range(0, width, 2 * LANES):
            pieces = [
                part[:, at : at + LANES] for at in range(lane, min(width, lane + 2 * LANES), LANES)
            ]
            start = 2 * TILE + lane // LANES * (TILE // 2)
            out_ref[section, start : start + len(pieces) * (TILE // 2)] = jnp.concatenate(
                pieces, axis=0
            ).astype(narrow)


def bundle_kernel(place_ref, own_ref, other_ref, arrived_ref, out_ref):
    half = place_ref[1]
    rows = own_ref.shape[0]
    for plane in range(out_ref.shape[0]):
        out_ref[plane, pl.ds(pl.multiple_of(half * rows, TILE), rows)] = own_ref[...]
        out_ref[plane, pl.ds(pl.multiple_of((1 - half) * rows, TILE), rows)] = other_ref[...]
        for section in range(arrived_ref.shape[0]):
            at = 2 * rows + section * 2 * TILE
            out_ref[plane, at : at + 2 * TILE] = arrived_ref[section, : 2 * TILE]


def position_order(frames):
    def source_row(rows):
        run = rows // frames
        return 4 * (rows % frames) + (run % 2) * 2 + run // 2

    return one_hot((4 * frames, 4 * frames), source_row)


def place_proj(source_ref, proj_ref, row_tiles, section_rows):
    sections = proj_ref.shape[0] // section_rows
    first = source_ref.shape[1] - 2 * sections

    def step(plane, carry):
        for section in range(sections):
            rows = pl.ds(pl.multiple_of(section * section_rows + plane * TILE, TILE), TILE)
            for k in range(2):
                proj_ref[rows, k * LANES : (k + 1) * LANES] = source_ref[
                    plane, first + section * 2 + k
                ]
        return carry

    lax.fori_loop(0, row_tiles, step, 0)


def early_kernel(input_ref, own_ref, grad_ref, shared_ref, part_ref, proj_ref, rows_ref):
    frames, width = rows_ref.shape
    sections = grad_ref.shape[0]
    channels = input_ref.shape[1]
    shared_ref[:, :channels] = matmul(position_order(frames), input_ref[...]).astype(narrow)

    run = frames // (2 * sections)

    def arrived_row(rows):
        utterance = rows // (sections * run)
        rest = rows % (sections * run)
        return (rest // run) * (2 * run) + utterance * run + rest % run

    eight = frames // sections
    for section in range(sections):
        for lane in range(width // LANES):
            start = 2 * TILE + lane * eight
            if lane % 2 == 0:
                count = min(2, width // LANES - lane)
                stacked = grad_ref[section, start : start + count * eight].astype(wide)
            rows_ref[
                section * eight : (section + 1) * eight, lane * LANES : (lane + 1) * LANES
            ] = stacked[(lane % 2) * eight : (lane % 2 + 1) * eight]
    grad_rows = matmul(
        one_hot((frames, frames), arrived_row), rows_ref[...].astype(narrow)
    ).astype(narrow)
    for k in range(4):
        lanes = min(channels, width - k * channels)
        shared_ref[k * frames : (k + 1) * frames, channels : channels + lanes] = grad_rows[
            :, k * channels : k * channels + lanes
        ]
    shared_ref[3 * frames :, channels + lanes :] = jnp.zeros((frames, channels - lanes), narrow)
    place_proj(own_ref, proj_ref, width // sections // TILE, width // sections)
    part_ref[...] = matmul(grad_rows, proj_ref[...])


def cotangents_of(shared_ref, width):
    frames, channels = shared_ref.shape[0] // 4, shared_ref.shape[1] // 2
    rows = jnp.concatenate(
        [shared_ref[k * frames : (k + 1) * frames, channels:] for k in range(4)], axis=1
    )
    return rows[:, :width]


def layer_kernel(
    width,
    place_ref,
    shared_ref,
    own_ref,
    other_ref,
    part_ref,
    gains_ref,
    biases_ref,
    six_ref,
    late_ref,
    seven_ref,
    proj_ref,
):
    core = place_ref[2]
    frames, channels = part_ref.shape[0], shared_ref.shape[1] // 2
    lane_tiles = channels // LANES
    planes = own_ref.shape[0]
    sections = (own_ref.shape[1] - 4 * lane_tiles) // 2
    section_rows = width // sections

    def place_tiles(plane, carry):
        for half in range(2):
            for source, index in ((own_ref, core), (other_ref, 1 - core)):
                rows = pl.ds(
                    pl.multiple_of(((plane * 2 + half) * 2 + index) * TILE, TILE), TILE
                )
                for lane in range(lane_tiles):
                    lanes = slice(lane * LANES, (lane + 1) * LANES)
                    tile = half * 2 * lane_tiles + lane
                    six_ref[rows, lanes] = source[plane, tile]
                    seven_ref[rows, lanes] = source[plane, tile + lane_tiles]
        return carry

    lax.fori_loop(0, planes, place_tiles, 0)

    place_proj(other_ref, proj_ref, section_rows // TILE, section_rows)
    tap_zero, tap_one = shared_ref[: 2 * frames, :channels], shared_ref[2 * frames :, :channels]
    hid_six = matmul(tap_zero, six_ref[:channels]) + matmul(tap_one, six_ref[channels:])
    pre_six, part_six, scale_six = norm_forward(hid_six, gains_ref[0:1], biases_ref[0:1])
    act_six_f, deriv_six = gelu_parts(pre_six)
    act_six = act_six_f.astype(narrow)
    act_zero, act_one = act_six[:frames], act_six[frames:]
    hid_seven = matmul(act_zero, seven_ref[:channels]) + matmul(act_one, seven_ref[channels:])
    pre_seven, part_seven, scale_seven = norm_forward(
        hid_seven, gains_ref[1:2], biases_ref[1:2]
    )
    act_seven_f, deriv_seven = gelu_parts(pre_seven)
    pre_feat, part_feat, scale_feat = norm_forward(
        act_seven_f.astype(narrow).astype(wide), gains_ref[2:3], biases_ref[2:3]
    )
    normed = pre_feat.astype(narrow)

    grad_rows = cotangents_of(shared_ref, width)
    own_half, other_half = part_ref[...], matmul(grad_rows, proj_ref[...])
    first = core == 0
    grad_normed = jnp.concatenate(
        [jnp.where(first, own_half, other_half), jnp.where(first, other_half, own_half)], axis=1
    )
    dact_seven = norm_backward(grad_normed, part_feat, scale_feat, gains_ref[2:3])
    dpre_seven = dact_seven * deriv_seven
    dhid_seven = norm_backward(dpre_seven, part_seven, scale_seven, gains_ref[1:2]).astype(narrow)
    dact_six = jnp.concatenate(
        [
            matmul(dhid_seven, seven_ref[:channels], (1, 1)),
            matmul(dhid_seven, seven_ref[channels:], (1, 1)),
        ],
        axis=0,
    )
    dpre_six = dact_six * deriv_six
    dhid_six = norm_backward(dpre_six, part_six, scale_six, gains_ref[0:1]).astype(narrow)
    def total(value):
        return jnp.sum(value, axis=0, keepdims=True)

    sums = jnp.concatenate(
        [
            total(dpre_six * part_six),
            total(dpre_seven * part_seven),
            total(grad_normed * part_feat),
            total(dpre_six),
            total(dpre_seven),
            total(grad_normed),
        ],
        axis=0,
    )
    late_ref[: 2 * frames] = dhid_six
    late_ref[2 * frames : 4 * frames] = act_six
    late_ref[4 * frames : 5 * frames] = dhid_seven
    late_ref[5 * frames : 6 * frames] = normed
    late_ref[6 * frames :] = jnp.concatenate(
        [sums, jnp.zeros((TILE - sums.shape[0], channels), wide)], axis=0
    ).astype(narrow)


def terms_kernel(
    width,
    place_ref,
    shared_ref,
    shared_other_ref,
    late_ref,
    late_other_ref,
    send_ref,
    term_six_ref,
    term_seven_ref,
    term_proj_ref,
):
    core = place_ref[2]
    frames, channels = shared_ref.shape[0] // 4, late_ref.shape[1]
    lane_tiles = channels // LANES
    planes = send_ref.shape[0]

    def both(start, stop, left=shared_ref, right=shared_other_ref):
        rows = slice(start * frames, stop * frames)
        return jnp.concatenate([left[rows, :channels], right[rows, :channels]], axis=0)

    def late(start, stop):
        return both(start, stop, late_ref, late_other_ref)

    dhid_six, dhid_seven, normed = late(0, 2), late(4, 5), late(5, 6)
    term_six_ref[:channels] = matmul(both(0, 2), dhid_six, (0, 0))
    term_six_ref[channels:] = matmul(both(2, 4), dhid_six, (0, 0))
    term_seven_ref[:channels] = matmul(late(2, 3), dhid_seven, (0, 0))
    term_seven_ref[channels:] = matmul(late(3, 4), dhid_seven, (0, 0))
    grad_rows = jnp.concatenate(
        [cotangents_of(shared_ref, width), cotangents_of(shared_other_ref, width)], axis=0
    )
    term_proj_ref[...] = matmul(normed, grad_rows, (0, 0))
    half_rows = TILE // 2

    def pack(plane, carry):
        proj_rows = []
        for half in range(2):
            group = (plane * 2 + half) * 2 + core
            rows = pl.ds(pl.multiple_of(group * TILE, TILE), TILE)
            for lane in range(lane_tiles):
                lanes = slice(lane * LANES, (lane + 1) * LANES)
                at = (half * lane_tiles + lane) * TILE
                send_ref[plane, at : at + TILE] = term_six_ref[rows, lanes].astype(narrow)
                at += 2 * lane_tiles * TILE
                send_ref[plane, at : at + TILE] = term_seven_ref[rows, lanes].astype(narrow)
            proj_rows.append(
                term_proj_ref[pl.ds(pl.multiple_of(group * half_rows, half_rows), half_rows)]
            )
        proj_block = jnp.concatenate(proj_rows, axis=0).astype(narrow)
        for lane in range(width // LANES):
            at = (4 * lane_tiles + lane) * TILE
            send_ref[plane, at : at + TILE] = proj_block[:, lane * LANES : (lane + 1) * LANES]
        return carry

    lax.fori_loop(0, planes, pack, 0)
    sums = (late_ref[6 * frames :].astype(wide) + late_other_ref[6 * frames :].astype(wide))[:6]
    sums = jnp.concatenate(
        [sums[:, lane * LANES : (lane + 1) * LANES] for lane in range(lane_tiles)], axis=0
    ).astype(narrow)
    at = (4 * lane_tiles + width // LANES) * TILE
    send_ref[:, at:] = jnp.broadcast_to(sums[None], (planes,) + sums.shape)


def input_kernel(late_ref, six_ref, back_ref):
    channels = back_ref.shape[1]
    dhid_six = late_ref[: back_ref.shape[0] // 2]
    back = jnp.concatenate(
        [
            matmul(dhid_six, six_ref[:channels], (1, 1)).astype(narrow),
            matmul(dhid_six, six_ref[channels:], (1, 1)).astype(narrow),
        ],
        axis=0,
    )
    back_ref[...] = matmul(position_order(back_ref.shape[0] // 4), back, (0, 0)).astype(narrow)


def plane_kernel(arrived_ref, out_ref, total_ref):
    planes, rows = arrived_ref.shape[0], arrived_ref.shape[1]
    running = arrived_ref[0].astype(wide)
    for plane in range(1, planes):
        running += arrived_ref[plane].astype(wide)
    total_ref[...] = running
    sections = out_ref.shape[0] // 2
    lane_tiles = sections // 2
    sum_rows = 6 * lane_tiles
    proj_tiles = (rows - sum_rows) // TILE - 4 * lane_tiles
    left = lax.broadcasted_iota(jnp.int32, (TILE, LANES), 1) < LANES // 2
    for half in range(2):
        for lane in range(lane_tiles):
            at = (half * lane_tiles + lane) * TILE
            six = total_ref[at : at + TILE]
            at += 2 * lane_tiles * TILE
            seven = total_ref[at : at + TILE]
            place = half * sections + 2 * lane
            out_ref[place, :TILE] = jnp.where(
                left, six, pltpu.roll(seven, LANES // 2, 1)
            ).astype(narrow)
            out_ref[place + 1, :TILE] = jnp.where(
                left, pltpu.roll(six, LANES // 2, 1), seven
            ).astype(narrow)
    base = 4 * lane_tiles * TILE
    proj = jnp.concatenate(
        [total_ref[base + lane * TILE : base + (lane + 1) * TILE] for lane in range(proj_tiles)],
        axis=1,
    )
    width = proj.shape[1]
    part = width // sections
    for section in range(sections):
        shift = (width - section * part) % width
        moved = pltpu.roll(proj, shift, 1) if shift else proj
        for half in range(2):
            rows_of = slice(half * (TILE // 2), (half + 1) * (TILE // 2))
            out_ref[half * sections + section, TILE : 2 * TILE] = jnp.concatenate(
                [moved[rows_of, :LANES], moved[rows_of, LANES : 2 * LANES]], axis=0
            ).astype(narrow)
    sums = total_ref[rows - sum_rows :].astype(narrow)
    out_ref[:, 2 * TILE :] = jnp.broadcast_to(sums[None], (2 * sections,) + sums.shape)


def line_kernel(arrived_ref, six_ref, seven_ref, proj_ref, gains_ref, biases_ref):
    running = arrived_ref[0].astype(wide)
    for source in range(1, arrived_ref.shape[0]):
        running += arrived_ref[source].astype(wide)
    half = LANES // 2
    six_ref[...] = running[:TILE, :half]
    seven_ref[...] = running[:TILE, half:]
    rows = TILE // 2
    proj = jnp.concatenate(
        [running[TILE : TILE + rows], running[TILE + rows : 2 * TILE]], axis=1
    )
    proj_ref[...] = proj[:, : proj_ref.shape[1]]
    sums = jnp.concatenate(
        [running[2 * TILE + k * 6 : 2 * TILE + (k + 1) * 6] for k in range(4)], axis=1
    )
    gains_ref[...] = sums[:3]
    biases_ref[...] = sums[3:6]


def on_device(layer_five, conv_six, conv_seven, gains, biases, proj_weight, feature_grad):
    utt_local, positions, channels = layer_five.shape
    width = feature_grad.shape[2]
    part_width = proj_weight.shape[1]
    sections = lax.axis_size("s")
    planes = lax.axis_size(("y", "x"))
    frames = utt_local * positions // 4
    shape = jax.ShapeDtypeStruct
    place = jnp.stack(
        [lax.axis_index(("y", "x")), lax.axis_index("zh"), lax.axis_index("c"), lax.axis_index("s")]
    ).astype(jnp.int32)

    lane_tiles = channels // LANES
    tile_rows = 2 * lane_tiles * TILE
    convs = on_core(conv_kernel, shape((tile_rows, LANES), narrow), [], [conv_six, conv_seven])
    row_tiles = part_width // TILE
    out_block = (sections, 2 * TILE + width // LANES * (TILE // 2), LANES)
    outgoing = pl.pallas_call(
        pick_kernel,
        out_shape=shape(out_block, narrow),
        grid_spec=pltpu.PrefetchScalarGridSpec(
            num_scalar_prefetch=1,
            grid=(1,),
            in_specs=[
                pl.BlockSpec(
                    (TILE, 2 * LANES), lambda i, at: (jnp.minimum(at[0], row_tiles - 1), at[2])
                ),
                pl.BlockSpec(feature_grad.shape, lambda i, at: (0, 0, 0)),
            ],
            out_specs=pl.BlockSpec(out_block, lambda i, at: (0, 0, 0)),
        ),
        compiler_params=pltpu.CompilerParams(vmem_limit_bytes=8 * 1024 * 1024),
    )(place, proj_weight.T, feature_grad)
    line = 2 * sections
    opposite = [
        (z, (1 - z // sections) * sections + (z % sections + sections // 2) % sections)
        for z in range(line)
    ]
    other_convs = lax.ppermute(convs, ("zh", "s"), opposite)
    arrived = exchange(outgoing, "s")
    bundle = on_core(
        bundle_kernel,
        shape((planes, 2 * tile_rows + sections * 2 * TILE, LANES), narrow),
        [place],
        [convs, other_convs, arrived],
    )
    gathered = exchange(bundle, ("y", "x"))
    sibling = swap(gathered.reshape(-1, LANES), "c")

    tiles_shape = (planes, bundle.shape[1] // TILE, TILE, LANES)
    shared, part = on_core(
        early_kernel,
        [shape((4 * frames, 2 * channels), narrow), shape((frames, 2 * LANES), wide)],
        [],
        [layer_five.reshape(4 * frames, channels), gathered.reshape(tiles_shape), arrived],
        scratch=[pltpu.VMEM((width, 2 * LANES), narrow), pltpu.VMEM((frames, width), wide)],
    )
    shared_other = swap(shared, "c")
    six_full, late = on_core(
        functools.partial(layer_kernel, width),
        [
            shape((2 * channels, channels), narrow),
            shape((6 * frames + TILE, channels), narrow),
        ],
        [place],
        [
            shared,
            gathered.reshape(tiles_shape),
            sibling.reshape(tiles_shape),
            part,
            gains,
            biases,
        ],
        scratch=[
            pltpu.VMEM((2 * channels, channels), narrow),
            pltpu.VMEM((width, 2 * LANES), narrow),
        ],
        megabytes=16,
    )
    late_other = swap(late, "c")
    back = on_core(input_kernel, shape((4 * frames, channels), narrow), [], [late, six_full])
    send_rows = (4 * lane_tiles + width // LANES) * TILE + 6 * lane_tiles
    chip = on_core(
        functools.partial(terms_kernel, width),
        shape((planes, send_rows, LANES), narrow),
        [place],
        [shared, shared_other, late, late_other],
        scratch=[
            pltpu.VMEM((2 * channels, channels), wide),
            pltpu.VMEM((2 * channels, channels), wide),
            pltpu.VMEM((channels, width), wide),
        ],
        megabytes=24,
    )
    plane_in = exchange(chip, ("y", "x"))
    line_out = on_core(
        plane_kernel,
        shape((2 * sections, 3 * TILE + TILE // 2, LANES), narrow),
        [],
        [plane_in],
        scratch=[pltpu.VMEM((send_rows, LANES), wide)],
    )
    line_in = exchange(line_out, ("zh", "s"))
    out_six, out_seven, out_proj, out_gains, out_biases = on_core(
        line_kernel,
        [
            shape((TILE, channels // sections), wide),
            shape((TILE, channels // sections), wide),
            shape((TILE // 2, part_width), wide),
            shape((3, channels), wide),
            shape((3, channels), wide),
        ],
        [],
        [line_in],
    )
    return (
        back.reshape(utt_local, positions, channels),
        out_six,
        out_seven,
        out_proj,
        out_gains,
        out_biases,
    )


def solution(mesh):
    fine = Mesh(mesh.devices.reshape(4, 4, 2, 2, 8), ("y", "x", "zh", "c", "s"))
    tm = ("y", "x", "zh", "c")
    return jax.shard_map(
        on_device,
        mesh=fine,
        in_specs=(
            P("s", tm, None),
            P(tm, None),
            P(tm, None),
            P(),
            P(),
            P(None, "s"),
            P(None, tm + ("s",), None),
        ),
        out_specs=(
            P("s", tm, None),
            P(tm, "s"),
            P(tm, "s"),
            P(tm, "s"),
            P(),
            P(),
        ),
        check_vma=False,
    )
```

```python
import functools

import jax
import jax.numpy as jnp
from jax import lax
from jax.experimental import pallas as pl
from jax.experimental.pallas import tpu as pltpu
from jax.sharding import Mesh, PartitionSpec as P

norm_epsilon = 1e-05
half_root = 0.7071067811865476
inv_root_tau = 0.3989422804014327
narrow = jnp.bfloat16
wide = jnp.float32
LANES = 128
TILE = 16


def gelu_parts(preact):
    normal_cdf = 0.5 * (1.0 + lax.erf(preact * half_root))
    density = jnp.exp(-0.5 * preact * preact) * inv_root_tau
    return (preact * normal_cdf, normal_cdf + preact * density)


def norm_forward(hidden, gain_row, bias_row):
    average = jnp.mean(hidden, axis=-1, keepdims=True)
    centred = hidden - average
    inv_scale = lax.rsqrt(jnp.mean(centred * centred, axis=-1, keepdims=True) + norm_epsilon)
    normal_part = centred * inv_scale
    return (normal_part * gain_row + bias_row, normal_part, inv_scale)


def norm_backward(incoming, normal_part, inv_scale, gain_row):
    scaled = incoming * gain_row
    first_mean = jnp.mean(scaled, axis=-1, keepdims=True)
    second_mean = jnp.mean(scaled * normal_part, axis=-1, keepdims=True)
    return inv_scale * (scaled - first_mean - normal_part * second_mean)


def matmul(left, right, over=(1, 0)):
    return lax.dot_general(
        left, right, (((over[0],), (over[1],)), ((), ())), preferred_element_type=wide
    )


def one_hot(shape, column_of_row):
    rows = lax.broadcasted_iota(jnp.int32, shape, 0)
    columns = lax.broadcasted_iota(jnp.int32, shape, 1)
    return jnp.where(columns == column_of_row(rows), 1.0, 0.0).astype(narrow)


def exchange(value, axes):
    return lax.all_to_all(value, axes, 0, 0, tiled=True)


def swap(value, axis):
    return lax.ppermute(value, axis, [(0, 1), (1, 0)])


def on_core(kernel, out_shape, scalars, arrays, scratch=(), megabytes=8):
    multiple = isinstance(out_shape, (list, tuple))
    vmem = pl.BlockSpec(memory_space=pltpu.VMEM)
    return pl.pallas_call(
        kernel,
        out_shape=out_shape,
        in_specs=[pl.BlockSpec(memory_space=pltpu.SMEM)] * len(scalars) + [vmem] * len(arrays),
        out_specs=[vmem] * len(out_shape) if multiple else vmem,
        scratch_shapes=list(scratch),
        compiler_params=pltpu.CompilerParams(vmem_limit_bytes=megabytes * 1024 * 1024),
    )(*scalars, *arrays)


def conv_kernel(six_ref, seven_ref, conv_ref):
    lane_tiles = six_ref.shape[1] // LANES
    for index, source in enumerate((six_ref, seven_ref)):
        for lane in range(lane_tiles):
            at = (index * lane_tiles + lane) * TILE
            conv_ref[at : at + TILE] = source[:, lane * LANES : (lane + 1) * LANES]


def pick_kernel(place_ref, proj_hbm, grad_hbm, out_ref, proj_ref, grad_ref, done):
    plane, core = place_ref[0], place_ref[2]
    row = pl.multiple_of(jnp.minimum(plane, proj_hbm.shape[0] // TILE - 1) * TILE, TILE)
    lane = pl.multiple_of(core * 2 * LANES, LANES)
    grad_copy = pltpu.make_async_copy(grad_hbm, grad_ref, done.at[0])
    proj_copy = pltpu.make_async_copy(
        proj_hbm.at[pl.ds(row, TILE), pl.ds(lane, 2 * LANES)], proj_ref, done.at[1]
    )
    grad_copy.start()
    proj_copy.start()
    grad_copy.wait()
    proj_copy.wait()
    sections = out_ref.shape[0]
    utterances = grad_ref.shape[0] // sections
    width = grad_ref.shape[2]
    for section in range(sections):
        for k in range(2):
            out_ref[section, k * TILE : (k + 1) * TILE] = proj_ref[:, k * LANES : (k + 1) * LANES]
        part = jnp.concatenate(
            [grad_ref[section * utterances + k].astype(wide) for k in range(utterances)], axis=0
        )
        for lane in range(0, width, 2 * LANES):
            pieces = [
                part[:, at : at + LANES] for at in range(lane, min(width, lane + 2 * LANES), LANES)
            ]
            start = 2 * TILE + lane // LANES * (TILE // 2)
            out_ref[section, start : start + len(pieces) * (TILE // 2)] = jnp.concatenate(
                pieces, axis=0
            ).astype(narrow)


def bundle_kernel(place_ref, own_ref, other_ref, arrived_ref, out_ref):
    half = place_ref[1]
    rows = own_ref.shape[0]
    for plane in range(out_ref.shape[0]):
        out_ref[plane, pl.ds(pl.multiple_of(half * rows, TILE), rows)] = own_ref[...]
        out_ref[plane, pl.ds(pl.multiple_of((1 - half) * rows, TILE), rows)] = other_ref[...]
        for section in range(arrived_ref.shape[0]):
            at = 2 * rows + section * 2 * TILE
            out_ref[plane, at : at + 2 * TILE] = arrived_ref[section, : 2 * TILE]


def position_order(frames):
    def source_row(rows):
        run = rows // frames
        return 4 * (rows % frames) + (run % 2) * 2 + run // 2

    return one_hot((4 * frames, 4 * frames), source_row)


def place_proj(source_ref, proj_ref, row_tiles, section_rows):
    sections = proj_ref.shape[0] // section_rows
    first = source_ref.shape[1] - 2 * sections

    def step(plane, carry):
        for section in range(sections):
            rows = pl.ds(pl.multiple_of(section * section_rows + plane * TILE, TILE), TILE)
            for k in range(2):
                proj_ref[rows, k * LANES : (k + 1) * LANES] = source_ref[
                    plane, first + section * 2 + k
                ]
        return carry

    lax.fori_loop(0, row_tiles, step, 0)


def early_kernel(input_ref, own_ref, grad_ref, shared_ref, part_ref, proj_ref, rows_ref):
    frames, width = rows_ref.shape
    sections = grad_ref.shape[0]
    channels = input_ref.shape[1]
    shared_ref[:, :channels] = matmul(position_order(frames), input_ref[...]).astype(narrow)

    run = frames // (2 * sections)

    def arrived_row(rows):
        utterance = rows // (sections * run)
        rest = rows % (sections * run)
        return (rest // run) * (2 * run) + utterance * run + rest % run

    eight = frames // sections
    for section in range(sections):
        for lane in range(width // LANES):
            start = 2 * TILE + lane * eight
            if lane % 2 == 0:
                count = min(2, width // LANES - lane)
                stacked = grad_ref[section, start : start + count * eight].astype(wide)
            rows_ref[
                section * eight : (section + 1) * eight, lane * LANES : (lane + 1) * LANES
            ] = stacked[(lane % 2) * eight : (lane % 2 + 1) * eight]
    grad_rows = matmul(
        one_hot((frames, frames), arrived_row), rows_ref[...].astype(narrow)
    ).astype(narrow)
    for k in range(4):
        lanes = min(channels, width - k * channels)
        shared_ref[k * frames : (k + 1) * frames, channels : channels + lanes] = grad_rows[
            :, k * channels : k * channels + lanes
        ]
    shared_ref[3 * frames :, channels + lanes :] = jnp.zeros((frames, channels - lanes), narrow)
    place_proj(own_ref, proj_ref, width // sections // TILE, width // sections)
    part_ref[...] = matmul(grad_rows, proj_ref[...])


def cotangents_of(shared_ref, width):
    frames, channels = shared_ref.shape[0] // 4, shared_ref.shape[1] // 2
    rows = jnp.concatenate(
        [shared_ref[k * frames : (k + 1) * frames, channels:] for k in range(4)], axis=1
    )
    return rows[:, :width]


def layer_kernel(
    width,
    place_ref,
    shared_ref,
    own_ref,
    other_ref,
    part_ref,
    gains_ref,
    biases_ref,
    six_ref,
    late_ref,
    seven_ref,
    proj_ref,
):
    core = place_ref[2]
    frames, channels = part_ref.shape[0], shared_ref.shape[1] // 2
    lane_tiles = channels // LANES
    planes = own_ref.shape[0]
    sections = (own_ref.shape[1] - 4 * lane_tiles) // 2
    section_rows = width // sections

    def place_tiles(plane, carry):
        for half in range(2):
            for source, index in ((own_ref, core), (other_ref, 1 - core)):
                rows = pl.ds(
                    pl.multiple_of(((plane * 2 + half) * 2 + index) * TILE, TILE), TILE
                )
                for lane in range(lane_tiles):
                    lanes = slice(lane * LANES, (lane + 1) * LANES)
                    tile = half * 2 * lane_tiles + lane
                    six_ref[rows, lanes] = source[plane, tile]
                    seven_ref[rows, lanes] = source[plane, tile + lane_tiles]
        return carry

    lax.fori_loop(0, planes, place_tiles, 0)

    place_proj(other_ref, proj_ref, section_rows // TILE, section_rows)
    tap_zero, tap_one = shared_ref[: 2 * frames, :channels], shared_ref[2 * frames :, :channels]
    hid_six = matmul(tap_zero, six_ref[:channels]) + matmul(tap_one, six_ref[channels:])
    pre_six, part_six, scale_six = norm_forward(hid_six, gains_ref[0:1], biases_ref[0:1])
    act_six_f, deriv_six = gelu_parts(pre_six)
    act_six = act_six_f.astype(narrow)
    act_zero, act_one = act_six[:frames], act_six[frames:]
    hid_seven = matmul(act_zero, seven_ref[:channels]) + matmul(act_one, seven_ref[channels:])
    pre_seven, part_seven, scale_seven = norm_forward(
        hid_seven, gains_ref[1:2], biases_ref[1:2]
    )
    act_seven_f, deriv_seven = gelu_parts(pre_seven)
    pre_feat, part_feat, scale_feat = norm_forward(
        act_seven_f.astype(narrow).astype(wide), gains_ref[2:3], biases_ref[2:3]
    )
    normed = pre_feat.astype(narrow)

    grad_rows = cotangents_of(shared_ref, width)
    own_half, other_half = part_ref[...], matmul(grad_rows, proj_ref[...])
    first = core == 0
    grad_normed = jnp.concatenate(
        [jnp.where(first, own_half, other_half), jnp.where(first, other_half, own_half)], axis=1
    )
    dact_seven = norm_backward(grad_normed, part_feat, scale_feat, gains_ref[2:3])
    dpre_seven = dact_seven * deriv_seven
    dhid_seven = norm_backward(dpre_seven, part_seven, scale_seven, gains_ref[1:2]).astype(narrow)
    dact_six = jnp.concatenate(
        [
            matmul(dhid_seven, seven_ref[:channels], (1, 1)),
            matmul(dhid_seven, seven_ref[channels:], (1, 1)),
        ],
        axis=0,
    )
    dpre_six = dact_six * deriv_six
    dhid_six = norm_backward(dpre_six, part_six, scale_six, gains_ref[0:1]).astype(narrow)
    def total(value):
        return jnp.sum(value, axis=0, keepdims=True)

    sums = jnp.concatenate(
        [
            total(dpre_six * part_six),
            total(dpre_seven * part_seven),
            total(grad_normed * part_feat),
            total(dpre_six),
            total(dpre_seven),
            total(grad_normed),
        ],
        axis=0,
    )
    late_ref[: 2 * frames] = dhid_six
    late_ref[2 * frames : 4 * frames] = act_six
    late_ref[4 * frames : 5 * frames] = dhid_seven
    late_ref[5 * frames : 6 * frames] = normed
    late_ref[6 * frames :] = jnp.concatenate(
        [sums, jnp.zeros((TILE - sums.shape[0], channels), wide)], axis=0
    ).astype(narrow)


def terms_kernel(
    width,
    place_ref,
    shared_ref,
    shared_other_ref,
    late_ref,
    late_other_ref,
    send_ref,
    term_six_ref,
    term_seven_ref,
    term_proj_ref,
):
    core = place_ref[2]
    frames, channels = shared_ref.shape[0] // 4, late_ref.shape[1]
    lane_tiles = channels // LANES
    planes = send_ref.shape[0]

    def both(start, stop, left=shared_ref, right=shared_other_ref):
        rows = slice(start * frames, stop * frames)
        return jnp.concatenate([left[rows, :channels], right[rows, :channels]], axis=0)

    def late(start, stop):
        return both(start, stop, late_ref, late_other_ref)

    dhid_six, dhid_seven, normed = late(0, 2), late(4, 5), late(5, 6)
    term_six_ref[:channels] = matmul(both(0, 2), dhid_six, (0, 0))
    term_six_ref[channels:] = matmul(both(2, 4), dhid_six, (0, 0))
    term_seven_ref[:channels] = matmul(late(2, 3), dhid_seven, (0, 0))
    term_seven_ref[channels:] = matmul(late(3, 4), dhid_seven, (0, 0))
    grad_rows = jnp.concatenate(
        [cotangents_of(shared_ref, width), cotangents_of(shared_other_ref, width)], axis=0
    )
    term_proj_ref[...] = matmul(normed, grad_rows, (0, 0))
    half_rows = TILE // 2

    def pack(plane, carry):
        proj_rows = []
        for half in range(2):
            group = (plane * 2 + half) * 2 + core
            rows = pl.ds(pl.multiple_of(group * TILE, TILE), TILE)
            for lane in range(lane_tiles):
                lanes = slice(lane * LANES, (lane + 1) * LANES)
                at = (half * lane_tiles + lane) * TILE
                send_ref[plane, at : at + TILE] = term_six_ref[rows, lanes].astype(narrow)
                at += 2 * lane_tiles * TILE
                send_ref[plane, at : at + TILE] = term_seven_ref[rows, lanes].astype(narrow)
            proj_rows.append(
                term_proj_ref[pl.ds(pl.multiple_of(group * half_rows, half_rows), half_rows)]
            )
        proj_block = jnp.concatenate(proj_rows, axis=0).astype(narrow)
        for lane in range(width // LANES):
            at = (4 * lane_tiles + lane) * TILE
            send_ref[plane, at : at + TILE] = proj_block[:, lane * LANES : (lane + 1) * LANES]
        return carry

    lax.fori_loop(0, planes, pack, 0)
    sums = (late_ref[6 * frames :].astype(wide) + late_other_ref[6 * frames :].astype(wide))[:6]
    sums = jnp.concatenate(
        [sums[:, lane * LANES : (lane + 1) * LANES] for lane in range(lane_tiles)], axis=0
    ).astype(narrow)
    at = (4 * lane_tiles + width // LANES) * TILE
    send_ref[:, at:] = jnp.broadcast_to(sums[None], (planes,) + sums.shape)


def input_kernel(late_ref, six_ref, back_ref):
    channels = back_ref.shape[1]
    dhid_six = late_ref[: back_ref.shape[0] // 2]
    back = jnp.concatenate(
        [
            matmul(dhid_six, six_ref[:channels], (1, 1)).astype(narrow),
            matmul(dhid_six, six_ref[channels:], (1, 1)).astype(narrow),
        ],
        axis=0,
    )
    back_ref[...] = matmul(position_order(back_ref.shape[0] // 4), back, (0, 0)).astype(narrow)


def plane_kernel(arrived_ref, out_ref, total_ref):
    planes, rows = arrived_ref.shape[0], arrived_ref.shape[1]
    for start in range(0, rows, TILE):
        at = slice(start, min(start + TILE, rows))
        running = arrived_ref[0, at].astype(wide)
        for plane in range(1, planes):
            running += arrived_ref[plane, at].astype(wide)
        total_ref[at] = running
    sections = out_ref.shape[0] // 2
    lane_tiles = sections // 2
    sum_rows = 6 * lane_tiles
    proj_tiles = (rows - sum_rows) // TILE - 4 * lane_tiles
    left = lax.broadcasted_iota(jnp.int32, (TILE, LANES), 1) < LANES // 2
    for half in range(2):
        for lane in range(lane_tiles):
            at = (half * lane_tiles + lane) * TILE
            six = total_ref[at : at + TILE]
            at += 2 * lane_tiles * TILE
            seven = total_ref[at : at + TILE]
            place = half * sections + 2 * lane
            out_ref[place, :TILE] = jnp.where(
                left, six, pltpu.roll(seven, LANES // 2, 1)
            ).astype(narrow)
            out_ref[place + 1, :TILE] = jnp.where(
                left, pltpu.roll(six, LANES // 2, 1), seven
            ).astype(narrow)
    base = 4 * lane_tiles * TILE
    proj = jnp.concatenate(
        [total_ref[base + lane * TILE : base + (lane + 1) * TILE] for lane in range(proj_tiles)],
        axis=1,
    )
    width = proj.shape[1]
    part = width // sections
    for section in range(sections):
        shift = (width - section * part) % width
        moved = pltpu.roll(proj, shift, 1) if shift else proj
        for half in range(2):
            rows_of = slice(half * (TILE // 2), (half + 1) * (TILE // 2))
            out_ref[half * sections + section, TILE : 2 * TILE] = jnp.concatenate(
                [moved[rows_of, :LANES], moved[rows_of, LANES : 2 * LANES]], axis=0
            ).astype(narrow)
    sums = total_ref[rows - sum_rows :].astype(narrow)
    out_ref[:, 2 * TILE :] = jnp.broadcast_to(sums[None], (2 * sections,) + sums.shape)


def line_kernel(arrived_ref, six_ref, seven_ref, proj_ref, gains_ref, biases_ref):
    running = arrived_ref[0].astype(wide)
    for source in range(1, arrived_ref.shape[0]):
        running += arrived_ref[source].astype(wide)
    half = LANES // 2
    six_ref[...] = running[:TILE, :half]
    seven_ref[...] = running[:TILE, half:]
    rows = TILE // 2
    proj = jnp.concatenate(
        [running[TILE : TILE + rows], running[TILE + rows : 2 * TILE]], axis=1
    )
    proj_ref[...] = proj[:, : proj_ref.shape[1]]
    sums = jnp.concatenate(
        [running[2 * TILE + k * 6 : 2 * TILE + (k + 1) * 6] for k in range(4)], axis=1
    )
    gains_ref[...] = sums[:3]
    biases_ref[...] = sums[3:6]


def on_device(layer_five, conv_six, conv_seven, gains, biases, proj_weight, feature_grad):
    utt_local, positions, channels = layer_five.shape
    width = feature_grad.shape[2]
    part_width = proj_weight.shape[1]
    sections = lax.axis_size("s")
    planes = lax.axis_size(("y", "x"))
    frames = utt_local * positions // 4
    shape = jax.ShapeDtypeStruct
    place = jnp.stack(
        [lax.axis_index(("y", "x")), lax.axis_index("zh"), lax.axis_index("c"), lax.axis_index("s")]
    ).astype(jnp.int32)

    lane_tiles = channels // LANES
    tile_rows = 2 * lane_tiles * TILE
    convs = on_core(conv_kernel, shape((tile_rows, LANES), narrow), [], [conv_six, conv_seven])
    in_hbm = pl.BlockSpec(memory_space=pl.ANY)
    outgoing = pl.pallas_call(
        pick_kernel,
        out_shape=shape((sections, 2 * TILE + width // LANES * (TILE // 2), LANES), narrow),
        in_specs=[pl.BlockSpec(memory_space=pltpu.SMEM), in_hbm, in_hbm],
        out_specs=pl.BlockSpec(memory_space=pltpu.VMEM),
        scratch_shapes=[
            pltpu.VMEM((TILE, 2 * LANES), narrow),
            pltpu.VMEM(feature_grad.shape, narrow),
            pltpu.SemaphoreType.DMA((2,)),
        ],
        compiler_params=pltpu.CompilerParams(vmem_limit_bytes=56 * 1024 * 1024),
    )(place, proj_weight.T, feature_grad)
    line = 2 * sections
    opposite = [
        (z, (1 - z // sections) * sections + (z % sections + sections // 2) % sections)
        for z in range(line)
    ]
    other_convs = lax.ppermute(convs, ("zh", "s"), opposite)
    arrived = exchange(outgoing, "s")
    bundle = on_core(
        bundle_kernel,
        shape((planes, 2 * tile_rows + sections * 2 * TILE, LANES), narrow),
        [place],
        [convs, other_convs, arrived],
    )
    gathered = exchange(bundle, ("y", "x"))
    sibling = swap(gathered.reshape(-1, LANES), "c")

    tiles_shape = (planes, bundle.shape[1] // TILE, TILE, LANES)
    shared, part = on_core(
        early_kernel,
        [shape((4 * frames, 2 * channels), narrow), shape((frames, 2 * LANES), wide)],
        [],
        [layer_five.reshape(4 * frames, channels), gathered.reshape(tiles_shape), arrived],
        scratch=[pltpu.VMEM((width, 2 * LANES), narrow), pltpu.VMEM((frames, width), wide)],
    )
    shared_other = swap(shared, "c")
    six_full, late = on_core(
        functools.partial(layer_kernel, width),
        [
            shape((2 * channels, channels), narrow),
            shape((6 * frames + TILE, channels), narrow),
        ],
        [place],
        [
            shared,
            gathered.reshape(tiles_shape),
            sibling.reshape(tiles_shape),
            part,
            gains,
            biases,
        ],
        scratch=[
            pltpu.VMEM((2 * channels, channels), narrow),
            pltpu.VMEM((width, 2 * LANES), narrow),
        ],
        megabytes=16,
    )
    late_other = swap(late, "c")
    back = on_core(input_kernel, shape((4 * frames, channels), narrow), [], [late, six_full])
    late, back = lax.optimization_barrier((late, back))
    send_rows = (4 * lane_tiles + width // LANES) * TILE + 6 * lane_tiles
    chip = on_core(
        functools.partial(terms_kernel, width),
        shape((planes, send_rows, LANES), narrow),
        [place],
        [shared, shared_other, late, late_other],
        scratch=[
            pltpu.VMEM((2 * channels, channels), wide),
            pltpu.VMEM((2 * channels, channels), wide),
            pltpu.VMEM((channels, width), wide),
        ],
        megabytes=24,
    )
    plane_in = exchange(chip, ("y", "x"))
    line_out = on_core(
        plane_kernel,
        shape((2 * sections, 3 * TILE + TILE // 2, LANES), narrow),
        [],
        [plane_in],
        scratch=[pltpu.VMEM((send_rows, LANES), wide)],
    )
    line_in = exchange(line_out, ("zh", "s"))
    out_six, out_seven, out_proj, out_gains, out_biases = on_core(
        line_kernel,
        [
            shape((TILE, channels // sections), wide),
            shape((TILE, channels // sections), wide),
            shape((TILE // 2, part_width), wide),
            shape((3, channels), wide),
            shape((3, channels), wide),
        ],
        [],
        [line_in],
    )
    return (
        back.reshape(utt_local, positions, channels),
        out_six,
        out_seven,
        out_proj,
        out_gains,
        out_biases,
    )


def solution(mesh):
    fine = Mesh(mesh.devices.reshape(4, 4, 2, 2, 8), ("y", "x", "zh", "c", "s"))
    tm = ("y", "x", "zh", "c")
    return jax.shard_map(
        on_device,
        mesh=fine,
        in_specs=(
            P("s", tm, None),
            P(tm, None),
            P(tm, None),
            P(),
            P(),
            P(None, "s"),
            P(None, tm + ("s",), None),
        ),
        out_specs=(
            P("s", tm, None),
            P(tm, "s"),
            P(tm, "s"),
            P(tm, "s"),
            P(),
            P(),
        ),
        check_vma=False,
    )
```

```python
import functools

import jax
import jax.numpy as jnp
from jax import lax
from jax.experimental import pallas as pl
from jax.experimental.pallas import tpu as pltpu
from jax.sharding import Mesh, PartitionSpec as P

norm_epsilon = 1e-05
half_root = 0.7071067811865476
inv_root_tau = 0.3989422804014327
narrow = jnp.bfloat16
wide = jnp.float32
LANES = 128
TILE = 16


def gelu_parts(preact):
    normal_cdf = 0.5 * (1.0 + lax.erf(preact * half_root))
    density = jnp.exp(-0.5 * preact * preact) * inv_root_tau
    return (preact * normal_cdf, normal_cdf + preact * density)


def norm_forward(hidden, gain_row, bias_row):
    average = jnp.mean(hidden, axis=-1, keepdims=True)
    centred = hidden - average
    inv_scale = lax.rsqrt(jnp.mean(centred * centred, axis=-1, keepdims=True) + norm_epsilon)
    normal_part = centred * inv_scale
    return (normal_part * gain_row + bias_row, normal_part, inv_scale)


def norm_backward(incoming, normal_part, inv_scale, gain_row):
    scaled = incoming * gain_row
    first_mean = jnp.mean(scaled, axis=-1, keepdims=True)
    second_mean = jnp.mean(scaled * normal_part, axis=-1, keepdims=True)
    return inv_scale * (scaled - first_mean - normal_part * second_mean)


def matmul(left, right, over=(1, 0)):
    return lax.dot_general(
        left, right, (((over[0],), (over[1],)), ((), ())), preferred_element_type=wide
    )


def one_hot(shape, column_of_row):
    rows = lax.broadcasted_iota(jnp.int32, shape, 0)
    columns = lax.broadcasted_iota(jnp.int32, shape, 1)
    return jnp.where(columns == column_of_row(rows), 1.0, 0.0).astype(narrow)


def exchange(value, axes):
    return lax.all_to_all(value, axes, 0, 0, tiled=True)


def swap(value, axis):
    return lax.ppermute(value, axis, [(0, 1), (1, 0)])


def on_core(kernel, out_shape, arrays, scratch=(), megabytes=8):
    multiple = isinstance(out_shape, (list, tuple))
    vmem = pl.BlockSpec(memory_space=pltpu.VMEM)
    return pl.pallas_call(
        kernel,
        out_shape=out_shape,
        in_specs=[vmem] * len(arrays),
        out_specs=[vmem] * len(out_shape) if multiple else vmem,
        scratch_shapes=list(scratch),
        compiler_params=pltpu.CompilerParams(vmem_limit_bytes=megabytes * 1024 * 1024),
    )(*arrays)


def conv_kernel(six_ref, seven_ref, conv_ref):
    lane_tiles = six_ref.shape[1] // LANES
    for index, source in enumerate((six_ref, seven_ref)):
        for lane in range(lane_tiles):
            at = (index * lane_tiles + lane) * TILE
            conv_ref[at : at + TILE] = source[:, lane * LANES : (lane + 1) * LANES]


def pick_kernel(proj_hbm, grad_hbm, out_ref, proj_ref, grad_ref, done):
    plane, core = lax.axis_index(("y", "x")), lax.axis_index("c")
    row = pl.multiple_of(jnp.minimum(plane, proj_hbm.shape[0] // TILE - 1) * TILE, TILE)
    lane = pl.multiple_of(core * 2 * LANES, LANES)
    grad_copy = pltpu.make_async_copy(grad_hbm, grad_ref, done.at[0])
    proj_copy = pltpu.make_async_copy(
        proj_hbm.at[pl.ds(row, TILE), pl.ds(lane, 2 * LANES)], proj_ref, done.at[1]
    )
    grad_copy.start()
    proj_copy.start()
    grad_copy.wait()
    proj_copy.wait()
    sections = out_ref.shape[0]
    utterances = grad_ref.shape[0] // sections
    width = grad_ref.shape[2]
    for section in range(sections):
        for k in range(2):
            out_ref[section, k * TILE : (k + 1) * TILE] = proj_ref[:, k * LANES : (k + 1) * LANES]
        part = jnp.concatenate(
            [grad_ref[section * utterances + k].astype(wide) for k in range(utterances)], axis=0
        )
        for lane in range(0, width, 2 * LANES):
            pieces = [
                part[:, at : at + LANES] for at in range(lane, min(width, lane + 2 * LANES), LANES)
            ]
            start = 2 * TILE + lane // LANES * (TILE // 2)
            out_ref[section, start : start + len(pieces) * (TILE // 2)] = jnp.concatenate(
                pieces, axis=0
            ).astype(narrow)


def bundle_kernel(own_ref, other_ref, arrived_ref, out_ref):
    half = lax.axis_index("zh")
    rows = own_ref.shape[0]
    for plane in range(out_ref.shape[0]):
        out_ref[plane, pl.ds(pl.multiple_of(half * rows, TILE), rows)] = own_ref[...]
        out_ref[plane, pl.ds(pl.multiple_of((1 - half) * rows, TILE), rows)] = other_ref[...]
        for section in range(arrived_ref.shape[0]):
            at = 2 * rows + section * 2 * TILE
            out_ref[plane, at : at + 2 * TILE] = arrived_ref[section, : 2 * TILE]


def position_order(frames):
    def source_row(rows):
        run = rows // frames
        return 4 * (rows % frames) + (run % 2) * 2 + run // 2

    return one_hot((4 * frames, 4 * frames), source_row)


def place_proj(source_ref, proj_ref, row_tiles, section_rows):
    sections = proj_ref.shape[0] // section_rows
    first = source_ref.shape[1] - 2 * sections

    def step(plane, carry):
        for section in range(sections):
            rows = pl.ds(pl.multiple_of(section * section_rows + plane * TILE, TILE), TILE)
            for k in range(2):
                proj_ref[rows, k * LANES : (k + 1) * LANES] = source_ref[
                    plane, first + section * 2 + k
                ]
        return carry

    lax.fori_loop(0, row_tiles, step, 0)


def early_kernel(input_ref, own_ref, grad_ref, shared_ref, part_ref, proj_ref, rows_ref):
    frames, width = rows_ref.shape
    sections = grad_ref.shape[0]
    channels = input_ref.shape[1]
    shared_ref[:, :channels] = matmul(position_order(frames), input_ref[...]).astype(narrow)

    run = frames // (2 * sections)

    def arrived_row(rows):
        utterance = rows // (sections * run)
        rest = rows % (sections * run)
        return (rest // run) * (2 * run) + utterance * run + rest % run

    eight = frames // sections
    for section in range(sections):
        for lane in range(width // LANES):
            start = 2 * TILE + lane * eight
            if lane % 2 == 0:
                count = min(2, width // LANES - lane)
                stacked = grad_ref[section, start : start + count * eight].astype(wide)
            rows_ref[
                section * eight : (section + 1) * eight, lane * LANES : (lane + 1) * LANES
            ] = stacked[(lane % 2) * eight : (lane % 2 + 1) * eight]
    grad_rows = matmul(
        one_hot((frames, frames), arrived_row), rows_ref[...].astype(narrow)
    ).astype(narrow)
    for k in range(4):
        lanes = min(channels, width - k * channels)
        shared_ref[k * frames : (k + 1) * frames, channels : channels + lanes] = grad_rows[
            :, k * channels : k * channels + lanes
        ]
    shared_ref[3 * frames :, channels + lanes :] = jnp.zeros((frames, channels - lanes), narrow)
    place_proj(own_ref, proj_ref, width // sections // TILE, width // sections)
    part_ref[...] = matmul(grad_rows, proj_ref[...])


def cotangents_of(shared_ref, width):
    frames, channels = shared_ref.shape[0] // 4, shared_ref.shape[1] // 2
    rows = jnp.concatenate(
        [shared_ref[k * frames : (k + 1) * frames, channels:] for k in range(4)], axis=1
    )
    return rows[:, :width]


def layer_kernel(
    width,
    shared_ref,
    own_ref,
    other_ref,
    part_ref,
    gains_ref,
    biases_ref,
    six_ref,
    late_ref,
    seven_ref,
    proj_ref,
):
    core = lax.axis_index("c")
    frames, channels = part_ref.shape[0], shared_ref.shape[1] // 2
    lane_tiles = channels // LANES
    planes = own_ref.shape[0]
    sections = (own_ref.shape[1] - 4 * lane_tiles) // 2
    section_rows = width // sections

    def place_tiles(plane, carry):
        for half in range(2):
            for source, index in ((own_ref, core), (other_ref, 1 - core)):
                rows = pl.ds(
                    pl.multiple_of(((plane * 2 + half) * 2 + index) * TILE, TILE), TILE
                )
                for lane in range(lane_tiles):
                    lanes = slice(lane * LANES, (lane + 1) * LANES)
                    tile = half * 2 * lane_tiles + lane
                    six_ref[rows, lanes] = source[plane, tile]
                    seven_ref[rows, lanes] = source[plane, tile + lane_tiles]
        return carry

    lax.fori_loop(0, planes, place_tiles, 0)

    place_proj(other_ref, proj_ref, section_rows // TILE, section_rows)
    tap_zero, tap_one = shared_ref[: 2 * frames, :channels], shared_ref[2 * frames :, :channels]
    hid_six = matmul(tap_zero, six_ref[:channels]) + matmul(tap_one, six_ref[channels:])
    pre_six, part_six, scale_six = norm_forward(hid_six, gains_ref[0:1], biases_ref[0:1])
    act_six_f, deriv_six = gelu_parts(pre_six)
    act_six = act_six_f.astype(narrow)
    act_zero, act_one = act_six[:frames], act_six[frames:]
    hid_seven = matmul(act_zero, seven_ref[:channels]) + matmul(act_one, seven_ref[channels:])
    pre_seven, part_seven, scale_seven = norm_forward(
        hid_seven, gains_ref[1:2], biases_ref[1:2]
    )
    act_seven_f, deriv_seven = gelu_parts(pre_seven)
    pre_feat, part_feat, scale_feat = norm_forward(
        act_seven_f.astype(narrow).astype(wide), gains_ref[2:3], biases_ref[2:3]
    )
    normed = pre_feat.astype(narrow)

    grad_rows = cotangents_of(shared_ref, width)
    own_half, other_half = part_ref[...], matmul(grad_rows, proj_ref[...])
    first = core == 0
    grad_normed = jnp.concatenate(
        [jnp.where(first, own_half, other_half), jnp.where(first, other_half, own_half)], axis=1
    )
    dact_seven = norm_backward(grad_normed, part_feat, scale_feat, gains_ref[2:3])
    dpre_seven = dact_seven * deriv_seven
    dhid_seven = norm_backward(dpre_seven, part_seven, scale_seven, gains_ref[1:2]).astype(narrow)
    dact_six = jnp.concatenate(
        [
            matmul(dhid_seven, seven_ref[:channels], (1, 1)),
            matmul(dhid_seven, seven_ref[channels:], (1, 1)),
        ],
        axis=0,
    )
    dpre_six = dact_six * deriv_six
    dhid_six = norm_backward(dpre_six, part_six, scale_six, gains_ref[0:1]).astype(narrow)
    def total(value):
        return jnp.sum(value, axis=0, keepdims=True)

    sums = jnp.concatenate(
        [
            total(dpre_six * part_six),
            total(dpre_seven * part_seven),
            total(grad_normed * part_feat),
            total(dpre_six),
            total(dpre_seven),
            total(grad_normed),
        ],
        axis=0,
    )
    late_ref[: 2 * frames] = dhid_six
    late_ref[2 * frames : 4 * frames] = act_six
    late_ref[4 * frames : 5 * frames] = dhid_seven
    late_ref[5 * frames : 6 * frames] = normed
    late_ref[6 * frames :] = jnp.concatenate(
        [sums, jnp.zeros((TILE - sums.shape[0], channels), wide)], axis=0
    ).astype(narrow)


def terms_kernel(
    width,
    shared_ref,
    shared_other_ref,
    late_ref,
    late_other_ref,
    send_ref,
    term_six_ref,
    term_seven_ref,
    term_proj_ref,
):
    core = lax.axis_index("c")
    frames, channels = shared_ref.shape[0] // 4, late_ref.shape[1]
    lane_tiles = channels // LANES
    planes = send_ref.shape[0]

    def both(start, stop, left=shared_ref, right=shared_other_ref):
        rows = slice(start * frames, stop * frames)
        return jnp.concatenate([left[rows, :channels], right[rows, :channels]], axis=0)

    def late(start, stop):
        return both(start, stop, late_ref, late_other_ref)

    dhid_six, dhid_seven, normed = late(0, 2), late(4, 5), late(5, 6)
    term_six_ref[:channels] = matmul(both(0, 2), dhid_six, (0, 0))
    term_six_ref[channels:] = matmul(both(2, 4), dhid_six, (0, 0))
    term_seven_ref[:channels] = matmul(late(2, 3), dhid_seven, (0, 0))
    term_seven_ref[channels:] = matmul(late(3, 4), dhid_seven, (0, 0))
    grad_rows = jnp.concatenate(
        [cotangents_of(shared_ref, width), cotangents_of(shared_other_ref, width)], axis=0
    )
    term_proj_ref[...] = matmul(normed, grad_rows, (0, 0))
    half_rows = TILE // 2

    def pack(plane, carry):
        proj_rows = []
        for half in range(2):
            group = (plane * 2 + half) * 2 + core
            rows = pl.ds(pl.multiple_of(group * TILE, TILE), TILE)
            for lane in range(lane_tiles):
                lanes = slice(lane * LANES, (lane + 1) * LANES)
                at = (half * lane_tiles + lane) * TILE
                send_ref[plane, at : at + TILE] = term_six_ref[rows, lanes].astype(narrow)
                at += 2 * lane_tiles * TILE
                send_ref[plane, at : at + TILE] = term_seven_ref[rows, lanes].astype(narrow)
            proj_rows.append(
                term_proj_ref[pl.ds(pl.multiple_of(group * half_rows, half_rows), half_rows)]
            )
        proj_block = jnp.concatenate(proj_rows, axis=0).astype(narrow)
        for lane in range(width // LANES):
            at = (4 * lane_tiles + lane) * TILE
            send_ref[plane, at : at + TILE] = proj_block[:, lane * LANES : (lane + 1) * LANES]
        return carry

    lax.fori_loop(0, planes, pack, 0)
    sums = (late_ref[6 * frames :].astype(wide) + late_other_ref[6 * frames :].astype(wide))[:6]
    sums = jnp.concatenate(
        [sums[:, lane * LANES : (lane + 1) * LANES] for lane in range(lane_tiles)], axis=0
    ).astype(narrow)
    at = (4 * lane_tiles + width // LANES) * TILE
    send_ref[:, at:] = jnp.broadcast_to(sums[None], (planes,) + sums.shape)


def input_kernel(late_ref, six_ref, back_ref):
    channels = back_ref.shape[1]
    dhid_six = late_ref[: back_ref.shape[0] // 2]
    back = jnp.concatenate(
        [
            matmul(dhid_six, six_ref[:channels], (1, 1)).astype(narrow),
            matmul(dhid_six, six_ref[channels:], (1, 1)).astype(narrow),
        ],
        axis=0,
    )
    back_ref[...] = matmul(position_order(back_ref.shape[0] // 4), back, (0, 0)).astype(narrow)


def plane_kernel(arrived_ref, out_ref, total_ref):
    planes, rows = arrived_ref.shape[0], arrived_ref.shape[1]
    for start in range(0, rows, TILE):
        at = slice(start, min(start + TILE, rows))
        running = arrived_ref[0, at].astype(wide)
        for plane in range(1, planes):
            running += arrived_ref[plane, at].astype(wide)
        total_ref[at] = running
    sections = out_ref.shape[0] // 2
    lane_tiles = sections // 2
    sum_rows = 6 * lane_tiles
    proj_tiles = (rows - sum_rows) // TILE - 4 * lane_tiles
    left = lax.broadcasted_iota(jnp.int32, (TILE, LANES), 1) < LANES // 2
    for half in range(2):
        for lane in range(lane_tiles):
            at = (half * lane_tiles + lane) * TILE
            six = total_ref[at : at + TILE]
            at += 2 * lane_tiles * TILE
            seven = total_ref[at : at + TILE]
            place = half * sections + 2 * lane
            out_ref[place, :TILE] = jnp.where(
                left, six, pltpu.roll(seven, LANES // 2, 1)
            ).astype(narrow)
            out_ref[place + 1, :TILE] = jnp.where(
                left, pltpu.roll(six, LANES // 2, 1), seven
            ).astype(narrow)
    base = 4 * lane_tiles * TILE
    proj = jnp.concatenate(
        [total_ref[base + lane * TILE : base + (lane + 1) * TILE] for lane in range(proj_tiles)],
        axis=1,
    )
    width = proj.shape[1]
    part = width // sections
    for section in range(sections):
        shift = (width - section * part) % width
        moved = pltpu.roll(proj, shift, 1) if shift else proj
        for half in range(2):
            rows_of = slice(half * (TILE // 2), (half + 1) * (TILE // 2))
            out_ref[half * sections + section, TILE : 2 * TILE] = jnp.concatenate(
                [moved[rows_of, :LANES], moved[rows_of, LANES : 2 * LANES]], axis=0
            ).astype(narrow)
    sums = total_ref[rows - sum_rows :].astype(narrow)
    out_ref[:, 2 * TILE :] = jnp.broadcast_to(sums[None], (2 * sections,) + sums.shape)


def line_kernel(arrived_ref, six_ref, seven_ref, proj_ref, gains_ref, biases_ref):
    running = arrived_ref[0].astype(wide)
    for source in range(1, arrived_ref.shape[0]):
        running += arrived_ref[source].astype(wide)
    half = LANES // 2
    six_ref[...] = running[:TILE, :half]
    seven_ref[...] = running[:TILE, half:]
    rows = TILE // 2
    proj = jnp.concatenate(
        [running[TILE : TILE + rows], running[TILE + rows : 2 * TILE]], axis=1
    )
    proj_ref[...] = proj[:, : proj_ref.shape[1]]
    sums = jnp.concatenate(
        [running[2 * TILE + k * 6 : 2 * TILE + (k + 1) * 6] for k in range(4)], axis=1
    )
    gains_ref[...] = sums[:3]
    biases_ref[...] = sums[3:6]


def on_device(layer_five, conv_six, conv_seven, gains, biases, proj_weight, feature_grad):
    utt_local, positions, channels = layer_five.shape
    width = feature_grad.shape[2]
    part_width = proj_weight.shape[1]
    sections = lax.axis_size("s")
    planes = lax.axis_size(("y", "x"))
    frames = utt_local * positions // 4
    shape = jax.ShapeDtypeStruct

    lane_tiles = channels // LANES
    tile_rows = 2 * lane_tiles * TILE
    convs = on_core(conv_kernel, shape((tile_rows, LANES), narrow), [conv_six, conv_seven])
    in_hbm = pl.BlockSpec(memory_space=pl.ANY)
    outgoing = pl.pallas_call(
        pick_kernel,
        out_shape=shape((sections, 2 * TILE + width // LANES * (TILE // 2), LANES), narrow),
        in_specs=[in_hbm, in_hbm],
        out_specs=pl.BlockSpec(memory_space=pltpu.VMEM),
        scratch_shapes=[
            pltpu.VMEM((TILE, 2 * LANES), narrow),
            pltpu.VMEM(feature_grad.shape, narrow),
            pltpu.SemaphoreType.DMA((2,)),
        ],
        compiler_params=pltpu.CompilerParams(vmem_limit_bytes=56 * 1024 * 1024),
    )(proj_weight.T, feature_grad)
    line = 2 * sections
    opposite = [
        (z, (1 - z // sections) * sections + (z % sections + sections // 2) % sections)
        for z in range(line)
    ]
    other_convs = lax.ppermute(convs, ("zh", "s"), opposite)
    arrived = exchange(outgoing, "s")
    bundle = on_core(
        bundle_kernel,
        shape((planes, 2 * tile_rows + sections * 2 * TILE, LANES), narrow),
        [convs, other_convs, arrived],
    )
    gathered = exchange(bundle, ("y", "x"))
    sibling = swap(gathered.reshape(-1, LANES), "c")

    tiles_shape = (planes, bundle.shape[1] // TILE, TILE, LANES)
    shared, part = on_core(
        early_kernel,
        [shape((4 * frames, 2 * channels), narrow), shape((frames, 2 * LANES), wide)],
        [layer_five.reshape(4 * frames, channels), gathered.reshape(tiles_shape), arrived],
        scratch=[pltpu.VMEM((width, 2 * LANES), narrow), pltpu.VMEM((frames, width), wide)],
    )
    shared_other = swap(shared, "c")
    six_full, late = on_core(
        functools.partial(layer_kernel, width),
        [
            shape((2 * channels, channels), narrow),
            shape((6 * frames + TILE, channels), narrow),
        ],
        [
            shared,
            gathered.reshape(tiles_shape),
            sibling.reshape(tiles_shape),
            part,
            gains,
            biases,
        ],
        scratch=[
            pltpu.VMEM((2 * channels, channels), narrow),
            pltpu.VMEM((width, 2 * LANES), narrow),
        ],
        megabytes=16,
    )
    late_other = swap(late, "c")
    back = on_core(input_kernel, shape((4 * frames, channels), narrow), [late, six_full])
    late, back = lax.optimization_barrier((late, back))
    send_rows = (4 * lane_tiles + width // LANES) * TILE + 6 * lane_tiles
    chip = on_core(
        functools.partial(terms_kernel, width),
        shape((planes, send_rows, LANES), narrow),
        [shared, shared_other, late, late_other],
        scratch=[
            pltpu.VMEM((2 * channels, channels), wide),
            pltpu.VMEM((2 * channels, channels), wide),
            pltpu.VMEM((channels, width), wide),
        ],
        megabytes=24,
    )
    plane_in = exchange(chip, ("y", "x"))
    line_out = on_core(
        plane_kernel,
        shape((2 * sections, 3 * TILE + TILE // 2, LANES), narrow),
        [plane_in],
        scratch=[pltpu.VMEM((send_rows, LANES), wide)],
    )
    line_in = exchange(line_out, ("zh", "s"))
    out_six, out_seven, out_proj, out_gains, out_biases = on_core(
        line_kernel,
        [
            shape((TILE, channels // sections), wide),
            shape((TILE, channels // sections), wide),
            shape((TILE // 2, part_width), wide),
            shape((3, channels), wide),
            shape((3, channels), wide),
        ],
        [line_in],
    )
    return (
        back.reshape(utt_local, positions, channels),
        out_six,
        out_seven,
        out_proj,
        out_gains,
        out_biases,
    )


def solution(mesh):
    fine = Mesh(mesh.devices.reshape(4, 4, 2, 2, 8), ("y", "x", "zh", "c", "s"))
    tm = ("y", "x", "zh", "c")
    return jax.shard_map(
        on_device,
        mesh=fine,
        in_specs=(
            P("s", tm, None),
            P(tm, None),
            P(tm, None),
            P(),
            P(),
            P(None, "s"),
            P(None, tm + ("s",), None),
        ),
        out_specs=(
            P("s", tm, None),
            P(tm, "s"),
            P(tm, "s"),
            P(tm, "s"),
            P(),
            P(),
        ),
        check_vma=False,
    )
```

```python
import functools

import jax
import jax.numpy as jnp
from jax import lax
from jax.experimental import pallas as pl
from jax.experimental.pallas import tpu as pltpu
from jax.sharding import Mesh, PartitionSpec as P

norm_epsilon = 1e-05
half_root = 0.7071067811865476
inv_root_tau = 0.3989422804014327
narrow = jnp.bfloat16
wide = jnp.float32
LANES = 128
TILE = 16


def gelu_parts(preact):
    normal_cdf = 0.5 * (1.0 + lax.erf(preact * half_root))
    density = jnp.exp(-0.5 * preact * preact) * inv_root_tau
    return (preact * normal_cdf, normal_cdf + preact * density)


def norm_forward(hidden, gain_row, bias_row):
    average = jnp.mean(hidden, axis=-1, keepdims=True)
    centred = hidden - average
    inv_scale = lax.rsqrt(jnp.mean(centred * centred, axis=-1, keepdims=True) + norm_epsilon)
    normal_part = centred * inv_scale
    return (normal_part * gain_row + bias_row, normal_part, inv_scale)


def norm_backward(incoming, normal_part, inv_scale, gain_row):
    scaled = incoming * gain_row
    first_mean = jnp.mean(scaled, axis=-1, keepdims=True)
    second_mean = jnp.mean(scaled * normal_part, axis=-1, keepdims=True)
    return inv_scale * (scaled - first_mean - normal_part * second_mean)


def matmul(left, right, over=(1, 0)):
    return lax.dot_general(
        left, right, (((over[0],), (over[1],)), ((), ())), preferred_element_type=wide
    )


def one_hot(shape, column_of_row):
    rows = lax.broadcasted_iota(jnp.int32, shape, 0)
    columns = lax.broadcasted_iota(jnp.int32, shape, 1)
    return jnp.where(columns == column_of_row(rows), 1.0, 0.0).astype(narrow)


def exchange(value, axes):
    return lax.all_to_all(value, axes, 0, 0, tiled=True)


def swap(value, axis):
    return lax.ppermute(value, axis, [(0, 1), (1, 0)])


def on_core(kernel, out_shape, arrays, scratch=(), megabytes=8):
    multiple = isinstance(out_shape, (list, tuple))
    vmem = pl.BlockSpec(memory_space=pltpu.VMEM)
    return pl.pallas_call(
        kernel,
        out_shape=out_shape,
        in_specs=[vmem] * len(arrays),
        out_specs=[vmem] * len(out_shape) if multiple else vmem,
        scratch_shapes=list(scratch),
        compiler_params=pltpu.CompilerParams(vmem_limit_bytes=megabytes * 1024 * 1024),
    )(*arrays)


def conv_kernel(six_ref, seven_ref, conv_ref):
    lane_tiles = six_ref.shape[1] // LANES
    for index, source in enumerate((six_ref, seven_ref)):
        for lane in range(lane_tiles):
            at = (index * lane_tiles + lane) * TILE
            conv_ref[at : at + TILE] = source[:, lane * LANES : (lane + 1) * LANES]


def pick_kernel(proj_hbm, grad_hbm, out_ref, proj_ref, grad_ref, done):
    plane, core = lax.axis_index(("y", "x")), lax.axis_index("c")
    row = pl.multiple_of(jnp.minimum(plane, proj_hbm.shape[0] // TILE - 1) * TILE, TILE)
    lane = pl.multiple_of(core * 2 * LANES, LANES)
    grad_copy = pltpu.make_async_copy(grad_hbm, grad_ref, done.at[0])
    proj_copy = pltpu.make_async_copy(
        proj_hbm.at[pl.ds(row, TILE), pl.ds(lane, 2 * LANES)], proj_ref, done.at[1]
    )
    grad_copy.start()
    proj_copy.start()
    grad_copy.wait()
    proj_copy.wait()
    sections = out_ref.shape[0]
    utterances = grad_ref.shape[0] // sections
    width = grad_ref.shape[2]
    for section in range(sections):
        for k in range(2):
            out_ref[section, k * TILE : (k + 1) * TILE] = proj_ref[:, k * LANES : (k + 1) * LANES]
        part = jnp.concatenate(
            [grad_ref[section * utterances + k].astype(wide) for k in range(utterances)], axis=0
        )
        for lane in range(0, width, 2 * LANES):
            pieces = [
                part[:, at : at + LANES] for at in range(lane, min(width, lane + 2 * LANES), LANES)
            ]
            if len(pieces) == 1:
                pieces.append(jnp.zeros(pieces[0].shape, wide))
            start = 2 * TILE + lane // LANES * (TILE // 2)
            out_ref[section, start : start + TILE] = jnp.concatenate(pieces, axis=0).astype(narrow)


def bundle_kernel(own_ref, other_ref, arrived_ref, out_ref):
    half = lax.axis_index("zh")
    rows = own_ref.shape[0]
    for plane in range(out_ref.shape[0]):
        out_ref[plane, pl.ds(pl.multiple_of(half * rows, TILE), rows)] = own_ref[...]
        out_ref[plane, pl.ds(pl.multiple_of((1 - half) * rows, TILE), rows)] = other_ref[...]
        for section in range(arrived_ref.shape[0]):
            at = 2 * rows + section * 2 * TILE
            out_ref[plane, at : at + 2 * TILE] = arrived_ref[section, : 2 * TILE]


def position_order(frames):
    def source_row(rows):
        run = rows // frames
        return 4 * (rows % frames) + (run % 2) * 2 + run // 2

    return one_hot((4 * frames, 4 * frames), source_row)


def place_proj(source_ref, proj_ref, row_tiles, section_rows):
    sections = proj_ref.shape[0] // section_rows
    first = source_ref.shape[1] - 2 * sections

    def step(plane, carry):
        for section in range(sections):
            rows = pl.ds(pl.multiple_of(section * section_rows + plane * TILE, TILE), TILE)
            for k in range(2):
                proj_ref[rows, k * LANES : (k + 1) * LANES] = source_ref[
                    plane, first + section * 2 + k
                ]
        return carry

    lax.fori_loop(0, row_tiles, step, 0)


def early_kernel(input_ref, own_ref, grad_ref, shared_ref, part_ref, proj_ref, rows_ref):
    frames, width = rows_ref.shape
    sections = grad_ref.shape[0]
    channels = input_ref.shape[1]
    shared_ref[:, :channels] = matmul(position_order(frames), input_ref[...]).astype(narrow)

    run = frames // (2 * sections)

    def arrived_row(rows):
        utterance = rows // (sections * run)
        rest = rows % (sections * run)
        return (rest // run) * (2 * run) + utterance * run + rest % run

    eight = frames // sections
    for section in range(sections):
        for lane in range(width // LANES):
            start = 2 * TILE + lane * eight
            if lane % 2 == 0:
                stacked = grad_ref[section, start : start + TILE].astype(wide)
            rows_ref[
                section * eight : (section + 1) * eight, lane * LANES : (lane + 1) * LANES
            ] = stacked[(lane % 2) * eight : (lane % 2 + 1) * eight]
    grad_rows = matmul(
        one_hot((frames, frames), arrived_row), rows_ref[...].astype(narrow)
    ).astype(narrow)
    for k in range(4):
        lanes = min(channels, width - k * channels)
        shared_ref[k * frames : (k + 1) * frames, channels : channels + lanes] = grad_rows[
            :, k * channels : k * channels + lanes
        ]
    shared_ref[3 * frames :, channels + lanes :] = jnp.zeros((frames, channels - lanes), narrow)
    place_proj(own_ref, proj_ref, width // sections // TILE, width // sections)
    part_ref[...] = matmul(grad_rows, proj_ref[...])


def cotangents_of(shared_ref, width):
    frames, channels = shared_ref.shape[0] // 4, shared_ref.shape[1] // 2
    rows = jnp.concatenate(
        [shared_ref[k * frames : (k + 1) * frames, channels:] for k in range(4)], axis=1
    )
    return rows[:, :width]


def layer_kernel(
    width,
    shared_ref,
    own_ref,
    other_ref,
    part_ref,
    gains_ref,
    biases_ref,
    six_ref,
    late_ref,
    seven_ref,
    proj_ref,
):
    core = lax.axis_index("c")
    frames, channels = part_ref.shape[0], shared_ref.shape[1] // 2
    lane_tiles = channels // LANES
    planes = own_ref.shape[0]
    sections = (own_ref.shape[1] - 4 * lane_tiles) // 2
    section_rows = width // sections

    def place_tiles(plane, carry):
        for half in range(2):
            for source, index in ((own_ref, core), (other_ref, 1 - core)):
                rows = pl.ds(
                    pl.multiple_of(((plane * 2 + half) * 2 + index) * TILE, TILE), TILE
                )
                for lane in range(lane_tiles):
                    lanes = slice(lane * LANES, (lane + 1) * LANES)
                    tile = half * 2 * lane_tiles + lane
                    six_ref[rows, lanes] = source[plane, tile]
                    seven_ref[rows, lanes] = source[plane, tile + lane_tiles]
        return carry

    lax.fori_loop(0, planes, place_tiles, 0)

    place_proj(other_ref, proj_ref, section_rows // TILE, section_rows)
    tap_zero, tap_one = shared_ref[: 2 * frames, :channels], shared_ref[2 * frames :, :channels]
    hid_six = matmul(tap_zero, six_ref[:channels]) + matmul(tap_one, six_ref[channels:])
    pre_six, part_six, scale_six = norm_forward(hid_six, gains_ref[0:1], biases_ref[0:1])
    act_six_f, deriv_six = gelu_parts(pre_six)
    act_six = act_six_f.astype(narrow)
    act_zero, act_one = act_six[:frames], act_six[frames:]
    hid_seven = matmul(act_zero, seven_ref[:channels]) + matmul(act_one, seven_ref[channels:])
    pre_seven, part_seven, scale_seven = norm_forward(
        hid_seven, gains_ref[1:2], biases_ref[1:2]
    )
    act_seven_f, deriv_seven = gelu_parts(pre_seven)
    pre_feat, part_feat, scale_feat = norm_forward(
        act_seven_f.astype(narrow).astype(wide), gains_ref[2:3], biases_ref[2:3]
    )
    normed = pre_feat.astype(narrow)

    grad_rows = cotangents_of(shared_ref, width)
    own_half, other_half = part_ref[...], matmul(grad_rows, proj_ref[...])
    first = core == 0
    grad_normed = jnp.concatenate(
        [jnp.where(first, own_half, other_half), jnp.where(first, other_half, own_half)], axis=1
    )
    dact_seven = norm_backward(grad_normed, part_feat, scale_feat, gains_ref[2:3])
    dpre_seven = dact_seven * deriv_seven
    dhid_seven = norm_backward(dpre_seven, part_seven, scale_seven, gains_ref[1:2]).astype(narrow)
    dact_six = jnp.concatenate(
        [
            matmul(dhid_seven, seven_ref[:channels], (1, 1)),
            matmul(dhid_seven, seven_ref[channels:], (1, 1)),
        ],
        axis=0,
    )
    dpre_six = dact_six * deriv_six
    dhid_six = norm_backward(dpre_six, part_six, scale_six, gains_ref[0:1]).astype(narrow)
    def total(value):
        return jnp.sum(value, axis=0, keepdims=True)

    sums = jnp.concatenate(
        [
            total(dpre_six * part_six),
            total(dpre_seven * part_seven),
            total(grad_normed * part_feat),
            total(dpre_six),
            total(dpre_seven),
            total(grad_normed),
        ],
        axis=0,
    )
    late_ref[: 2 * frames] = dhid_six
    late_ref[2 * frames : 4 * frames] = act_six
    late_ref[4 * frames : 5 * frames] = dhid_seven
    late_ref[5 * frames : 6 * frames] = normed
    late_ref[6 * frames :] = jnp.concatenate(
        [sums, jnp.zeros((TILE - sums.shape[0], channels), wide)], axis=0
    ).astype(narrow)


def terms_kernel(
    width,
    shared_ref,
    shared_other_ref,
    late_ref,
    late_other_ref,
    send_ref,
    term_six_ref,
    term_seven_ref,
    term_proj_ref,
):
    core = lax.axis_index("c")
    frames, channels = shared_ref.shape[0] // 4, late_ref.shape[1]
    lane_tiles = channels // LANES
    planes = send_ref.shape[0]

    def both(start, stop, left=shared_ref, right=shared_other_ref):
        rows = slice(start * frames, stop * frames)
        return jnp.concatenate([left[rows, :channels], right[rows, :channels]], axis=0)

    def late(start, stop):
        return both(start, stop, late_ref, late_other_ref)

    dhid_six, dhid_seven, normed = late(0, 2), late(4, 5), late(5, 6)
    term_six_ref[:channels] = matmul(both(0, 2), dhid_six, (0, 0))
    term_six_ref[channels:] = matmul(both(2, 4), dhid_six, (0, 0))
    term_seven_ref[:channels] = matmul(late(2, 3), dhid_seven, (0, 0))
    term_seven_ref[channels:] = matmul(late(3, 4), dhid_seven, (0, 0))
    grad_rows = jnp.concatenate(
        [cotangents_of(shared_ref, width), cotangents_of(shared_other_ref, width)], axis=0
    )
    term_proj_ref[...] = matmul(normed, grad_rows, (0, 0))
    half_rows = TILE // 2

    def pack(plane, carry):
        proj_rows = []
        for half in range(2):
            group = (plane * 2 + half) * 2 + core
            rows = pl.ds(pl.multiple_of(group * TILE, TILE), TILE)
            for lane in range(lane_tiles):
                lanes = slice(lane * LANES, (lane + 1) * LANES)
                at = (half * lane_tiles + lane) * TILE
                send_ref[plane, at : at + TILE] = term_six_ref[rows, lanes].astype(narrow)
                at += 2 * lane_tiles * TILE
                send_ref[plane, at : at + TILE] = term_seven_ref[rows, lanes].astype(narrow)
            proj_rows.append(
                term_proj_ref[pl.ds(pl.multiple_of(group * half_rows, half_rows), half_rows)]
            )
        proj_block = jnp.concatenate(proj_rows, axis=0).astype(narrow)
        for lane in range(width // LANES):
            at = (4 * lane_tiles + lane) * TILE
            send_ref[plane, at : at + TILE] = proj_block[:, lane * LANES : (lane + 1) * LANES]
        return carry

    lax.fori_loop(0, planes, pack, 0)
    sums = (late_ref[6 * frames :].astype(wide) + late_other_ref[6 * frames :].astype(wide))[:6]
    sums = jnp.concatenate(
        [sums[:, lane * LANES : (lane + 1) * LANES] for lane in range(lane_tiles)]
        + [jnp.zeros((TILE // 2, LANES), wide)],
        axis=0,
    ).astype(narrow)
    at = (4 * lane_tiles + width // LANES) * TILE
    send_ref[:, at:] = jnp.broadcast_to(sums[None], (planes,) + sums.shape)


def input_kernel(late_ref, six_ref, back_ref):
    channels = back_ref.shape[1]
    dhid_six = late_ref[: back_ref.shape[0] // 2]
    back = jnp.concatenate(
        [
            matmul(dhid_six, six_ref[:channels], (1, 1)).astype(narrow),
            matmul(dhid_six, six_ref[channels:], (1, 1)).astype(narrow),
        ],
        axis=0,
    )
    back_ref[...] = matmul(position_order(back_ref.shape[0] // 4), back, (0, 0)).astype(narrow)


def plane_kernel(arrived_ref, out_ref, total_ref):
    planes, rows = arrived_ref.shape[0], arrived_ref.shape[1]
    for start in range(0, rows, TILE):
        at = slice(start, min(start + TILE, rows))
        running = arrived_ref[0, at].astype(wide)
        for plane in range(1, planes):
            running += arrived_ref[plane, at].astype(wide)
        total_ref[at] = running
    sections = out_ref.shape[0] // 2
    lane_tiles = sections // 2
    sum_rows = 2 * TILE
    proj_tiles = (rows - sum_rows) // TILE - 4 * lane_tiles
    left = lax.broadcasted_iota(jnp.int32, (TILE, LANES), 1) < LANES // 2
    for half in range(2):
        for lane in range(lane_tiles):
            at = (half * lane_tiles + lane) * TILE
            six = total_ref[at : at + TILE]
            at += 2 * lane_tiles * TILE
            seven = total_ref[at : at + TILE]
            place = half * sections + 2 * lane
            out_ref[place, :TILE] = jnp.where(
                left, six, pltpu.roll(seven, LANES // 2, 1)
            ).astype(narrow)
            out_ref[place + 1, :TILE] = jnp.where(
                left, pltpu.roll(six, LANES // 2, 1), seven
            ).astype(narrow)
    base = 4 * lane_tiles * TILE
    proj = jnp.concatenate(
        [total_ref[base + lane * TILE : base + (lane + 1) * TILE] for lane in range(proj_tiles)],
        axis=1,
    )
    width = proj.shape[1]
    part = width // sections
    for section in range(sections):
        shift = (width - section * part) % width
        moved = pltpu.roll(proj, shift, 1) if shift else proj
        for half in range(2):
            rows_of = slice(half * (TILE // 2), (half + 1) * (TILE // 2))
            out_ref[half * sections + section, TILE : 2 * TILE] = jnp.concatenate(
                [moved[rows_of, :LANES], moved[rows_of, LANES : 2 * LANES]], axis=0
            ).astype(narrow)
    sums = total_ref[rows - sum_rows :].astype(narrow)
    out_ref[:, 2 * TILE :] = jnp.broadcast_to(sums[None], (2 * sections,) + sums.shape)


def line_kernel(arrived_ref, six_ref, seven_ref, proj_ref, gains_ref, biases_ref):
    running = arrived_ref[0].astype(wide)
    for source in range(1, arrived_ref.shape[0]):
        running += arrived_ref[source].astype(wide)
    half = LANES // 2
    six_ref[...] = running[:TILE, :half]
    seven_ref[...] = running[:TILE, half:]
    rows = TILE // 2
    proj = jnp.concatenate(
        [running[TILE : TILE + rows], running[TILE + rows : 2 * TILE]], axis=1
    )
    proj_ref[...] = proj[:, : proj_ref.shape[1]]
    sums = jnp.concatenate(
        [running[2 * TILE + k * 6 : 2 * TILE + (k + 1) * 6] for k in range(4)], axis=1
    )
    gains_ref[...] = sums[:3]
    biases_ref[...] = sums[3:6]


def on_device(layer_five, conv_six, conv_seven, gains, biases, proj_weight, feature_grad):
    utt_local, positions, channels = layer_five.shape
    width = feature_grad.shape[2]
    part_width = proj_weight.shape[1]
    sections = lax.axis_size("s")
    planes = lax.axis_size(("y", "x"))
    frames = utt_local * positions // 4
    shape = jax.ShapeDtypeStruct

    lane_tiles = channels // LANES
    tile_rows = 2 * lane_tiles * TILE
    convs = on_core(conv_kernel, shape((tile_rows, LANES), narrow), [conv_six, conv_seven])
    in_hbm = pl.BlockSpec(memory_space=pl.ANY)
    outgoing = pl.pallas_call(
        pick_kernel,
        out_shape=shape((sections, 2 * TILE + (width // LANES + 1) // 2 * TILE, LANES), narrow),
        in_specs=[in_hbm, in_hbm],
        out_specs=pl.BlockSpec(memory_space=pltpu.VMEM),
        scratch_shapes=[
            pltpu.VMEM((TILE, 2 * LANES), narrow),
            pltpu.VMEM(feature_grad.shape, narrow),
            pltpu.SemaphoreType.DMA((2,)),
        ],
        compiler_params=pltpu.CompilerParams(vmem_limit_bytes=56 * 1024 * 1024),
    )(proj_weight.T, feature_grad)
    line = 2 * sections
    opposite = [
        (z, (1 - z // sections) * sections + (z % sections + sections // 2) % sections)
        for z in range(line)
    ]
    other_convs = lax.ppermute(convs, ("zh", "s"), opposite)
    arrived = exchange(outgoing, "s")
    bundle = on_core(
        bundle_kernel,
        shape((planes, 2 * tile_rows + sections * 2 * TILE, LANES), narrow),
        [convs, other_convs, arrived],
    )
    gathered = exchange(bundle, ("y", "x"))
    sibling = swap(gathered.reshape(-1, LANES), "c")

    tiles_shape = (planes, bundle.shape[1] // TILE, TILE, LANES)
    shared, part = on_core(
        early_kernel,
        [shape((4 * frames, 2 * channels), narrow), shape((frames, 2 * LANES), wide)],
        [layer_five.reshape(4 * frames, channels), gathered.reshape(tiles_shape), arrived],
        scratch=[pltpu.VMEM((width, 2 * LANES), narrow), pltpu.VMEM((frames, width), wide)],
    )
    shared_other = swap(shared, "c")
    six_full, late = on_core(
        functools.partial(layer_kernel, width),
        [
            shape((2 * channels, channels), narrow),
            shape((6 * frames + TILE, channels), narrow),
        ],
        [
            shared,
            gathered.reshape(tiles_shape),
            sibling.reshape(tiles_shape),
            part,
            gains,
            biases,
        ],
        scratch=[
            pltpu.VMEM((2 * channels, channels), narrow),
            pltpu.VMEM((width, 2 * LANES), narrow),
        ],
        megabytes=16,
    )
    late_other = swap(late, "c")
    back = on_core(input_kernel, shape((4 * frames, channels), narrow), [late, six_full])
    late, back = lax.optimization_barrier((late, back))
    send_rows = (4 * lane_tiles + width // LANES + 2) * TILE
    chip = on_core(
        functools.partial(terms_kernel, width),
        shape((planes, send_rows, LANES), narrow),
        [shared, shared_other, late, late_other],
        scratch=[
            pltpu.VMEM((2 * channels, channels), wide),
            pltpu.VMEM((2 * channels, channels), wide),
            pltpu.VMEM((channels, width), wide),
        ],
        megabytes=24,
    )
    plane_in = exchange(chip, ("y", "x"))
    line_out = on_core(
        plane_kernel,
        shape((2 * sections, 4 * TILE, LANES), narrow),
        [plane_in],
        scratch=[pltpu.VMEM((send_rows, LANES), wide)],
    )
    line_in = exchange(line_out, ("zh", "s"))
    out_six, out_seven, out_proj, out_gains, out_biases = on_core(
        line_kernel,
        [
            shape((TILE, channels // sections), wide),
            shape((TILE, channels // sections), wide),
            shape((TILE // 2, part_width), wide),
            shape((3, channels), wide),
            shape((3, channels), wide),
        ],
        [line_in],
    )
    return (
        back.reshape(utt_local, positions, channels),
        out_six,
        out_seven,
        out_proj,
        out_gains,
        out_biases,
    )


def solution(mesh):
    fine = Mesh(mesh.devices.reshape(4, 4, 2, 2, 8), ("y", "x", "zh", "c", "s"))
    tm = ("y", "x", "zh", "c")
    return jax.shard_map(
        on_device,
        mesh=fine,
        in_specs=(
            P("s", tm, None),
            P(tm, None),
            P(tm, None),
            P(),
            P(),
            P(None, "s"),
            P(None, tm + ("s",), None),
        ),
        out_specs=(
            P("s", tm, None),
            P(tm, "s"),
            P(tm, "s"),
            P(tm, "s"),
            P(),
            P(),
        ),
        check_vma=False,
    )
```

```python
import functools

import jax
import jax.numpy as jnp
from jax import lax
from jax.experimental import pallas as pl
from jax.experimental.pallas import tpu as pltpu
from jax.sharding import Mesh, PartitionSpec as P

norm_epsilon = 1e-05
half_root = 0.7071067811865476
inv_root_tau = 0.3989422804014327
narrow = jnp.bfloat16
wide = jnp.float32
LANES = 128
TILE = 16


def gelu_parts(preact):
    normal_cdf = 0.5 * (1.0 + lax.erf(preact * half_root))
    density = jnp.exp(-0.5 * preact * preact) * inv_root_tau
    return (preact * normal_cdf, normal_cdf + preact * density)


def norm_forward(hidden, gain_row, bias_row):
    average = jnp.mean(hidden, axis=-1, keepdims=True)
    centred = hidden - average
    inv_scale = lax.rsqrt(jnp.mean(centred * centred, axis=-1, keepdims=True) + norm_epsilon)
    normal_part = centred * inv_scale
    return (normal_part * gain_row + bias_row, normal_part, inv_scale)


def norm_backward(incoming, normal_part, inv_scale, gain_row):
    scaled = incoming * gain_row
    first_mean = jnp.mean(scaled, axis=-1, keepdims=True)
    second_mean = jnp.mean(scaled * normal_part, axis=-1, keepdims=True)
    return inv_scale * (scaled - first_mean - normal_part * second_mean)


def matmul(left, right, over=(1, 0)):
    return lax.dot_general(
        left, right, (((over[0],), (over[1],)), ((), ())), preferred_element_type=wide
    )


def one_hot(shape, column_of_row):
    rows = lax.broadcasted_iota(jnp.int32, shape, 0)
    columns = lax.broadcasted_iota(jnp.int32, shape, 1)
    return jnp.where(columns == column_of_row(rows), 1.0, 0.0).astype(narrow)


def exchange(value, axes):
    return lax.all_to_all(value, axes, 0, 0, tiled=True)


def swap(value, axis):
    return lax.ppermute(value, axis, [(0, 1), (1, 0)])


def on_core(kernel, out_shape, arrays, scratch=(), megabytes=8):
    multiple = isinstance(out_shape, (list, tuple))
    vmem = pl.BlockSpec(memory_space=pltpu.VMEM)
    return pl.pallas_call(
        kernel,
        out_shape=out_shape,
        in_specs=[vmem] * len(arrays),
        out_specs=[vmem] * len(out_shape) if multiple else vmem,
        scratch_shapes=list(scratch),
        compiler_params=pltpu.CompilerParams(vmem_limit_bytes=megabytes * 1024 * 1024),
    )(*arrays)


def conv_kernel(six_ref, seven_ref, conv_ref):
    lane_tiles = six_ref.shape[1] // LANES
    for index, source in enumerate((six_ref, seven_ref)):
        for lane in range(lane_tiles):
            at = (index * lane_tiles + lane) * TILE
            conv_ref[at : at + TILE] = source[:, lane * LANES : (lane + 1) * LANES]


def pick_kernel(proj_hbm, grad_hbm, out_ref, proj_ref, grad_ref, done):
    plane, core = lax.axis_index(("y", "x")), lax.axis_index("c")
    row = pl.multiple_of(jnp.minimum(plane, proj_hbm.shape[0] // TILE - 1) * TILE, TILE)
    lane = pl.multiple_of(core * 2 * LANES, LANES)
    grad_copy = pltpu.make_async_copy(grad_hbm, grad_ref, done.at[0])
    proj_copy = pltpu.make_async_copy(
        proj_hbm.at[pl.ds(row, TILE), pl.ds(lane, 2 * LANES)], proj_ref, done.at[1]
    )
    grad_copy.start()
    proj_copy.start()
    grad_copy.wait()
    proj_copy.wait()
    sections = out_ref.shape[0]
    utterances = grad_ref.shape[0] // sections
    width = grad_ref.shape[2]
    for section in range(sections):
        for k in range(2):
            out_ref[section, k * TILE : (k + 1) * TILE] = proj_ref[:, k * LANES : (k + 1) * LANES]
        part = jnp.concatenate(
            [grad_ref[section * utterances + k].astype(wide) for k in range(utterances)], axis=0
        )
        for lane in range(0, width, 2 * LANES):
            pieces = [
                part[:, at : at + LANES] for at in range(lane, min(width, lane + 2 * LANES), LANES)
            ]
            start = 2 * TILE + lane // LANES * (TILE // 2)
            out_ref[section, start : start + len(pieces) * (TILE // 2)] = jnp.concatenate(
                pieces, axis=0
            ).astype(narrow)


def bundle_kernel(own_ref, other_ref, arrived_ref, out_ref):
    half = lax.axis_index("zh")
    rows = own_ref.shape[0]
    for plane in range(out_ref.shape[0]):
        out_ref[plane, pl.ds(pl.multiple_of(half * rows, TILE), rows)] = own_ref[...]
        out_ref[plane, pl.ds(pl.multiple_of((1 - half) * rows, TILE), rows)] = other_ref[...]
        for section in range(arrived_ref.shape[0]):
            at = 2 * rows + section * 2 * TILE
            out_ref[plane, at : at + 2 * TILE] = arrived_ref[section, : 2 * TILE]


def position_order(frames):
    def source_row(rows):
        run = rows // frames
        return 4 * (rows % frames) + (run % 2) * 2 + run // 2

    return one_hot((4 * frames, 4 * frames), source_row)


def place_proj(source_ref, proj_ref, row_tiles, section_rows):
    sections = proj_ref.shape[0] // section_rows
    first = source_ref.shape[1] - 2 * sections

    def step(plane, carry):
        for section in range(sections):
            rows = pl.ds(pl.multiple_of(section * section_rows + plane * TILE, TILE), TILE)
            for k in range(2):
                proj_ref[rows, k * LANES : (k + 1) * LANES] = source_ref[
                    plane, first + section * 2 + k
                ]
        return carry

    lax.fori_loop(0, row_tiles, step, 0)


def early_kernel(input_ref, own_ref, grad_ref, shared_ref, part_ref, proj_ref, rows_ref):
    frames, width = rows_ref.shape
    sections = grad_ref.shape[0]
    channels = input_ref.shape[1]
    shared_ref[:, :channels] = matmul(position_order(frames), input_ref[...]).astype(narrow)

    run = frames // (2 * sections)

    def arrived_row(rows):
        utterance = rows // (sections * run)
        rest = rows % (sections * run)
        return (rest // run) * (2 * run) + utterance * run + rest % run

    eight = frames // sections
    for section in range(sections):
        for lane in range(width // LANES):
            start = 2 * TILE + lane * eight
            if lane % 2 == 0:
                count = min(2, width // LANES - lane)
                stacked = grad_ref[section, start : start + count * eight].astype(wide)
            rows_ref[
                section * eight : (section + 1) * eight, lane * LANES : (lane + 1) * LANES
            ] = stacked[(lane % 2) * eight : (lane % 2 + 1) * eight]
    grad_rows = matmul(
        one_hot((frames, frames), arrived_row), rows_ref[...].astype(narrow)
    ).astype(narrow)
    for k in range(4):
        lanes = min(channels, width - k * channels)
        shared_ref[k * frames : (k + 1) * frames, channels : channels + lanes] = grad_rows[
            :, k * channels : k * channels + lanes
        ]
    shared_ref[3 * frames :, channels + lanes :] = jnp.zeros((frames, channels - lanes), narrow)
    place_proj(own_ref, proj_ref, width // sections // TILE, width // sections)
    part_ref[...] = matmul(grad_rows, proj_ref[...])


def cotangents_of(shared_ref, width):
    frames, channels = shared_ref.shape[0] // 4, shared_ref.shape[1] // 2
    rows = jnp.concatenate(
        [shared_ref[k * frames : (k + 1) * frames, channels:] for k in range(4)], axis=1
    )
    return rows[:, :width]


def layer_kernel(
    width,
    shared_ref,
    own_ref,
    other_ref,
    part_ref,
    gains_ref,
    biases_ref,
    six_ref,
    late_ref,
    seven_ref,
    proj_ref,
):
    core = lax.axis_index("c")
    frames, channels = part_ref.shape[0], shared_ref.shape[1] // 2
    lane_tiles = channels // LANES
    planes = own_ref.shape[0]
    sections = (own_ref.shape[1] - 4 * lane_tiles) // 2
    section_rows = width // sections

    def place_tiles(plane, carry):
        for half in range(2):
            for source, index in ((own_ref, core), (other_ref, 1 - core)):
                rows = pl.ds(
                    pl.multiple_of(((plane * 2 + half) * 2 + index) * TILE, TILE), TILE
                )
                for lane in range(lane_tiles):
                    lanes = slice(lane * LANES, (lane + 1) * LANES)
                    tile = half * 2 * lane_tiles + lane
                    six_ref[rows, lanes] = source[plane, tile]
                    seven_ref[rows, lanes] = source[plane, tile + lane_tiles]
        return carry

    lax.fori_loop(0, planes, place_tiles, 0)

    place_proj(other_ref, proj_ref, section_rows // TILE, section_rows)
    tap_zero, tap_one = shared_ref[: 2 * frames, :channels], shared_ref[2 * frames :, :channels]
    hid_six = matmul(tap_zero, six_ref[:channels]) + matmul(tap_one, six_ref[channels:])
    pre_six, part_six, scale_six = norm_forward(hid_six, gains_ref[0:1], biases_ref[0:1])
    act_six_f, deriv_six = gelu_parts(pre_six)
    act_six = act_six_f.astype(narrow)
    act_zero, act_one = act_six[:frames], act_six[frames:]
    hid_seven = matmul(act_zero, seven_ref[:channels]) + matmul(act_one, seven_ref[channels:])
    pre_seven, part_seven, scale_seven = norm_forward(
        hid_seven, gains_ref[1:2], biases_ref[1:2]
    )
    act_seven_f, deriv_seven = gelu_parts(pre_seven)
    pre_feat, part_feat, scale_feat = norm_forward(
        act_seven_f.astype(narrow).astype(wide), gains_ref[2:3], biases_ref[2:3]
    )
    normed = pre_feat.astype(narrow)

    grad_rows = cotangents_of(shared_ref, width)
    own_half, other_half = part_ref[...], matmul(grad_rows, proj_ref[...])
    first = core == 0
    grad_normed = jnp.concatenate(
        [jnp.where(first, own_half, other_half), jnp.where(first, other_half, own_half)], axis=1
    )
    dact_seven = norm_backward(grad_normed, part_feat, scale_feat, gains_ref[2:3])
    dpre_seven = dact_seven * deriv_seven
    dhid_seven = norm_backward(dpre_seven, part_seven, scale_seven, gains_ref[1:2]).astype(narrow)
    dact_six = jnp.concatenate(
        [
            matmul(dhid_seven, seven_ref[:channels], (1, 1)),
            matmul(dhid_seven, seven_ref[channels:], (1, 1)),
        ],
        axis=0,
    )
    dpre_six = dact_six * deriv_six
    dhid_six = norm_backward(dpre_six, part_six, scale_six, gains_ref[0:1]).astype(narrow)
    def total(value):
        return jnp.sum(value, axis=0, keepdims=True)

    sums = jnp.concatenate(
        [
            total(dpre_six * part_six),
            total(dpre_seven * part_seven),
            total(grad_normed * part_feat),
            total(dpre_six),
            total(dpre_seven),
            total(grad_normed),
        ],
        axis=0,
    )
    late_ref[: 2 * frames] = dhid_six
    late_ref[2 * frames : 4 * frames] = act_six
    late_ref[4 * frames : 5 * frames] = dhid_seven
    late_ref[5 * frames : 6 * frames] = normed
    late_ref[6 * frames :] = jnp.concatenate(
        [sums, jnp.zeros((TILE - sums.shape[0], channels), wide)], axis=0
    ).astype(narrow)


def terms_kernel(
    width,
    shared_ref,
    shared_other_ref,
    late_ref,
    late_other_ref,
    send_ref,
):
    core = lax.axis_index("c")
    frames, channels = shared_ref.shape[0] // 4, late_ref.shape[1]
    lane_tiles = channels // LANES
    planes = send_ref.shape[0]

    def both(start, stop, left=shared_ref, right=shared_other_ref):
        rows = slice(start * frames, stop * frames)
        return jnp.concatenate([left[rows, :channels], right[rows, :channels]], axis=0)

    def late(start, stop):
        return both(start, stop, late_ref, late_other_ref)

    def own_columns(rows, group):
        chosen = one_hot(
            (channels // 2, channels), lambda j: (j // group * 2 + core) * group + j % group
        )
        return matmul(rows, chosen, (1, 1)).astype(narrow)

    dhid_six, dhid_seven, normed = late(0, 2), late(4, 5), late(5, 6)
    for tap in range(2):
        first = tap * planes // 2
        rows_six = own_columns(both(2 * tap, 2 * tap + 2), TILE)
        rows_seven = own_columns(late(2 + tap, 3 + tap), TILE)
        for start, term in (
            (0, matmul(rows_six, dhid_six, (0, 0)).astype(narrow)),
            (2 * lane_tiles, matmul(rows_seven, dhid_seven, (0, 0)).astype(narrow)),
        ):
            for group in range(planes):
                for lane in range(lane_tiles):
                    at = (start + group % 2 * lane_tiles + lane) * TILE
                    send_ref[first + group // 2, at : at + TILE] = term[
                        group * TILE : (group + 1) * TILE, lane * LANES : (lane + 1) * LANES
                    ]
    grad_rows = jnp.concatenate(
        [cotangents_of(shared_ref, width), cotangents_of(shared_other_ref, width)], axis=0
    )
    term = matmul(own_columns(normed, TILE // 2), grad_rows, (0, 0)).astype(narrow)
    for plane in range(planes):
        for lane in range(width // LANES):
            at = (4 * lane_tiles + lane) * TILE
            send_ref[plane, at : at + TILE] = term[
                plane * TILE : (plane + 1) * TILE, lane * LANES : (lane + 1) * LANES
            ]
    sums = (late_ref[6 * frames :].astype(wide) + late_other_ref[6 * frames :].astype(wide))[:6]
    sums = jnp.concatenate(
        [sums[:, lane * LANES : (lane + 1) * LANES] for lane in range(lane_tiles)], axis=0
    ).astype(narrow)
    at = (4 * lane_tiles + width // LANES) * TILE
    send_ref[:, at:] = jnp.broadcast_to(sums[None], (planes,) + sums.shape)


def input_kernel(late_ref, six_ref, back_ref):
    channels = back_ref.shape[1]
    dhid_six = late_ref[: back_ref.shape[0] // 2]
    back = jnp.concatenate(
        [
            matmul(dhid_six, six_ref[:channels], (1, 1)).astype(narrow),
            matmul(dhid_six, six_ref[channels:], (1, 1)).astype(narrow),
        ],
        axis=0,
    )
    back_ref[...] = matmul(position_order(back_ref.shape[0] // 4), back, (0, 0)).astype(narrow)


def plane_kernel(arrived_ref, out_ref, total_ref):
    planes, rows = arrived_ref.shape[0], arrived_ref.shape[1]
    for start in range(0, rows, TILE):
        at = slice(start, min(start + TILE, rows))
        running = arrived_ref[0, at].astype(wide)
        for plane in range(1, planes):
            running += arrived_ref[plane, at].astype(wide)
        total_ref[at] = running
    sections = out_ref.shape[0] // 2
    lane_tiles = sections // 2
    sum_rows = 6 * lane_tiles
    proj_tiles = (rows - sum_rows) // TILE - 4 * lane_tiles
    left = lax.broadcasted_iota(jnp.int32, (TILE, LANES), 1) < LANES // 2
    for half in range(2):
        for lane in range(lane_tiles):
            at = (half * lane_tiles + lane) * TILE
            six = total_ref[at : at + TILE]
            at += 2 * lane_tiles * TILE
            seven = total_ref[at : at + TILE]
            place = half * sections + 2 * lane
            out_ref[place, :TILE] = jnp.where(
                left, six, pltpu.roll(seven, LANES // 2, 1)
            ).astype(narrow)
            out_ref[place + 1, :TILE] = jnp.where(
                left, pltpu.roll(six, LANES // 2, 1), seven
            ).astype(narrow)
    base = 4 * lane_tiles * TILE
    proj = jnp.concatenate(
        [total_ref[base + lane * TILE : base + (lane + 1) * TILE] for lane in range(proj_tiles)],
        axis=1,
    )
    width = proj.shape[1]
    part = width // sections
    for section in range(sections):
        shift = (width - section * part) % width
        moved = pltpu.roll(proj, shift, 1) if shift else proj
        for half in range(2):
            rows_of = slice(half * (TILE // 2), (half + 1) * (TILE // 2))
            out_ref[half * sections + section, TILE : 2 * TILE] = jnp.concatenate(
                [moved[rows_of, :LANES], moved[rows_of, LANES : 2 * LANES]], axis=0
            ).astype(narrow)
    sums = total_ref[rows - sum_rows :].astype(narrow)
    out_ref[:, 2 * TILE :] = jnp.broadcast_to(sums[None], (2 * sections,) + sums.shape)


def line_kernel(arrived_ref, six_ref, seven_ref, proj_ref, gains_ref, biases_ref):
    running = arrived_ref[0].astype(wide)
    for source in range(1, arrived_ref.shape[0]):
        running += arrived_ref[source].astype(wide)
    half = LANES // 2
    six_ref[...] = running[:TILE, :half]
    seven_ref[...] = running[:TILE, half:]
    rows = TILE // 2
    proj = jnp.concatenate(
        [running[TILE : TILE + rows], running[TILE + rows : 2 * TILE]], axis=1
    )
    proj_ref[...] = proj[:, : proj_ref.shape[1]]
    sums = jnp.concatenate(
        [running[2 * TILE + k * 6 : 2 * TILE + (k + 1) * 6] for k in range(4)], axis=1
    )
    gains_ref[...] = sums[:3]
    biases_ref[...] = sums[3:6]


def on_device(layer_five, conv_six, conv_seven, gains, biases, proj_weight, feature_grad):
    utt_local, positions, channels = layer_five.shape
    width = feature_grad.shape[2]
    part_width = proj_weight.shape[1]
    sections = lax.axis_size("s")
    planes = lax.axis_size(("y", "x"))
    frames = utt_local * positions // 4
    shape = jax.ShapeDtypeStruct

    lane_tiles = channels // LANES
    tile_rows = 2 * lane_tiles * TILE
    convs = on_core(conv_kernel, shape((tile_rows, LANES), narrow), [conv_six, conv_seven])
    in_hbm = pl.BlockSpec(memory_space=pl.ANY)
    outgoing = pl.pallas_call(
        pick_kernel,
        out_shape=shape((sections, 2 * TILE + width // LANES * (TILE // 2), LANES), narrow),
        in_specs=[in_hbm, in_hbm],
        out_specs=pl.BlockSpec(memory_space=pltpu.VMEM),
        scratch_shapes=[
            pltpu.VMEM((TILE, 2 * LANES), narrow),
            pltpu.VMEM(feature_grad.shape, narrow),
            pltpu.SemaphoreType.DMA((2,)),
        ],
        compiler_params=pltpu.CompilerParams(vmem_limit_bytes=56 * 1024 * 1024),
    )(proj_weight.T, feature_grad)
    line = 2 * sections
    opposite = [
        (z, (1 - z // sections) * sections + (z % sections + sections // 2) % sections)
        for z in range(line)
    ]
    other_convs = lax.ppermute(convs, ("zh", "s"), opposite)
    arrived = exchange(outgoing, "s")
    bundle = on_core(
        bundle_kernel,
        shape((planes, 2 * tile_rows + sections * 2 * TILE, LANES), narrow),
        [convs, other_convs, arrived],
    )
    gathered = exchange(bundle, ("y", "x"))
    sibling = swap(gathered.reshape(-1, LANES), "c")

    tiles_shape = (planes, bundle.shape[1] // TILE, TILE, LANES)
    shared, part = on_core(
        early_kernel,
        [shape((4 * frames, 2 * channels), narrow), shape((frames, 2 * LANES), wide)],
        [layer_five.reshape(4 * frames, channels), gathered.reshape(tiles_shape), arrived],
        scratch=[pltpu.VMEM((width, 2 * LANES), narrow), pltpu.VMEM((frames, width), wide)],
    )
    shared_other = swap(shared, "c")
    six_full, late = on_core(
        functools.partial(layer_kernel, width),
        [
            shape((2 * channels, channels), narrow),
            shape((6 * frames + TILE, channels), narrow),
        ],
        [
            shared,
            gathered.reshape(tiles_shape),
            sibling.reshape(tiles_shape),
            part,
            gains,
            biases,
        ],
        scratch=[
            pltpu.VMEM((2 * channels, channels), narrow),
            pltpu.VMEM((width, 2 * LANES), narrow),
        ],
        megabytes=16,
    )
    late_other = swap(late, "c")
    back = on_core(input_kernel, shape((4 * frames, channels), narrow), [late, six_full])
    late, back = lax.optimization_barrier((late, back))
    send_rows = (4 * lane_tiles + width // LANES) * TILE + 6 * lane_tiles
    chip = on_core(
        functools.partial(terms_kernel, width),
        shape((planes, send_rows, LANES), narrow),
        [shared, shared_other, late, late_other],
        megabytes=24,
    )
    plane_in = exchange(chip, ("y", "x"))
    line_out = on_core(
        plane_kernel,
        shape((2 * sections, 3 * TILE + TILE // 2, LANES), narrow),
        [plane_in],
        scratch=[pltpu.VMEM((send_rows, LANES), wide)],
    )
    line_in = exchange(line_out, ("zh", "s"))
    out_six, out_seven, out_proj, out_gains, out_biases = on_core(
        line_kernel,
        [
            shape((TILE, channels // sections), wide),
            shape((TILE, channels // sections), wide),
            shape((TILE // 2, part_width), wide),
            shape((3, channels), wide),
            shape((3, channels), wide),
        ],
        [line_in],
    )
    return (
        back.reshape(utt_local, positions, channels),
        out_six,
        out_seven,
        out_proj,
        out_gains,
        out_biases,
    )


def solution(mesh):
    fine = Mesh(mesh.devices.reshape(4, 4, 2, 2, 8), ("y", "x", "zh", "c", "s"))
    tm = ("y", "x", "zh", "c")
    return jax.shard_map(
        on_device,
        mesh=fine,
        in_specs=(
            P("s", tm, None),
            P(tm, None),
            P(tm, None),
            P(),
            P(),
            P(None, "s"),
            P(None, tm + ("s",), None),
        ),
        out_specs=(
            P("s", tm, None),
            P(tm, "s"),
            P(tm, "s"),
            P(tm, "s"),
            P(),
            P(),
        ),
        check_vma=False,
    )
```

```python
import functools

import jax
import jax.numpy as jnp
from jax import lax
from jax.experimental import pallas as pl
from jax.experimental.pallas import tpu as pltpu
from jax.sharding import Mesh, PartitionSpec as P

norm_epsilon = 1e-05
half_root = 0.7071067811865476
inv_root_tau = 0.3989422804014327
narrow = jnp.bfloat16
wide = jnp.float32
LANES = 128
TILE = 16


def gelu_parts(preact):
    normal_cdf = 0.5 * (1.0 + lax.erf(preact * half_root))
    density = jnp.exp(-0.5 * preact * preact) * inv_root_tau
    return (preact * normal_cdf, normal_cdf + preact * density)


def norm_forward(hidden, gain_row, bias_row):
    average = jnp.mean(hidden, axis=-1, keepdims=True)
    centred = hidden - average
    inv_scale = lax.rsqrt(jnp.mean(centred * centred, axis=-1, keepdims=True) + norm_epsilon)
    normal_part = centred * inv_scale
    return (normal_part * gain_row + bias_row, normal_part, inv_scale)


def norm_backward(incoming, normal_part, inv_scale, gain_row):
    scaled = incoming * gain_row
    first_mean = jnp.mean(scaled, axis=-1, keepdims=True)
    second_mean = jnp.mean(scaled * normal_part, axis=-1, keepdims=True)
    return inv_scale * (scaled - first_mean - normal_part * second_mean)


def matmul(left, right, over=(1, 0)):
    return lax.dot_general(
        left, right, (((over[0],), (over[1],)), ((), ())), preferred_element_type=wide
    )


def one_hot(shape, column_of_row):
    rows = lax.broadcasted_iota(jnp.int32, shape, 0)
    columns = lax.broadcasted_iota(jnp.int32, shape, 1)
    return jnp.where(columns == column_of_row(rows), 1.0, 0.0).astype(narrow)


def exchange(value, axes):
    return lax.all_to_all(value, axes, 0, 0, tiled=True)


def swap(value, axis):
    return lax.ppermute(value, axis, [(0, 1), (1, 0)])


def on_core(kernel, out_shape, arrays, scratch=(), megabytes=8):
    multiple = isinstance(out_shape, (list, tuple))
    vmem = pl.BlockSpec(memory_space=pltpu.VMEM)
    return pl.pallas_call(
        kernel,
        out_shape=out_shape,
        in_specs=[vmem] * len(arrays),
        out_specs=[vmem] * len(out_shape) if multiple else vmem,
        scratch_shapes=list(scratch),
        compiler_params=pltpu.CompilerParams(vmem_limit_bytes=megabytes * 1024 * 1024),
    )(*arrays)


def conv_kernel(six_ref, seven_ref, conv_ref):
    lane_tiles = six_ref.shape[1] // LANES
    for index, source in enumerate((six_ref, seven_ref)):
        for lane in range(lane_tiles):
            at = (index * lane_tiles + lane) * TILE
            conv_ref[at : at + TILE] = source[:, lane * LANES : (lane + 1) * LANES]


def pick_kernel(proj_hbm, grad_hbm, out_ref, proj_ref, grad_ref, done):
    plane, core = lax.axis_index(("y", "x")), lax.axis_index("c")
    row = pl.multiple_of(jnp.minimum(plane, proj_hbm.shape[0] // TILE - 1) * TILE, TILE)
    lane = pl.multiple_of(core * 2 * LANES, LANES)
    grad_copy = pltpu.make_async_copy(grad_hbm, grad_ref, done.at[0])
    proj_copy = pltpu.make_async_copy(
        proj_hbm.at[pl.ds(row, TILE), pl.ds(lane, 2 * LANES)], proj_ref, done.at[1]
    )
    grad_copy.start()
    proj_copy.start()
    grad_copy.wait()
    proj_copy.wait()
    sections = out_ref.shape[0]
    utterances = grad_ref.shape[0] // sections
    width = grad_ref.shape[2]
    for section in range(sections):
        for k in range(2):
            out_ref[section, k * TILE : (k + 1) * TILE] = proj_ref[:, k * LANES : (k + 1) * LANES]
        part = jnp.concatenate(
            [grad_ref[section * utterances + k].astype(wide) for k in range(utterances)], axis=0
        )
        for lane in range(0, width, 2 * LANES):
            pieces = [
                part[:, at : at + LANES] for at in range(lane, min(width, lane + 2 * LANES), LANES)
            ]
            start = 2 * TILE + lane // LANES * (TILE // 2)
            out_ref[section, start : start + len(pieces) * (TILE // 2)] = jnp.concatenate(
                pieces, axis=0
            ).astype(narrow)


def bundle_kernel(own_ref, other_ref, arrived_ref, out_ref):
    half = lax.axis_index("zh")
    rows = own_ref.shape[0]
    for plane in range(out_ref.shape[0]):
        out_ref[plane, pl.ds(pl.multiple_of(half * rows, TILE), rows)] = own_ref[...]
        out_ref[plane, pl.ds(pl.multiple_of((1 - half) * rows, TILE), rows)] = other_ref[...]
        for section in range(arrived_ref.shape[0]):
            at = 2 * rows + section * 2 * TILE
            out_ref[plane, at : at + 2 * TILE] = arrived_ref[section, : 2 * TILE]


def position_order(frames):
    def source_row(rows):
        run = rows // frames
        return 4 * (rows % frames) + (run % 2) * 2 + run // 2

    return one_hot((4 * frames, 4 * frames), source_row)


def place_proj(source_ref, proj_ref, row_tiles, section_rows):
    sections = proj_ref.shape[0] // section_rows
    first = source_ref.shape[1] - 2 * sections

    def step(plane, carry):
        for section in range(sections):
            rows = pl.ds(pl.multiple_of(section * section_rows + plane * TILE, TILE), TILE)
            for k in range(2):
                proj_ref[rows, k * LANES : (k + 1) * LANES] = source_ref[
                    plane, first + section * 2 + k
                ]
        return carry

    lax.fori_loop(0, row_tiles, step, 0)


def early_kernel(input_ref, own_ref, grad_ref, shared_ref, part_ref, proj_ref, rows_ref):
    frames, width = rows_ref.shape
    sections = grad_ref.shape[0]
    channels = input_ref.shape[1]
    shared_ref[:, :channels] = matmul(position_order(frames), input_ref[...]).astype(narrow)

    run = frames // (2 * sections)

    def arrived_row(rows):
        utterance = rows // (sections * run)
        rest = rows % (sections * run)
        return (rest // run) * (2 * run) + utterance * run + rest % run

    eight = frames // sections
    for section in range(sections):
        for lane in range(width // LANES):
            start = 2 * TILE + lane * eight
            if lane % 2 == 0:
                count = min(2, width // LANES - lane)
                stacked = grad_ref[section, start : start + count * eight].astype(wide)
            rows_ref[
                section * eight : (section + 1) * eight, lane * LANES : (lane + 1) * LANES
            ] = stacked[(lane % 2) * eight : (lane % 2 + 1) * eight]
    grad_rows = matmul(
        one_hot((frames, frames), arrived_row), rows_ref[...].astype(narrow)
    ).astype(narrow)
    for k in range(4):
        lanes = min(channels, width - k * channels)
        shared_ref[k * frames : (k + 1) * frames, channels : channels + lanes] = grad_rows[
            :, k * channels : k * channels + lanes
        ]
    shared_ref[3 * frames :, channels + lanes :] = jnp.zeros((frames, channels - lanes), narrow)
    place_proj(own_ref, proj_ref, width // sections // TILE, width // sections)
    part_ref[...] = matmul(grad_rows, proj_ref[...])


def cotangents_of(shared_ref, width):
    frames, channels = shared_ref.shape[0] // 4, shared_ref.shape[1] // 2
    rows = jnp.concatenate(
        [shared_ref[k * frames : (k + 1) * frames, channels:] for k in range(4)], axis=1
    )
    return rows[:, :width]


def layer_kernel(
    width,
    shared_ref,
    own_ref,
    other_ref,
    part_ref,
    gains_ref,
    biases_ref,
    six_ref,
    late_ref,
    seven_ref,
    proj_ref,
):
    core = lax.axis_index("c")
    frames, channels = part_ref.shape[0], shared_ref.shape[1] // 2
    lane_tiles = channels // LANES
    planes = own_ref.shape[0]
    sections = (own_ref.shape[1] - 4 * lane_tiles) // 2
    section_rows = width // sections

    def place_tiles(plane, carry):
        for half in range(2):
            for source, index in ((own_ref, core), (other_ref, 1 - core)):
                rows = pl.ds(
                    pl.multiple_of(((plane * 2 + half) * 2 + index) * TILE, TILE), TILE
                )
                for lane in range(lane_tiles):
                    lanes = slice(lane * LANES, (lane + 1) * LANES)
                    tile = half * 2 * lane_tiles + lane
                    six_ref[rows, lanes] = source[plane, tile]
                    seven_ref[rows, lanes] = source[plane, tile + lane_tiles]
        return carry

    lax.fori_loop(0, planes, place_tiles, 0)

    place_proj(other_ref, proj_ref, section_rows // TILE, section_rows)
    tap_zero, tap_one = shared_ref[: 2 * frames, :channels], shared_ref[2 * frames :, :channels]
    hid_six = matmul(tap_zero, six_ref[:channels]) + matmul(tap_one, six_ref[channels:])
    pre_six, part_six, scale_six = norm_forward(hid_six, gains_ref[0:1], biases_ref[0:1])
    act_six_f, deriv_six = gelu_parts(pre_six)
    act_six = act_six_f.astype(narrow)
    act_zero, act_one = act_six[:frames], act_six[frames:]
    hid_seven = matmul(act_zero, seven_ref[:channels]) + matmul(act_one, seven_ref[channels:])
    pre_seven, part_seven, scale_seven = norm_forward(
        hid_seven, gains_ref[1:2], biases_ref[1:2]
    )
    act_seven_f, deriv_seven = gelu_parts(pre_seven)
    pre_feat, part_feat, scale_feat = norm_forward(
        act_seven_f.astype(narrow).astype(wide), gains_ref[2:3], biases_ref[2:3]
    )
    normed = pre_feat.astype(narrow)

    grad_rows = cotangents_of(shared_ref, width)
    own_half, other_half = part_ref[...], matmul(grad_rows, proj_ref[...])
    first = core == 0
    grad_normed = jnp.concatenate(
        [jnp.where(first, own_half, other_half), jnp.where(first, other_half, own_half)], axis=1
    )
    dact_seven = norm_backward(grad_normed, part_feat, scale_feat, gains_ref[2:3])
    dpre_seven = dact_seven * deriv_seven
    dhid_seven = norm_backward(dpre_seven, part_seven, scale_seven, gains_ref[1:2]).astype(narrow)
    dact_six = jnp.concatenate(
        [
            matmul(dhid_seven, seven_ref[:channels], (1, 1)),
            matmul(dhid_seven, seven_ref[channels:], (1, 1)),
        ],
        axis=0,
    )
    dpre_six = dact_six * deriv_six
    dhid_six = norm_backward(dpre_six, part_six, scale_six, gains_ref[0:1]).astype(narrow)
    def total(value):
        return jnp.sum(value, axis=0, keepdims=True)

    sums = jnp.concatenate(
        [
            total(dpre_six * part_six),
            total(dpre_seven * part_seven),
            total(grad_normed * part_feat),
            total(dpre_six),
            total(dpre_seven),
            total(grad_normed),
        ],
        axis=0,
    )
    late_ref[: 2 * frames] = dhid_six
    late_ref[2 * frames : 4 * frames] = act_six
    late_ref[4 * frames : 5 * frames] = dhid_seven
    late_ref[5 * frames : 6 * frames] = normed
    late_ref[6 * frames :] = jnp.concatenate(
        [sums, jnp.zeros((TILE - sums.shape[0], channels), wide)], axis=0
    ).astype(narrow)


def terms_kernel(
    width,
    shared_ref,
    shared_other_ref,
    late_ref,
    late_other_ref,
    send_ref,
):
    core = lax.axis_index("c")
    frames, channels = shared_ref.shape[0] // 4, late_ref.shape[1]
    lane_tiles = channels // LANES
    planes = send_ref.shape[0]

    def both(start, stop, left=shared_ref, right=shared_other_ref):
        rows = slice(start * frames, stop * frames)
        return jnp.concatenate([left[rows, :channels], right[rows, :channels]], axis=0)

    def late(start, stop):
        return both(start, stop, late_ref, late_other_ref)

    def own_columns(rows, group):
        chosen = one_hot(
            (channels // 2, channels), lambda j: (j // group * 2 + core) * group + j % group
        )
        return matmul(rows, chosen, (1, 1)).astype(narrow)

    dhid_six, dhid_seven, normed = late(0, 2), late(4, 5), late(5, 6)
    for tap in range(2):
        first = tap * planes // 2
        rows_six = own_columns(both(2 * tap, 2 * tap + 2), TILE)
        rows_seven = own_columns(late(2 + tap, 3 + tap), TILE)
        for start, term in (
            (0, matmul(rows_six, dhid_six, (0, 0))),
            (2 * lane_tiles, matmul(rows_seven, dhid_seven, (0, 0))),
        ):
            for group in range(planes):
                for lane in range(lane_tiles):
                    at = (start + group % 2 * lane_tiles + lane) * TILE
                    send_ref[first + group // 2, at : at + TILE] = term[
                        group * TILE : (group + 1) * TILE, lane * LANES : (lane + 1) * LANES
                    ].astype(narrow)
    grad_rows = jnp.concatenate(
        [cotangents_of(shared_ref, width), cotangents_of(shared_other_ref, width)], axis=0
    )
    term = matmul(own_columns(normed, TILE // 2), grad_rows, (0, 0)).astype(narrow)
    for plane in range(planes):
        for lane in range(width // LANES):
            at = (4 * lane_tiles + lane) * TILE
            send_ref[plane, at : at + TILE] = term[
                plane * TILE : (plane + 1) * TILE, lane * LANES : (lane + 1) * LANES
            ]
    sums = (late_ref[6 * frames :].astype(wide) + late_other_ref[6 * frames :].astype(wide))[:6]
    sums = jnp.concatenate(
        [sums[:, lane * LANES : (lane + 1) * LANES] for lane in range(lane_tiles)], axis=0
    ).astype(narrow)
    at = (4 * lane_tiles + width // LANES) * TILE
    send_ref[:, at:] = jnp.broadcast_to(sums[None], (planes,) + sums.shape)


def input_kernel(late_ref, six_ref, back_ref):
    channels = back_ref.shape[1]
    dhid_six = late_ref[: back_ref.shape[0] // 2]
    back = jnp.concatenate(
        [
            matmul(dhid_six, six_ref[:channels], (1, 1)).astype(narrow),
            matmul(dhid_six, six_ref[channels:], (1, 1)).astype(narrow),
        ],
        axis=0,
    )
    back_ref[...] = matmul(position_order(back_ref.shape[0] // 4), back, (0, 0)).astype(narrow)


def plane_kernel(arrived_ref, out_ref, total_ref):
    planes, rows = arrived_ref.shape[0], arrived_ref.shape[1]
    for start in range(0, rows, TILE):
        at = slice(start, min(start + TILE, rows))
        running = arrived_ref[0, at].astype(wide)
        for plane in range(1, planes):
            running += arrived_ref[plane, at].astype(wide)
        total_ref[at] = running
    sections = out_ref.shape[0] // 2
    lane_tiles = sections // 2
    sum_rows = 6 * lane_tiles
    proj_tiles = (rows - sum_rows) // TILE - 4 * lane_tiles
    left = lax.broadcasted_iota(jnp.int32, (TILE, LANES), 1) < LANES // 2
    for half in range(2):
        for lane in range(lane_tiles):
            at = (half * lane_tiles + lane) * TILE
            six = total_ref[at : at + TILE]
            at += 2 * lane_tiles * TILE
            seven = total_ref[at : at + TILE]
            place = half * sections + 2 * lane
            out_ref[place, :TILE] = jnp.where(
                left, six, pltpu.roll(seven, LANES // 2, 1)
            ).astype(narrow)
            out_ref[place + 1, :TILE] = jnp.where(
                left, pltpu.roll(six, LANES // 2, 1), seven
            ).astype(narrow)
    base = 4 * lane_tiles * TILE
    proj = jnp.concatenate(
        [total_ref[base + lane * TILE : base + (lane + 1) * TILE] for lane in range(proj_tiles)],
        axis=1,
    )
    width = proj.shape[1]
    part = width // sections
    for section in range(sections):
        shift = (width - section * part) % width
        moved = pltpu.roll(proj, shift, 1) if shift else proj
        for half in range(2):
            rows_of = slice(half * (TILE // 2), (half + 1) * (TILE // 2))
            out_ref[half * sections + section, TILE : 2 * TILE] = jnp.concatenate(
                [moved[rows_of, :LANES], moved[rows_of, LANES : 2 * LANES]], axis=0
            ).astype(narrow)
    sums = total_ref[rows - sum_rows :].astype(narrow)
    out_ref[:, 2 * TILE :] = jnp.broadcast_to(sums[None], (2 * sections,) + sums.shape)


def line_kernel(arrived_ref, six_ref, seven_ref, proj_ref, gains_ref, biases_ref):
    running = arrived_ref[0].astype(wide)
    for source in range(1, arrived_ref.shape[0]):
        running += arrived_ref[source].astype(wide)
    half = LANES // 2
    six_ref[...] = running[:TILE, :half]
    seven_ref[...] = running[:TILE, half:]
    rows = TILE // 2
    proj = jnp.concatenate(
        [running[TILE : TILE + rows], running[TILE + rows : 2 * TILE]], axis=1
    )
    proj_ref[...] = proj[:, : proj_ref.shape[1]]
    sums = jnp.concatenate(
        [running[2 * TILE + k * 6 : 2 * TILE + (k + 1) * 6] for k in range(4)], axis=1
    )
    gains_ref[...] = sums[:3]
    biases_ref[...] = sums[3:6]


def on_device(layer_five, conv_six, conv_seven, gains, biases, proj_weight, feature_grad):
    utt_local, positions, channels = layer_five.shape
    width = feature_grad.shape[2]
    part_width = proj_weight.shape[1]
    sections = lax.axis_size("s")
    planes = lax.axis_size(("y", "x"))
    frames = utt_local * positions // 4
    shape = jax.ShapeDtypeStruct

    lane_tiles = channels // LANES
    tile_rows = 2 * lane_tiles * TILE
    convs = on_core(conv_kernel, shape((tile_rows, LANES), narrow), [conv_six, conv_seven])
    in_hbm = pl.BlockSpec(memory_space=pl.ANY)
    outgoing = pl.pallas_call(
        pick_kernel,
        out_shape=shape((sections, 2 * TILE + width // LANES * (TILE // 2), LANES), narrow),
        in_specs=[in_hbm, in_hbm],
        out_specs=pl.BlockSpec(memory_space=pltpu.VMEM),
        scratch_shapes=[
            pltpu.VMEM((TILE, 2 * LANES), narrow),
            pltpu.VMEM(feature_grad.shape, narrow),
            pltpu.SemaphoreType.DMA((2,)),
        ],
        compiler_params=pltpu.CompilerParams(vmem_limit_bytes=56 * 1024 * 1024),
    )(proj_weight.T, feature_grad)
    line = 2 * sections
    opposite = [
        (z, (1 - z // sections) * sections + (z % sections + sections // 2) % sections)
        for z in range(line)
    ]
    other_convs = lax.ppermute(convs, ("zh", "s"), opposite)
    arrived = exchange(outgoing, "s")
    bundle = on_core(
        bundle_kernel,
        shape((planes, 2 * tile_rows + sections * 2 * TILE, LANES), narrow),
        [convs, other_convs, arrived],
    )
    gathered = exchange(bundle, ("y", "x"))
    sibling = swap(gathered.reshape(-1, LANES), "c")

    tiles_shape = (planes, bundle.shape[1] // TILE, TILE, LANES)
    shared, part = on_core(
        early_kernel,
        [shape((4 * frames, 2 * channels), narrow), shape((frames, 2 * LANES), wide)],
        [layer_five.reshape(4 * frames, channels), gathered.reshape(tiles_shape), arrived],
        scratch=[pltpu.VMEM((width, 2 * LANES), narrow), pltpu.VMEM((frames, width), wide)],
    )
    shared_other = swap(shared, "c")
    six_full, late = on_core(
        functools.partial(layer_kernel, width),
        [
            shape((2 * channels, channels), narrow),
            shape((6 * frames + TILE, channels), narrow),
        ],
        [
            shared,
            gathered.reshape(tiles_shape),
            sibling.reshape(tiles_shape),
            part,
            gains,
            biases,
        ],
        scratch=[
            pltpu.VMEM((2 * channels, channels), narrow),
            pltpu.VMEM((width, 2 * LANES), narrow),
        ],
        megabytes=16,
    )
    late_other = swap(late, "c")
    back = on_core(input_kernel, shape((4 * frames, channels), narrow), [late, six_full])
    late, back = lax.optimization_barrier((late, back))
    send_rows = (4 * lane_tiles + width // LANES) * TILE + 6 * lane_tiles
    chip = on_core(
        functools.partial(terms_kernel, width),
        shape((planes, send_rows, LANES), narrow),
        [shared, shared_other, late, late_other],
        megabytes=24,
    )
    plane_in = exchange(chip, ("y", "x"))
    line_out = on_core(
        plane_kernel,
        shape((2 * sections, 3 * TILE + TILE // 2, LANES), narrow),
        [plane_in],
        scratch=[pltpu.VMEM((send_rows, LANES), wide)],
    )
    line_in = exchange(line_out, ("zh", "s"))
    out_six, out_seven, out_proj, out_gains, out_biases = on_core(
        line_kernel,
        [
            shape((TILE, channels // sections), wide),
            shape((TILE, channels // sections), wide),
            shape((TILE // 2, part_width), wide),
            shape((3, channels), wide),
            shape((3, channels), wide),
        ],
        [line_in],
    )
    return (
        back.reshape(utt_local, positions, channels),
        out_six,
        out_seven,
        out_proj,
        out_gains,
        out_biases,
    )


def solution(mesh):
    fine = Mesh(mesh.devices.reshape(4, 4, 2, 2, 8), ("y", "x", "zh", "c", "s"))
    tm = ("y", "x", "zh", "c")
    return jax.shard_map(
        on_device,
        mesh=fine,
        in_specs=(
            P("s", tm, None),
            P(tm, None),
            P(tm, None),
            P(),
            P(),
            P(None, "s"),
            P(None, tm + ("s",), None),
        ),
        out_specs=(
            P("s", tm, None),
            P(tm, "s"),
            P(tm, "s"),
            P(tm, "s"),
            P(),
            P(),
        ),
        check_vma=False,
    )
```
